32 devices in a mesh: node: 16 (over z, y, x), local: 2 (over core).
Axes of the slice: x: 2, y: 2, z: 4, core: 2. Of those that a mesh axis runs over, the one named last changes fastest.
Arguments:
- grad_out: bfloat16 [2048, 6144], P('node', 'local'), may hold values from -6 to 6
- gate_prob: float32 [2048, 8], P('node'), may hold values from 0.05 to 0.5
- routes: int32 [2048, 8], P('node'), may hold values from 0 to 15, all different within a row; in each aligned block of 128 rows (0 to 127, 128 to 255, ...) at most 64 rows name the same one
- paired: int32 [8], replicated, may hold values from 0 to 1, as said below
- saved_pre: bfloat16 [16, 16, 64, 2, 1024], P('node'), may hold values from -6 to 6
- w_gate: bfloat16 [16, 6144, 1024], P('node', 'local'), may hold values from -0.078125 to 0.078125
- w_up: bfloat16 [16, 6144, 1024], P('node', 'local'), may hold values from -0.078125 to 0.078125
- w_down: bfloat16 [16, 1024, 6144], P('node', None, 'local'), may hold values from -0.1875 to 0.1875
Outputs:
- grad_in: bfloat16 [2048, 6144], P('node', 'local')
- grad_down: bfloat16 [16, 1024, 6144], P('node', None, 'local')
The draws below stay inside these ranges and needn't reach their ends.
Inputs may be any that keep to these rules, and one draw needn't show every extreme that they name: `routes`: each token names 8 different slots. Within the 128 tokens of one block (one index of node), no slot is named by more than 64 tokens, a bound that some block reaches. Exactly half of the pairs are paired, which ones drawn from the seed.
All inputs are finite; a program needn't handle non-finite values.
Results may differ from the reference program's by a relative error of at most 0.023.
Values may be sent and summed in bfloat16 or wider, within the bound.
No kernel may reach another device: no remote copies, remote signals or barrier semaphores. Data moves between devices by JAX's collectives and lax.ppermute only.
A program may use at most 128 MiB of HBM per device.

```python
import math
import jax
import jax.numpy as jnp
import numpy as np
from jax import lax

D = 6144
EXPERT_HIDDEN = 1024
TOP = 8
TOK_NODE = 128
C = 64
TOKENS = 2048
N_NODE = 16
N_LOCAL = 2


def draw_paired(key, part):
    order = jax.random.permutation(key, N_NODE // 2)
    return (order % 2).astype(jnp.int32)


def levels(own_key, extent, split, least, high):
    level, own = 1.0, jax.random.fold_in(own_key, 6)
    for dim, parts in split:
        heights = jnp.exp(jax.random.uniform(jax.random.fold_in(own, dim), (parts,), jnp.float32, least / len(split), high / len(split)))
        level = level * jnp.repeat(heights, extent[dim] // parts).reshape([-1 if axis == dim else 1 for axis in range(len(extent))])
    return level


def assign_block(own_key, own, number, rows, amount, top, reach, skew):
    ranking = jax.random.permutation(own_key, amount)
    packed, common = shares(amount, rows * top, reach, skew, True), shares(amount, rows * top, reach, skew, False)
    places = jnp.arange(amount)

    def named(tallies, rotation):
        used = int((tallies > 0).sum())
        fixed = max(1, used // 4)
        shifted = fixed + (places - fixed + rotation * (used - fixed)) % max(1, amount - fixed)
        return jnp.zeros((amount,), jnp.int32).at[ranking[jnp.where(places < fixed, places, shifted)]].set(jnp.asarray(tallies, jnp.int32))

    tallies = jnp.where(number % 4 == 0, named(packed, number // 4), named(common, number - number // 4 - 1))
    mixed = jax.random.permutation(jax.random.fold_in(own, 3), amount)
    source_of, taker = mixed[0:amount // 2 * 2:2], mixed[1:amount // 2 * 2:2]
    margin = jnp.minimum(tallies[source_of] - 1, reach - tallies[taker]) // 2
    margin = jnp.where((source_of == ranking[0]) | (taker == ranking[0]) | (tallies[taker] == 0), 0, jnp.maximum(margin, 0))
    shifted = jax.random.randint(jax.random.fold_in(own, 4), (amount // 2,), 0, 1 << 20) % (margin + 1)
    tallies = tallies.at[source_of].add(-shifted).at[taker].add(shifted)
    members = jnp.searchsorted(jnp.cumsum(tallies), jnp.arange(rows * top), side="right").astype(jnp.int32)
    table = members.reshape(top, rows).T
    table = table[jax.random.permutation(jax.random.fold_in(own, 1), rows)]
    rotation = jax.random.randint(jax.random.fold_in(own, 2), (rows, 1), 0, top)
    return jnp.take_along_axis(table, (jnp.arange(top)[None, :] + rotation) % top, axis=1)


def shares(number_of, total, bound, skew, full):
    weights = [(1 << 20) // math.isqrt(grade ** skew) + 1 for grade in range(1, number_of + 1)]
    largest = bound if full else min(bound, max(-(-total // number_of), total * weights[0] // sum(weights)))
    least = 1 if total - largest >= number_of - 1 else 0
    given, rest = [largest] + [least] * (number_of - 1), total - largest - least * (number_of - 1)
    while rest > 0:
        candidates = [i for i in range(1, number_of) if given[i] < largest] or [i for i in range(1, number_of) if given[i] < bound]
        mass, left = sum([weights[i] for i in candidates]), rest
        for i in candidates:
            extra = min(bound - given[i], max(1, left * weights[i] // mass), rest)
            given[i] = given[i] + extra
            rest = rest - extra
    return np.array(given)


def centred(rng, shape, width, bound, pieces=(), kind=jnp.bfloat16):
    result = jax.random.normal(rng, shape, jnp.float32) * width
    if len(pieces) > 0:
        result = levels(rng, shape, pieces, -0.22, 0.18) * result
    return jnp.clip(result, min=-bound, max=bound).astype(kind)


def setup_inputs(seed: int = 0) -> dict:
    key_of = jax.random.split(jax.random.key(seed), 9)
    grad_out = centred(key_of[0], (TOKENS, D), 1.0, 6.0, ((0, 16), (1, 2)))
    gate_prob = jnp.clip(jnp.exp(math.log(0.5) - 2.3025851 * jax.random.uniform(key_of[1], (TOKENS, TOP), jnp.float32) ** levels(key_of[1], (TOKENS, TOP), ((0, 16),), -0.2, 0.2)), 0.05, 0.5)
    routes_keys = jax.random.split(jax.random.fold_in(key_of[2], 1), TOKENS // TOK_NODE)
    routes_turns = jax.random.permutation(jax.random.fold_in(key_of[2], 3), TOKENS // TOK_NODE)
    routes = jax.vmap(lambda own, number: assign_block(jax.random.fold_in(key_of[2], 2), own, number, TOK_NODE, N_NODE, TOP, C, 2))(routes_keys, routes_turns).reshape((TOKENS, TOP))
    paired = draw_paired(jax.random.fold_in(key_of[8], 71), 0)
    saved_pre = centred(key_of[4], (N_NODE, N_NODE, C, 2, EXPERT_HIDDEN), 1.0, 6.0, ((0, 16),))
    w_gate = centred(key_of[5], (N_NODE, D, EXPERT_HIDDEN), D ** -0.5, 0.078125, ((0, 16), (1, 2)))
    w_up = centred(key_of[6], (N_NODE, D, EXPERT_HIDDEN), D ** -0.5, 0.078125, ((0, 16), (1, 2)))
    w_down = centred(key_of[7], (N_NODE, EXPERT_HIDDEN, D), EXPERT_HIDDEN ** -0.5, 0.1875, ((0, 16), (2, 2)))
    return dict(grad_out=grad_out, gate_prob=gate_prob, routes=routes, paired=paired, saved_pre=saved_pre, w_gate=w_gate, w_up=w_up, w_down=w_down)


def swiglu_back(dhid, pre):
    gval = pre[:, 0, :].astype(jnp.float32)
    uval = pre[:, 1, :].astype(jnp.float32)
    sigm = jax.nn.sigmoid(gval)
    silu_val = gval * sigm
    dgate = (dhid * uval * sigm * (1.0 + gval * (1.0 - sigm))).astype(jnp.bfloat16)
    dup = (dhid * silu_val).astype(jnp.bfloat16)
    act = (silu_val * uval).astype(jnp.bfloat16)
    return dgate, dup, act


def reference(grad_out, gate_prob, routes, paired, saved_pre, w_gate, w_up, w_down):
    blocks = routes.reshape(N_NODE, TOK_NODE * TOP)
    experts_row = jnp.arange(N_NODE, dtype=jnp.int32)
    onehot = (blocks[:, :, None] == experts_row[None, None, :]).astype(jnp.int32)
    before = jnp.cumsum(onehot, axis=1) - onehot
    row_rank = jnp.sum(before * onehot, axis=2).astype(jnp.int32)
    source = jnp.broadcast_to(jnp.arange(N_NODE, dtype=jnp.int32)[:, None], blocks.shape)
    flat_index = jnp.arange(TOKENS * TOP, dtype=jnp.int32).reshape(N_NODE, TOK_NODE * TOP)
    table = jnp.full((N_NODE, N_NODE, C), -1, jnp.int32)
    table = table.at[blocks.reshape(-1), source.reshape(-1), row_rank.reshape(-1)].set(flat_index.reshape(-1))
    rows_per_slot = N_NODE * C
    part_slice = D // N_LOCAL

    def one_slot(expert):
        index_row = table[expert].reshape(rows_per_slot)
        valid = index_row >= 0
        safe = jnp.where(valid, index_row, 0)
        token_id = safe // TOP
        which = safe - token_id * TOP
        scale = gate_prob[token_id, which] * valid.astype(jnp.float32)
        token_rows = (grad_out[token_id].astype(jnp.float32) * scale[:, None]).astype(jnp.bfloat16)
        down_matrix = w_down[expert]
        part_count = jnp.einsum("ugp,tgp->gut", token_rows.reshape(rows_per_slot, N_LOCAL, part_slice).astype(jnp.float32), down_matrix.reshape(EXPERT_HIDDEN, N_LOCAL, part_slice).astype(jnp.float32))
        part_count = part_count.astype(jnp.bfloat16)
        dhid = jnp.sum(part_count.astype(jnp.float32), axis=0)
        pre = saved_pre[expert].reshape(rows_per_slot, 2, EXPERT_HIDDEN)
        dgate, dup, act = swiglu_back(dhid, pre)
        back = jnp.dot(dgate, w_gate[expert].T, preferred_element_type=jnp.float32) + jnp.dot(dup, w_up[expert].T, preferred_element_type=jnp.float32)
        back = back.astype(jnp.bfloat16)
        own = jnp.dot(act.T, token_rows, preferred_element_type=jnp.float32).astype(jnp.bfloat16)
        return back, own

    backs, owns = lax.map(one_slot, jnp.arange(N_NODE, dtype=jnp.int32))
    targets = table.reshape(-1)
    targets = jnp.where(targets >= 0, targets, TOKENS * TOP)
    spread_rows = jnp.zeros((TOKENS * TOP, D), jnp.bfloat16).at[targets].set(backs.reshape(N_NODE * rows_per_slot, D), mode="drop")
    grad_in = jnp.sum(spread_rows.reshape(TOKENS, TOP, D).astype(jnp.float32), axis=1).astype(jnp.bfloat16)
    partner = jnp.roll(owns, N_NODE // 2, axis=0)
    flags = jnp.concatenate([paired, paired]).astype(jnp.float32)
    own_f = lax.optimization_barrier(owns).astype(jnp.float32)
    grad_down = (own_f + flags[:, None, None] * partner.astype(jnp.float32)).astype(jnp.bfloat16)
    return grad_in, grad_down
```

```python
import functools

import jax
import jax.numpy as jnp
from jax import lax
from jax.experimental import pallas as pl
from jax.experimental.pallas import tpu as pltpu
from jax.sharding import PartitionSpec as P

F32 = jnp.float32
BF16 = jnp.bfloat16
LANES = 128
MIB = 1 << 20
PLANE = 4
CONTRACT_LAST = (((1,), (1,)), ((), ()))


def params(mib, ndims=0):
    sem = ("arbitrary",) * ndims if ndims else None
    return pltpu.CompilerParams(vmem_limit_bytes=mib * MIB, dimension_semantics=sem)


def cost(flops, nbytes):
    return pl.CostEstimate(flops=int(flops), bytes_accessed=int(nbytes), transcendentals=0)


def dot(a, b):
    return jnp.dot(a, b, preferred_element_type=F32)


def attach_kernel(top, grad_ref, routes_ref, gate_ref, out_ref):
    tok, feats = grad_ref.shape
    out_ref[:, :feats] = grad_ref[...]
    gate = gate_ref[...]
    high = gate.astype(BF16).astype(F32)
    mid = (gate - high).astype(BF16).astype(F32)
    low = gate - high - mid
    names = routes_ref[...].astype(F32)
    pad = jnp.zeros((tok, LANES - 4 * top), F32)
    out_ref[:, feats:] = jnp.concatenate([names, high, mid, low, pad], axis=1).astype(BF16)


def attach(grad_out, routes, gate_prob):
    tok, feats = grad_out.shape
    top = routes.shape[1]
    return pl.pallas_call(
        functools.partial(attach_kernel, top),
        out_shape=jax.ShapeDtypeStruct((tok, feats + LANES), BF16),
        compiler_params=params(16),
        name="attach",
    )(grad_out, routes, gate_prob)


def ranks(meta, slot, top, width):
    tok = meta.shape[0]
    lane = lax.broadcasted_iota(jnp.int32, meta.shape, 1)
    hit = jnp.where((lane < top) & (meta == slot.astype(F32)), 1.0, 0.0)
    named = jnp.broadcast_to(jnp.sum(hit, axis=1, keepdims=True), (tok, width))
    row = lax.broadcasted_iota(jnp.int32, (tok, tok), 0)
    col = lax.broadcasted_iota(jnp.int32, (tok, tok), 1)
    earlier = jnp.where(row > col, 1.0, 0.0).astype(BF16)
    return jnp.where(named > 0.5, dot(earlier, named.astype(BF16)), -1.0)


def row_gates(picked, slot, top):
    lane = lax.broadcasted_iota(jnp.int32, picked.shape, 1)
    high = pltpu.roll(picked, LANES - top, 1)
    mid = pltpu.roll(picked, LANES - 2 * top, 1)
    low = pltpu.roll(picked, LANES - 3 * top, 1)
    gate = (high + mid) + low
    chosen = jnp.where((lane < top) & (picked == slot.astype(F32)), gate, 0.0)
    return jnp.sum(chosen, axis=1, keepdims=True)


def selection(meta_refs, slot, top, cap, sel_ref, gate_ref):
    for q, meta_ref in enumerate(meta_refs):
        meta = meta_ref[...]
        rank = ranks(meta.astype(F32), slot, top, LANES)
        turned = jnp.transpose(rank)[:cap]
        want = lax.broadcasted_iota(jnp.int32, turned.shape, 0).astype(F32)
        sel = jnp.where(turned == want, 1.0, 0.0).astype(BF16)
        sel_ref[q * cap : (q + 1) * cap, :] = sel
        gates = row_gates(dot(sel, meta), slot, top)
        gate_ref[q * cap : (q + 1) * cap, :] = jnp.broadcast_to(gates, (cap, LANES))


def rows_kernel(top, cap, first, with_product, who_ref, *refs):
    z_ref, x_ref, y_ref, xya_ref, xyb_ref, mz_ref, mx_ref, my_ref, mxy_ref = refs[:9]
    if with_product:
        wd_ref, rows_ref, part_ref, sel_ref, gate_ref, acc_ref = refs[9:]
        slot = who_ref[0]
    else:
        rows_ref, sel_ref, gate_ref = refs[9:]
        slot = who_ref[2]
    step = pl.program_id(0)

    @pl.when(step == 0)
    def _():
        selection((mz_ref, mx_ref, my_ref, mxy_ref), slot, top, cap, sel_ref, gate_ref)
        if with_product:
            acc_ref[...] = jnp.zeros_like(acc_ref)

    def put(q, block):
        at = slice(q * cap, (q + 1) * cap)
        rows_ref[at, :] = (dot(sel_ref[at, :], block) * gate_ref[at, :1]).astype(BF16)

    put(0, z_ref[...])
    put(1, x_ref[...])
    put(2, y_ref[...])

    @pl.when(step < first)
    def _():
        put(3, xya_ref[...])

    @pl.when(step >= first)
    def _():
        put(3, xyb_ref[...])

    if with_product:
        acc_ref[...] += lax.dot_general(
            rows_ref[...], wd_ref[...], CONTRACT_LAST, preferred_element_type=F32
        )

        @pl.when(step == pl.num_programs(0) - 1)
        def _():
            part_ref[...] = acc_ref[...].astype(BF16)


def make_rows(who, blocks, w_down, sizes, name):
    tok, feats, piece_a, chunk, cap, top = sizes
    piece_b = feats - piece_a
    first = piece_a // chunk
    steps = feats // chunk
    z, x, y, xya, xyb = blocks
    by_step = pl.BlockSpec((tok, chunk), lambda i, who: (0, i))
    meta = pl.BlockSpec((tok, LANES), lambda i, who: (0, feats // LANES))
    in_specs = [by_step] * 3 + [
        pl.BlockSpec((tok, chunk), lambda i, who: (0, jnp.minimum(i, first - 1))),
        pl.BlockSpec((tok, chunk), lambda i, who: (0, jnp.maximum(i - first, 0))),
        meta,
        meta,
        meta,
        pl.BlockSpec((tok, LANES), lambda i, who: (0, piece_b // LANES)),
    ]
    args = [z, x, y, xya, xyb, z, x, y, xyb]
    count = PLANE * cap
    out_shape = [jax.ShapeDtypeStruct((count, feats), BF16)]
    out_specs = [pl.BlockSpec((count, chunk), lambda i, who: (0, i))]
    scratch = [pltpu.VMEM((count, tok), BF16), pltpu.VMEM((count, LANES), F32)]
    flops = 2 * count * tok * feats
    nbytes = 2 * feats * (PLANE * tok + count)
    if w_down is not None:
        hidden = w_down.shape[0]
        in_specs.append(pl.BlockSpec((hidden, chunk), lambda i, who: (0, i)))
        args.append(w_down)
        out_shape.append(jax.ShapeDtypeStruct((count, hidden), BF16))
        out_specs.append(pl.BlockSpec((count, hidden), lambda i, who: (0, 0)))
        scratch.append(pltpu.VMEM((count, hidden), F32))
        flops += 2 * count * feats * hidden
        nbytes += 2 * hidden * feats
    return pl.pallas_call(
        functools.partial(rows_kernel, top, cap, first, w_down is not None),
        grid_spec=pltpu.PrefetchScalarGridSpec(
            num_scalar_prefetch=1,
            grid=(steps,),
            in_specs=in_specs,
            out_specs=out_specs,
            scratch_shapes=scratch,
        ),
        out_shape=out_shape,
        compiler_params=params(24, 1),
        cost_estimate=cost(flops, nbytes),
        name=name,
    )(who, *args)


def act_kernel(cap, many, who_ref, g_ref, u_ref, out_ref):
    rows = g_ref.shape[0]
    width = many * cap
    for i in range(rows // width):
        pieces = []
        for q in range(many):
            at = pl.ds(pl.multiple_of((who_ref[0] ^ (i * many + q)) * cap, cap), cap)
            g = g_ref[at, :].astype(F32)
            pieces.append(g * jax.nn.sigmoid(g) * u_ref[at, :].astype(F32))
        block = jnp.concatenate(pieces, axis=0) if many > 1 else pieces[0]
        out_ref[:, i * width : (i + 1) * width] = jnp.transpose(block).astype(BF16)


def activations(who, g, u, cap):
    rows, hidden = g.shape
    many = max(1, LANES // cap)
    return pl.pallas_call(
        functools.partial(act_kernel, cap, many),
        in_specs=[
            pl.BlockSpec(memory_space=pltpu.SMEM),
            pl.BlockSpec(memory_space=pltpu.VMEM),
            pl.BlockSpec(memory_space=pltpu.VMEM),
        ],
        out_specs=pl.BlockSpec(memory_space=pltpu.VMEM),
        out_shape=jax.ShapeDtypeStruct((hidden, rows), BF16),
        compiler_params=params(24),
        cost_estimate=cost(20 * rows * hidden, 6 * rows * hidden),
        name="activation",
    )(who, g, u)


def back_kernel(cap, first, who_ref, po_ref, pr_ref, *refs):
    g_refs, u_refs = refs[:PLANE], refs[PLANE : 2 * PLANE]
    wg_ref, wu_ref, keep_ref, sa_ref, sb_ref, dg_ref, du_ref = refs[2 * PLANE :]
    step = pl.program_id(0)

    @pl.when(step == 0)
    def _():
        for q in range(PLANE):
            at = slice(q * cap, (q + 1) * cap)
            dhid = po_ref[at, :].astype(F32) + pr_ref[at, :].astype(F32)
            g = g_refs[q][...].astype(F32)
            u = u_refs[q][...].astype(F32)
            sig = jax.nn.sigmoid(g)
            dg_ref[at, :] = (dhid * u * sig * (1.0 + g * (1.0 - sig))).astype(BF16)
            du_ref[at, :] = (dhid * g * sig).astype(BF16)

    back = lax.dot_general(dg_ref[...], wg_ref[...], CONTRACT_LAST, preferred_element_type=F32)
    back += lax.dot_general(du_ref[...], wu_ref[...], CONTRACT_LAST, preferred_element_type=F32)
    back = back.astype(BF16)

    @pl.when(step < first)
    def _():
        keep_ref[:cap, :] = back[:cap]
        keep_ref[cap:, :] = back[2 * cap : 3 * cap]
        sa_ref[:cap, :] = back[cap : 2 * cap]
        sa_ref[cap:, :] = back[3 * cap :]

    @pl.when(step >= first)
    def _():
        keep_ref[...] = back[: 2 * cap]
        sb_ref[...] = back[2 * cap :]


def make_back(who, part_own, part_other, g, u, w_gate, w_up, sizes, group, name):
    tok, feats, piece_a, chunk, cap, top = sizes
    hidden = g.shape[1]
    first = piece_a // chunk
    count = PLANE * cap

    def saved(q):
        return pl.BlockSpec((cap, hidden), lambda i, who: (who[0] ^ (PLANE * group + q), 0))

    whole = pl.BlockSpec((count, hidden), lambda i, who: (0, 0))
    weight = pl.BlockSpec((chunk, hidden), lambda i, who: (i, 0))
    return pl.pallas_call(
        functools.partial(back_kernel, cap, first),
        grid_spec=pltpu.PrefetchScalarGridSpec(
            num_scalar_prefetch=1,
            grid=(feats // chunk,),
            in_specs=[whole, whole]
            + [saved(q) for q in range(PLANE)] * 2
            + [weight, weight],
            out_specs=[
                pl.BlockSpec((2 * cap, chunk), lambda i, who: (0, i)),
                pl.BlockSpec((2 * cap, chunk), lambda i, who: (0, jnp.minimum(i, first - 1))),
                pl.BlockSpec((2 * cap, chunk), lambda i, who: (0, jnp.maximum(i - first, 0))),
            ],
            scratch_shapes=[pltpu.VMEM((count, hidden), BF16)] * 2,
        ),
        out_shape=[
            jax.ShapeDtypeStruct((2 * cap, feats), BF16),
            jax.ShapeDtypeStruct((2 * cap, piece_a), BF16),
            jax.ShapeDtypeStruct((2 * cap, feats - piece_a), BF16),
        ],
        compiler_params=params(24, 1),
        cost_estimate=cost(4 * count * feats * hidden, 4 * feats * hidden + 2 * count * feats),
        name=name,
    )(who, part_own, part_other, *([g] * PLANE), *([u] * PLANE), w_gate, w_up)


def spread(meta, slot, other, top, cap):
    width = max(LANES, 2 * cap)
    mine = ranks(meta, slot, top, width)[:, : 2 * cap]
    theirs = ranks(meta, other, top, width)[:, : 2 * cap]
    lane = lax.broadcasted_iota(jnp.int32, mine.shape, 1)
    want = lane.astype(F32)
    off = jnp.where(lane < cap, mine, theirs + cap) - want
    return jnp.where(off == 0.0, 1.0, 0.0).astype(BF16)


def join_kernel(top, cap, piece_a, who_ref, mz, mx, my, keep, ra, rb, out_ref, sa_ref, sb_ref):
    me = who_ref[0]
    z, x, y = mz[...].astype(F32), mx[...].astype(F32), my[...].astype(F32)

    def tokens(meta, other, kept, got):
        hot = spread(meta, me, me ^ other, top, cap)
        return dot(hot, jnp.concatenate([kept, got], axis=0)).astype(BF16)

    out_ref[:, :piece_a] = tokens(z, 1, keep[:cap, :piece_a], ra[:cap, :])
    sa_ref[...] = tokens(y, 1, keep[cap:, :piece_a], ra[cap:, :])
    out_ref[:, piece_a:] = tokens(z, 2, keep[:cap, piece_a:], rb[:cap, :])
    sb_ref[...] = tokens(x, 2, keep[cap:, piece_a:], rb[cap:, :])


def join(who, z, x, y, keep, got_a, got_b, sizes, name):
    tok, feats, piece_a, chunk, cap, top = sizes
    piece_b = feats - piece_a
    meta = pl.BlockSpec((tok, LANES), lambda i, who: (0, feats // LANES))

    def full(a):
        return pl.BlockSpec(a.shape, lambda i, who: (0, 0))

    shapes = [(tok, feats), (tok, piece_a), (tok, piece_b)]
    return pl.pallas_call(
        functools.partial(join_kernel, top, cap, piece_a),
        grid_spec=pltpu.PrefetchScalarGridSpec(
            num_scalar_prefetch=1,
            grid=(1,),
            in_specs=[meta, meta, meta, full(keep), full(got_a), full(got_b)],
            out_specs=[pl.BlockSpec(s, lambda i, who: (0, 0)) for s in shapes],
        ),
        out_shape=[jax.ShapeDtypeStruct(s, BF16) for s in shapes],
        compiler_params=params(24, 1),
        cost_estimate=cost(8 * tok * cap * feats, 4 * (2 * cap + tok) * feats),
        name=name,
    )(who, z, x, y, keep, got_a, got_b)


def add_kernel(piece_a, kept, ga, gb, *refs):
    *others, out_ref = refs
    for at, got in ((slice(0, piece_a), ga), (slice(piece_a, kept.shape[1]), gb)):
        total = kept[:, at].astype(F32) + got[...].astype(F32)
        for other in others:
            total += other[:, at].astype(F32)
        out_ref[:, at] = total.astype(BF16)


def add(kept, got_a, got_b, others, name):
    return pl.pallas_call(
        functools.partial(add_kernel, got_a.shape[1]),
        out_shape=jax.ShapeDtypeStruct(kept.shape, BF16),
        compiler_params=params(24),
        cost_estimate=cost(4 * kept.size, 2 * kept.size * (3 + len(others))),
        name=name,
    )(kept, got_a, got_b, *others)


def own_kernel(groups, flag_ref, act_ref, pact_ref, *refs):
    rows, prows, out_ref = refs[:groups], refs[groups : 2 * groups], refs[-1]
    count = rows[0].shape[0]

    def product(a_ref, b_refs, order):
        total = None
        for g in range(groups):
            at = order(g) * count
            term = dot(a_ref[:, at : at + count], b_refs[g][...])
            total = term if total is None else total + term
        return total.astype(BF16).astype(F32)

    own = product(act_ref, rows, lambda g: g)
    paired = product(pact_ref, prows, lambda g: g ^ (groups // 2))
    out_ref[...] = (own + flag_ref[0] * paired).astype(BF16)


def make_own(flag, act, pact, rows, prows, before, start, count, chunk, feats, name):
    groups = len(rows)
    hidden, width = act.shape
    full = pl.BlockSpec((hidden, width), lambda i, flag: (0, 0))
    part = pl.BlockSpec((rows[0].shape[0], chunk), lambda i, flag: (0, i + start))
    in_specs = [full, full] + [part] * (2 * groups)
    args = [flag, act, pact, *rows, *prows]
    aliases = {}
    if before is not None:
        in_specs.append(pl.BlockSpec(memory_space=pl.ANY))
        aliases = {len(args): 0}
        args.append(before)
    return pl.pallas_call(
        functools.partial(own_kernel, groups),
        grid_spec=pltpu.PrefetchScalarGridSpec(
            num_scalar_prefetch=1,
            grid=(count,),
            in_specs=in_specs,
            out_specs=pl.BlockSpec((hidden, chunk), lambda i, flag: (0, i + start)),
        ),
        out_shape=jax.ShapeDtypeStruct((hidden, feats), BF16),
        input_output_aliases=aliases,
        compiler_params=params(32, 1),
        cost_estimate=cost(4 * hidden * width * chunk * count, 4 * hidden * width + 6 * width * chunk * count),
        name=name,
    )(*args)


def flip(block, bits):
    count = lax.axis_size("node")
    return lax.ppermute(block, "node", [(i, i ^ bits) for i in range(count)])


def planes(block, pairs):
    route = [(PLANE * a + i, PLANE * b + i) for a, b in pairs for i in range(PLANE)]
    return lax.ppermute(block, "node", route)


def plane_blocks(block, groups):
    if groups != 4:
        return [block] + [flip(block, PLANE * g) for g in range(1, groups)]
    plane = lax.axis_index("node") // PLANE
    middle = (plane == 1) | (plane == 2)
    inward, outward = [(1, 2), (2, 1)], [(1, 0), (2, 3)]
    one = flip(block, PLANE)
    across = planes(block, inward)
    second = planes(one, inward)
    edge_two = planes(across, outward)
    edge_three = planes(second, outward)
    return [block, one, jnp.where(middle, second, edge_two), jnp.where(middle, across, edge_three)]


def body(grad_out, gate_prob, routes, paired, saved_pre, w_gate, w_up, w_down):
    tok, feats = grad_out.shape
    nodes = lax.axis_size("node")
    locals_ = lax.axis_size("local")
    top = routes.shape[1]
    cap = saved_pre.shape[2]
    hidden = saved_pre.shape[4]
    groups = nodes // PLANE
    half = nodes // 2
    piece_a = feats // (2 * LANES) * LANES
    chunk = max(c for c in (512, 384, 256, 128) if piece_a % c == 0 and (feats - piece_a) % c == 0)
    sizes = (tok, feats, piece_a, chunk, cap, top)
    w_down, w_gate, w_up = w_down[0], w_gate[0], w_up[0]

    me = lax.axis_index("node")
    side = lax.axis_index("local")
    who = jnp.stack([me, side, me ^ half]).astype(jnp.int32)
    flag = jnp.sum(jnp.where(jnp.arange(half, dtype=jnp.int32) == me % half, paired, 0)).astype(F32)[None]

    block = attach(grad_out, routes, gate_prob)
    zs = plane_blocks(block, groups)
    xs = [flip(z, 1) for z in zs]
    ys = [flip(z, 2) for z in zs]
    xyas = [flip(x[:, :piece_a], 2) for x in xs]
    xybs = [flip(y[:, piece_a:], 1) for y in ys]

    saved_rows = saved_pre[0].reshape(nodes * cap, 2, hidden)
    g_rows, u_rows = saved_rows[:, 0, :], saved_rows[:, 1, :]
    act = activations(who, g_rows, u_rows, cap)

    share = hidden // locals_
    mine = flip(lax.dynamic_slice_in_dim(act, side * share, share, 0), half)
    ring = [(i, (i + 1) % locals_) for i in range(locals_)]
    pieces = [mine]
    for _ in range(locals_ - 1):
        pieces.append(lax.ppermute(pieces[-1], "local", ring))
    pact = jnp.zeros((hidden, nodes * cap), BF16)
    for i, piece in enumerate(pieces):
        pact = lax.dynamic_update_slice_in_dim(pact, piece, (side - i) % locals_ * share, 0)

    order = list(range(1, groups)) + [0]
    rows, prows, homing = [None] * groups, [None] * groups, []
    for g in order:
        blocks = (zs[g], xs[g], ys[g], xyas[g], xybs[g])
        rows[g], part = make_rows(who, blocks, w_down, sizes, f"partial_{g}")
        if locals_ == 2:
            other = lax.ppermute(part, "local", ring)
        else:
            other = jnp.zeros(part.shape, F32)
            piece = part
            for _ in range(locals_ - 1):
                piece = lax.ppermute(piece, "local", ring)
                other = other + piece.astype(F32)
        keep, send_a, send_b = make_back(
            who, part, other, g_rows, u_rows, w_gate, w_up, sizes, g, f"back_{g}"
        )
        got_a, got_b = flip(send_a, 1), flip(send_b, 2)
        kept, send_a, send_b = join(who, zs[g], xs[g], ys[g], keep, got_a, got_b, sizes, f"join_{g}")
        got_a, got_b = flip(send_a, 2), flip(send_b, 1)
        if g:
            homing.append(flip(add(kept, got_a, got_b, [], f"sum_{g}"), PLANE * g))
        else:
            grad_in = add(kept, got_a, got_b, homing, "sum_last")
        (prows[g],) = make_rows(who, blocks, None, sizes, f"partner_rows_{g}")

    steps = feats // chunk
    calls = min(3, steps)
    grad_down = None
    for c in range(calls):
        start, stop = steps * c // calls, steps * (c + 1) // calls
        grad_down = make_own(
            flag, act, pact, rows, prows, grad_down, start, stop - start, chunk, feats, f"own_{c}"
        )
    return (grad_in, grad_down[None])


def solution(mesh):
    in_specs = (
        P("node", "local"),
        P("node", None),
        P("node", None),
        P(),
        P("node", None, None, None, None),
        P("node", "local", None),
        P("node", "local", None),
        P("node", None, "local"),
    )
    out_specs = (P("node", "local"), P("node", None, "local"))
    return jax.shard_map(body, mesh=mesh, in_specs=in_specs, out_specs=out_specs, check_vma=False)
```

```python
import functools

import jax
import jax.numpy as jnp
from jax import lax
from jax.experimental import pallas as pl
from jax.experimental.pallas import tpu as pltpu
from jax.sharding import PartitionSpec as P

F32 = jnp.float32
BF16 = jnp.bfloat16
LANES = 128
MIB = 1 << 20
VMEM_MIB = 63
PLANE = 4
CONTRACT_LAST = (((1,), (1,)), ((), ()))


def params(mib, ndims=0):
    sem = ("arbitrary",) * ndims if ndims else None
    return pltpu.CompilerParams(vmem_limit_bytes=mib * MIB, dimension_semantics=sem)


COST = pl.CostEstimate(flops=1000, bytes_accessed=1000, transcendentals=0)


def dot(a, b):
    return jnp.dot(a, b, preferred_element_type=F32)


def attach_kernel(top, grad_ref, routes_ref, gate_ref, out_ref):
    tok, feats = grad_ref.shape
    out_ref[:, :feats] = grad_ref[...]
    gate = gate_ref[...]
    high = gate.astype(BF16).astype(F32)
    mid = (gate - high).astype(BF16).astype(F32)
    low = gate - high - mid
    names = routes_ref[...].astype(F32)
    pad = jnp.zeros((LANES - 4 * top, tok), F32)
    meta = jnp.concatenate([names, high, mid, low, pad], axis=0)
    out_ref[:, feats:] = jnp.transpose(meta).astype(BF16)


def attach(grad_out, routes, gate_prob):
    tok, feats = grad_out.shape
    routes, gate_prob = routes.T, gate_prob.T
    return pl.pallas_call(
        functools.partial(attach_kernel, routes.shape[0]),
        out_shape=jax.ShapeDtypeStruct((tok, feats + LANES), BF16),
        compiler_params=params(VMEM_MIB),
        cost_estimate=COST,
        name="attach",
    )(grad_out, routes, gate_prob)


def cut_kernel(piece_a, x, y, a_out, b_out, a_ref, b_ref, sem):
    pieces = ((x.at[:, :piece_a], a_ref, a_out), (y.at[:, piece_a:], b_ref, b_out))
    loads = [pltpu.make_async_copy(s, v, sem.at[i]) for i, (s, v, _) in enumerate(pieces)]
    stores = [pltpu.make_async_copy(v, t, sem.at[2 + i]) for i, (_, v, t) in enumerate(pieces)]
    for load in loads:
        load.start()
    for load, store in zip(loads, stores):
        load.wait()
        store.start()
    for store in stores:
        store.wait()


def cut(x, y, piece_a):
    tok, width = x.shape
    anywhere = pl.BlockSpec(memory_space=pl.ANY)
    widths = (piece_a, width - piece_a)
    return pl.pallas_call(
        functools.partial(cut_kernel, piece_a),
        in_specs=[anywhere] * 2,
        out_specs=[anywhere] * 2,
        out_shape=[jax.ShapeDtypeStruct((tok, w), BF16) for w in widths],
        scratch_shapes=[*[pltpu.VMEM((tok, w), BF16) for w in widths], pltpu.SemaphoreType.DMA((4,))],
        compiler_params=params(VMEM_MIB),
        cost_estimate=COST,
        name="cut",
    )(x, y)


def ranks(meta, slot, top, width):
    tok = meta.shape[0]
    lane = lax.broadcasted_iota(jnp.int32, meta.shape, 1)
    hit = jnp.where((lane < top) & (meta == slot.astype(F32)), 1.0, 0.0)
    named = jnp.broadcast_to(jnp.sum(hit, axis=1, keepdims=True), (tok, width))
    row = lax.broadcasted_iota(jnp.int32, (tok, tok), 0)
    col = lax.broadcasted_iota(jnp.int32, (tok, tok), 1)
    earlier = jnp.where(row > col, 1.0, 0.0).astype(BF16)
    return jnp.where(named > 0.5, dot(earlier, named.astype(BF16)), -1.0)


def row_gates(picked, slot, top):
    lane = lax.broadcasted_iota(jnp.int32, picked.shape, 1)
    high = pltpu.roll(picked, LANES - top, 1)
    mid = pltpu.roll(picked, LANES - 2 * top, 1)
    low = pltpu.roll(picked, LANES - 3 * top, 1)
    gate = (high + mid) + low
    chosen = jnp.where((lane < top) & (picked == slot.astype(F32)), gate, 0.0)
    return jnp.sum(chosen, axis=1, keepdims=True)


def selection(meta_refs, slots, top, cap, sel_ref, gate_ref):
    at = 0
    for meta_ref in meta_refs:
        meta = meta_ref[...]
        for slot in slots:
            rank = ranks(meta.astype(F32), slot, top, LANES)
            turned = jnp.transpose(rank)[:cap]
            want = lax.broadcasted_iota(jnp.int32, turned.shape, 0).astype(F32)
            sel = jnp.where(turned == want, 1.0, 0.0).astype(BF16)
            sel_ref[at : at + cap, :] = sel
            gates = row_gates(dot(sel, meta), slot, top)
            gate_ref[at : at + cap, :] = jnp.broadcast_to(gates, (cap, LANES))
            at += cap


def staged(copies, ahead=2):
    for copy in copies[:ahead]:
        copy.start()
    place = iter(range(len(copies)))

    def arrive():
        c = next(place)
        copies[c].wait()
        if c + ahead < len(copies):
            copies[c + ahead].start()

    return arrive


def rows_kernel(sizes, layout, who_ref, wd, *refs):
    tok, feats, piece_a, chunk, cap, top = sizes
    blocks, refs = refs[: len(layout)], refs[len(layout) :]
    rows_out, prows_out, part_ref, *refs = refs
    tok_ref, wd_ref, rows_ref, prows_ref, sel_ref, gate_ref, acc_ref, sem, w_sem, out_sem = refs
    steps = feats // chunk
    metas, bodies, writes = [], [], []
    for (q, lo), block in zip(layout, blocks):
        hi = min(lo + block.shape[1], feats)
        if lo + block.shape[1] > feats:
            copy = pltpu.make_async_copy(
                block.at[:, feats - lo :], tok_ref.at[q, :, feats:], sem.at[len(layout) + q]
            )
            metas.append(copy)
        copy = pltpu.make_async_copy(
            block.at[:, : hi - lo], tok_ref.at[q, :, lo:hi], sem.at[len(bodies)]
        )
        bodies.append(copy)
    for copy in metas + bodies:
        copy.start()
    weights = []
    for c in range(steps):
        cols = slice(c * chunk, (c + 1) * chunk)
        weights.append(pltpu.make_async_copy(wd.at[:, cols], wd_ref.at[:, cols], w_sem.at[c]))
    weight_arrives = staged(weights)
    for copy in metas:
        copy.wait()
    selection(
        [tok_ref.at[q, :, feats:] for q in range(PLANE)], (who_ref[0], who_ref[2]), top, cap, sel_ref, gate_ref
    )
    for copy in bodies:
        copy.wait()
    for c in range(steps):
        cols = slice(c * chunk, (c + 1) * chunk)
        for q in range(PLANE):
            at = slice(2 * q * cap, 2 * (q + 1) * cap)
            both = (dot(sel_ref[at, :], tok_ref[q, :, cols]) * gate_ref[at, :1]).astype(BF16)
            rows_ref[q * cap : (q + 1) * cap, cols] = both[:cap]
            prows_ref[q * cap : (q + 1) * cap, cols] = both[cap:]
        for i, (source, target) in enumerate(((rows_ref, rows_out), (prows_ref, prows_out))):
            writes.append(
                pltpu.make_async_copy(source.at[:, cols], target.at[:, cols], out_sem.at[2 * c + i])
            )
            writes[-1].start()
        weight_arrives()
        term = lax.dot_general(
            rows_ref[:, cols], wd_ref[:, cols], CONTRACT_LAST, preferred_element_type=F32
        )
        if c == 0 and steps > 1:
            acc_ref[...] = term
        elif c < steps - 1:
            acc_ref[...] += term
        else:
            part_ref[...] = ((acc_ref[...] + term) if steps > 1 else term).astype(BF16)
    for copy in writes:
        copy.wait()


def make_rows(who, blocks, w_down, sizes, name):
    tok, feats, piece_a, chunk, cap, top = sizes
    hidden = w_down.shape[0]
    count = PLANE * cap
    steps = feats // chunk
    layout, pieces = [], []
    for q, block in enumerate(blocks):
        lo = 0
        for piece in block:
            layout.append((q, lo))
            pieces.append(piece)
            lo += piece.shape[1]
    anywhere = pl.BlockSpec(memory_space=pl.ANY)
    vmem = pl.BlockSpec(memory_space=pltpu.VMEM)
    return pl.pallas_call(
        functools.partial(rows_kernel, sizes, layout),
        in_specs=[pl.BlockSpec(memory_space=pltpu.SMEM)] + [anywhere] * (1 + len(pieces)),
        out_specs=[anywhere, anywhere, vmem],
        scratch_shapes=[
            pltpu.VMEM((PLANE, tok, feats + LANES), BF16),
            pltpu.VMEM((hidden, feats), BF16),
            pltpu.VMEM((count, feats), BF16),
            pltpu.VMEM((count, feats), BF16),
            pltpu.VMEM((2 * count, tok), BF16),
            pltpu.VMEM((2 * count, LANES), F32),
            pltpu.VMEM((count, hidden), F32),
            pltpu.SemaphoreType.DMA((PLANE + len(layout),)),
            pltpu.SemaphoreType.DMA((steps,)),
            pltpu.SemaphoreType.DMA((2 * steps,)),
        ],
        out_shape=[
            jax.ShapeDtypeStruct((count, feats), BF16),
            jax.ShapeDtypeStruct((count, feats), BF16),
            jax.ShapeDtypeStruct((count, hidden), BF16),
        ],
        compiler_params=params(VMEM_MIB),
        cost_estimate=COST,
        name=name,
    )(who, w_down, *pieces)


def act_kernel(cap, many, who_ref, g_ref, u_ref, act_ref, dg_ref, du_ref):
    rows = g_ref.shape[0]
    width = many * cap
    for i in range(rows // width):
        pieces = []
        for q in range(many):
            at = pl.ds(pl.multiple_of((who_ref[0] ^ (i * many + q)) * cap, cap), cap)
            g = g_ref[at, :].astype(F32)
            u = u_ref[at, :].astype(F32)
            sig = jax.nn.sigmoid(g)
            pieces.append(g * sig * u)
            to = slice((i * many + q) * cap, (i * many + q + 1) * cap)
            dg_ref[to, :] = (u * sig * (1.0 + g * (1.0 - sig))).astype(BF16)
            du_ref[to, :] = (g * sig).astype(BF16)
        block = jnp.concatenate(pieces, axis=0) if many > 1 else pieces[0]
        act_ref[:, i * width : (i + 1) * width] = jnp.transpose(block).astype(BF16)


def activations(who, g, u, cap):
    rows, hidden = g.shape
    many = max(1, LANES // cap)
    vmem = pl.BlockSpec(memory_space=pltpu.VMEM)
    return pl.pallas_call(
        functools.partial(act_kernel, cap, many),
        in_specs=[pl.BlockSpec(memory_space=pltpu.SMEM), vmem, vmem],
        out_specs=[vmem] * 3,
        out_shape=[
            jax.ShapeDtypeStruct((hidden, rows), BF16),
            jax.ShapeDtypeStruct((rows, hidden), BF16),
            jax.ShapeDtypeStruct((rows, hidden), BF16),
        ],
        compiler_params=params(VMEM_MIB),
        cost_estimate=COST,
        name="activation",
    )(who, g, u)


def back_kernel(sizes, group, room, mine, other, dg_all, du_all, wg, wu, keep_out, a_out, b_out, *refs):
    tok, feats, piece_a, chunk, cap, top = sizes
    m_ref, o_ref, fg_ref, fu_ref, wg_ref, wu_ref, dg_ref, du_ref, keep_ref, a_ref, b_ref, sem, w_sem, out_sem = refs
    steps = feats // chunk
    count = PLANE * cap
    at = slice(group * count, (group + 1) * count)
    loads, weights, writes = [], [], []
    pairs = ((mine, m_ref), (other, o_ref), (dg_all.at[at, :], fg_ref), (du_all.at[at, :], fu_ref))
    for i, (source, target) in enumerate(pairs):
        loads.append(pltpu.make_async_copy(source, target, sem.at[i]))
        loads[-1].start()
    for c in range(steps):
        rows = slice(c * chunk, (c + 1) * chunk)
        for i, (source, target) in enumerate(((wg, wg_ref), (wu, wu_ref))):
            weights.append(
                pltpu.make_async_copy(source.at[rows, :], target.at[rows, :], w_sem.at[2 * c + i])
            )
    weight_arrives = staged(weights, 4)
    for copy in loads:
        copy.wait()
    for q in range(PLANE):
        rows = slice(q * cap, (q + 1) * cap)
        dhid = m_ref[rows, :].astype(F32) + o_ref[rows, :].astype(F32)
        dg_ref[rows, :] = (dhid * fg_ref[rows, :].astype(F32)).astype(BF16)
        du_ref[rows, :] = (dhid * fu_ref[rows, :].astype(F32)).astype(BF16)
    for c in range(steps):
        cols = slice(c * chunk, (c + 1) * chunk)
        weight_arrives()
        weight_arrives()
        back = lax.dot_general(
            dg_ref[...], wg_ref[cols, :], CONTRACT_LAST, preferred_element_type=F32
        )
        back += lax.dot_general(
            du_ref[...], wu_ref[cols, :], CONTRACT_LAST, preferred_element_type=F32
        )
        back = back.astype(BF16)
        if c * chunk < piece_a:
            keep_ref[:cap, cols] = back[:cap]
            keep_ref[cap:, cols] = back[2 * cap : 3 * cap]
            a_ref[:cap, cols] = back[cap : 2 * cap]
            a_ref[cap:, cols] = back[3 * cap :]
            source, target, to = a_ref, a_out, cols
        else:
            to = slice(c * chunk - piece_a, (c + 1) * chunk - piece_a)
            keep_ref[:, cols] = back[: 2 * cap]
            b_ref[:, to] = back[2 * cap :]
            source, target = b_ref, b_out
        writes.append(
            pltpu.make_async_copy(keep_ref.at[:, cols], keep_out.at[:, cols], out_sem.at[2 * c])
        )
        writes[-1].start()
        writes.append(
            pltpu.make_async_copy(
                source.at[:, to], target.at[: 2 * cap, to], out_sem.at[2 * c + 1]
            )
        )
        writes[-1].start()
    for copy in writes:
        copy.wait()


def make_back(part, other, factors, w_gate, w_up, sizes, group, room, name):
    tok, feats, piece_a, chunk, cap, top = sizes
    hidden = part.shape[1]
    count = PLANE * cap
    steps = feats // chunk
    anywhere = pl.BlockSpec(memory_space=pl.ANY)
    widths = [feats, piece_a, feats - piece_a]
    heights = [2 * cap, 2 * cap + room, 2 * cap + room]
    return pl.pallas_call(
        functools.partial(back_kernel, sizes, group, room),
        in_specs=[anywhere] * 6,
        out_specs=[anywhere] * 3,
        scratch_shapes=[
            pltpu.VMEM((count, hidden), part.dtype),
            pltpu.VMEM((count, hidden), other.dtype),
            pltpu.VMEM((count, hidden), BF16),
            pltpu.VMEM((count, hidden), BF16),
            pltpu.VMEM((feats, hidden), BF16),
            pltpu.VMEM((feats, hidden), BF16),
            pltpu.VMEM((count, hidden), BF16),
            pltpu.VMEM((count, hidden), BF16),
            *[pltpu.VMEM((2 * cap, w), BF16) for w in widths],
            pltpu.SemaphoreType.DMA((4,)),
            pltpu.SemaphoreType.DMA((2 * steps,)),
            pltpu.SemaphoreType.DMA((2 * steps,)),
        ],
        out_shape=[jax.ShapeDtypeStruct((h, w), BF16) for h, w in zip(heights, widths)],
        compiler_params=params(VMEM_MIB),
        cost_estimate=COST,
        name=name,
    )(part, other, *factors, w_gate, w_up)


def spread_kernel(top, cap, who_ref, mz, mx, my, out_ref):
    me = who_ref[0]
    width = max(LANES, 2 * cap)
    tok = mz.shape[0]
    for i, (meta_ref, bit) in enumerate(((mz, 1), (my, 1), (mz, 2), (mx, 2))):
        meta = meta_ref[...].astype(F32)
        mine = ranks(meta, me, top, width)[:, : 2 * cap]
        theirs = ranks(meta, me ^ bit, top, width)[:, : 2 * cap]
        lane = lax.broadcasted_iota(jnp.int32, mine.shape, 1)
        off = jnp.where(lane < cap, mine, theirs + cap) - lane.astype(F32)
        out_ref[i * tok : (i + 1) * tok, :] = jnp.where(off == 0.0, 1.0, 0.0).astype(BF16)


def make_spread(who, z, x, y, sizes, name):
    tok, feats, piece_a, chunk, cap, top = sizes

    def meta(piece):
        place = piece.shape[1] // LANES - 1
        return pl.BlockSpec((tok, LANES), lambda i, who: (0, place))

    return pl.pallas_call(
        functools.partial(spread_kernel, top, cap),
        grid_spec=pltpu.PrefetchScalarGridSpec(
            num_scalar_prefetch=1,
            grid=(1,),
            in_specs=[meta(z), meta(x), meta(y)],
            out_specs=pl.BlockSpec((4 * tok, 2 * cap), lambda i, who: (0, 0)),
        ),
        out_shape=jax.ShapeDtypeStruct((4 * tok, 2 * cap), BF16),
        compiler_params=params(VMEM_MIB, 1),
        cost_estimate=COST,
        name=name,
    )(who, z, x, y)


def join_kernel(sizes, hot, keep, got_a, got_b, *refs):
    tok, feats, piece_a, chunk, cap, top = sizes
    out_ref, a_ref, b_ref = refs[-3:]

    def tokens(i, at, cols, got):
        both = jnp.concatenate([keep[at, cols], got[at, :]], axis=0)
        return dot(hot[i * tok : (i + 1) * tok, :], both).astype(BF16)

    near, far = slice(0, cap), slice(cap, 2 * cap)
    cols_a, cols_b = slice(0, piece_a), slice(piece_a, feats)
    a_ref[...] = tokens(1, far, cols_a, got_a)
    b_ref[...] = tokens(3, far, cols_b, got_b)
    out_ref[:, cols_a] = tokens(0, near, cols_a, got_a)
    out_ref[:, cols_b] = tokens(2, near, cols_b, got_b)


def join(hot, keep, got_a, got_b, into, sizes, name):
    tok, feats, piece_a, chunk, cap, top = sizes
    widths = (feats, piece_a, feats - piece_a)

    def whole(shape, row=0):
        return pl.BlockSpec(shape, lambda i: (row, 0))

    out_specs = [whole((tok, w)) for w in widths]
    out_shape = [jax.ShapeDtypeStruct((tok, w), BF16) for w in widths]
    aliases = {}
    if into:
        for_x, for_y = into
        place = for_x.shape[0] // tok - 1
        out_specs[1:] = [whole((tok, w), place) for w in widths[1:]]
        out_shape[1:] = [jax.ShapeDtypeStruct(a.shape, BF16) for a in (for_y, for_x)]
        aliases = {4: 1, 5: 2}
        into = [for_y, for_x]
    in_specs = [whole(a.shape) for a in (hot, keep)] + [whole((2 * cap, w)) for w in widths[1:]]
    return pl.pallas_call(
        functools.partial(join_kernel, sizes),
        grid=(1,),
        in_specs=in_specs + [pl.BlockSpec(memory_space=pl.ANY)] * len(into),
        out_specs=out_specs,
        out_shape=out_shape,
        input_output_aliases=aliases,
        compiler_params=params(VMEM_MIB, 1),
        cost_estimate=COST,
        name=name,
    )(hot, keep, got_a, got_b, *into)


def add_kernel(pieces, kept, *refs):
    got, others, out_ref = refs[:pieces], refs[pieces:-1], refs[-1]
    lo = 0
    for got_ref in got:
        at = slice(lo, lo + got_ref.shape[1])
        total = kept[:, at].astype(F32) + got_ref[...].astype(F32)
        for other in others:
            total += other[:, at].astype(F32)
        out_ref[:, at] = total.astype(BF16)
        lo = at.stop


def add(kept, got, others, name):
    tok = kept.shape[0]
    some = tok // 2 if tok % 32 == 0 else tok

    def part(a):
        skip = (a.shape[0] - tok) // some
        return pl.BlockSpec((some, a.shape[1]), lambda i: (i + skip, 0))

    args = [kept, *got, *others]
    return pl.pallas_call(
        functools.partial(add_kernel, len(got)),
        grid=(tok // some,),
        in_specs=[part(a) for a in args],
        out_specs=part(kept),
        out_shape=jax.ShapeDtypeStruct(kept.shape, BF16),
        compiler_params=params(VMEM_MIB, 1),
        cost_estimate=COST,
        name=name,
    )(*args)


def total_kernel(*refs):
    *parts, out_ref = refs
    total = parts[0][...].astype(F32)
    for part in parts[1:]:
        total += part[...].astype(F32)
    out_ref[...] = total.astype(BF16)


def total_of(first, others):
    vmem = pl.BlockSpec(memory_space=pltpu.VMEM)
    return pl.pallas_call(
        total_kernel,
        in_specs=[vmem] * (1 + len(others)),
        out_specs=vmem,
        out_shape=jax.ShapeDtypeStruct(first.shape, BF16),
        compiler_params=params(VMEM_MIB),
        cost_estimate=COST,
        name="total",
    )(first, *others)


def own_kernel(groups, flag_ref, act_ref, pact_ref, *refs):
    rows, prows, out_ref = refs[:groups], refs[groups : 2 * groups], refs[-1]
    count = rows[0].shape[0]

    def product(a_ref, b_refs, order):
        total = None
        for g in range(groups):
            at = order(g) * count
            term = dot(a_ref[:, at : at + count], b_refs[g][...])
            total = term if total is None else total + term
        return total.astype(BF16).astype(F32)

    own = product(act_ref, rows, lambda g: g)
    paired = product(pact_ref, prows, lambda g: g ^ (groups // 2))
    out_ref[...] = (own + flag_ref[0] * paired).astype(BF16)


def make_own(flag, act, pact, rows, prows, before, start, count, chunk, feats, name):
    groups = len(rows)
    hidden, width = act.shape
    full = pl.BlockSpec((hidden, width), lambda i, flag: (0, 0))
    part = pl.BlockSpec((rows[0].shape[0], chunk), lambda i, flag: (0, i + start))
    in_specs = [full, full] + [part] * (2 * groups)
    args = [flag, act, pact, *rows, *prows]
    aliases = {}
    if before is not None:
        in_specs.append(pl.BlockSpec(memory_space=pl.ANY))
        aliases = {len(args): 0}
        args.append(before)
    return pl.pallas_call(
        functools.partial(own_kernel, groups),
        grid_spec=pltpu.PrefetchScalarGridSpec(
            num_scalar_prefetch=1,
            grid=(count,),
            in_specs=in_specs,
            out_specs=pl.BlockSpec((hidden, chunk), lambda i, flag: (0, i + start)),
        ),
        out_shape=jax.ShapeDtypeStruct((hidden, feats), BF16),
        input_output_aliases=aliases,
        compiler_params=params(VMEM_MIB, 1),
        cost_estimate=COST,
        name=name,
    )(*args)


def after(value, *first):
    return lax.optimization_barrier((value, first))[0]


def sync(*values):
    return lax.optimization_barrier(values)


def flip(block, bits):
    count = lax.axis_size("node")
    return lax.ppermute(block, "node", [(i, i ^ bits) for i in range(count)])


def planes(block, pairs):
    route = [(PLANE * a + i, PLANE * b + i) for a, b in pairs for i in range(PLANE)]
    return lax.ppermute(block, "node", route)


def body(grad_out, gate_prob, routes, paired, saved_pre, w_gate, w_up, w_down):
    tok, feats = grad_out.shape
    nodes = lax.axis_size("node")
    locals_ = lax.axis_size("local")
    top = routes.shape[1]
    cap = saved_pre.shape[2]
    hidden = saved_pre.shape[4]
    groups = nodes // PLANE
    half = nodes // 2
    piece_a = feats // (2 * LANES) * LANES
    widths = (512, 384, 256, 128)
    chunk = max(c for c in widths if piece_a % c == 0 and (feats - piece_a) % c == 0)
    own_chunk = max(c for c in (512, 384, 256, 128) if feats % c == 0)
    sizes = (tok, feats, piece_a, chunk, cap, top)
    w_down, w_gate, w_up = w_down[0], w_gate[0], w_up[0]
    ring = [(i, (i + 1) % locals_) for i in range(locals_)]

    me = lax.axis_index("node")
    side = lax.axis_index("local")
    who = jnp.stack([me, side, me ^ half]).astype(jnp.int32)
    flag = jnp.sum(jnp.where(jnp.arange(half, dtype=jnp.int32) == me % half, paired, 0)).astype(F32)[None]

    zs, xs, ys, ds, hot, rows, prows, parts, state, sums = ({} for _ in range(10))
    block = attach(grad_out, routes, gate_prob)
    zs[0] = [block]
    saved_rows = saved_pre[0].reshape(nodes * cap, 2, hidden)
    g_rows, u_rows = saved_rows[:, 0, :], saved_rows[:, 1, :]

    def flips(pieces, bits):
        return [flip(piece, bits) for piece in pieces]

    def beside(g):
        xs[g], ys[g] = flips(zs[g], 1), flips(zs[g], 2)

    def corner(g, pieces=None):
        from_x, from_y = pieces or cut(xs[g][0], ys[g][0], piece_a)
        ds[g] = [flip(from_x, 2), flip(from_y, 1)]

    def spreads(g, done):
        hot[g] = make_spread(after(who, done), zs[g][-1], xs[g][-1], ys[g][-1], sizes, f"spread_{g}")

    def to_rows(g, done):
        blocks = [zs[g], xs[g], ys[g], ds[g]]
        rows[g], prows[g], parts[g] = make_rows(after(who, done), blocks, w_down, sizes, f"partial_{g}")

    def exchange(g):
        piece = lax.ppermute(parts[g], "local", ring)
        if locals_ > 2:
            other = piece.astype(F32)
            for _ in range(locals_ - 2):
                piece = lax.ppermute(piece, "local", ring)
                other = other + piece.astype(F32)
            piece = other
        parts[g] = [parts[g], piece]

    def to_back(g, done, room=0):
        mine, other = parts[g]
        state[g] = make_back(
            after(mine, done), other, factors, w_gate, w_up, sizes, g, room, f"back_{g}"
        )

    def first_hop(g):
        keep, send_a, send_b = state[g]
        state[g] = [keep, flip(send_a, 1), flip(send_b, 2)]

    def second_hop(g):
        kept, send_a, send_b = join(hot[g], *state[g], [], sizes, f"join_{g}")
        state[g] = [kept, flip(send_a, 2), flip(send_b, 1)]

    def both_hops(g, h):
        keep, for_x, for_y = state[h]
        kept, for_y, for_x = join(hot[g], *state[g], [for_x, for_y], sizes, f"join_{g}")
        got_x, got_y = flip(for_x, 1), flip(for_y, 2)
        state[g] = [kept, got_y, got_x]
        state[h] = [keep, got_x, got_y]

    def plane_sum(g, others):
        kept, *got = state[g]
        return add(kept, got, others, f"sum_{g}")

    share = hidden // locals_

    def fetch_share():
        return flip(lax.dynamic_slice_in_dim(act, side * share, share, 0), half)

    def all_shares(piece):
        whole = jnp.zeros((hidden, nodes * cap), BF16)
        for i in range(locals_):
            whole = lax.dynamic_update_slice_in_dim(whole, piece, (side - i) % locals_ * share, 0)
            if i < locals_ - 1:
                piece = lax.ppermute(piece, "local", ring)
        return whole

    steps = feats // own_chunk
    calls = min(2, steps)

    def own(c, before, done):
        start, stop = steps * c // calls, steps * (c + 1) // calls
        lists = [[r[g] for g in range(groups)] for r in (rows, prows)]
        return make_own(
            after(flag, done), act, pact, *lists, before, start, stop - start, own_chunk, feats, f"own_{c}"
        )

    def activate(done):
        return activations(after(who, done), g_rows, u_rows, cap)

    if groups != 4 or 2 * piece_a != feats or tok != 2 * cap:
        act, *factors = activate(block)
        pact = all_shares(fetch_share())
        done = act
        for g in range(groups):
            if g:
                zs[g] = [flip(after(block, done), PLANE * g)]
            beside(g)
            corner(g)
            spreads(g, done)
            to_rows(g, done)
            exchange(g)
            to_back(g, done)
            first_hop(g)
            second_hop(g)
            sums[g] = done = plane_sum(g, [])
            if g:
                sums[g] = done = flip(sums[g], PLANE * g)
        grad_down = None
        for c in range(calls):
            grad_down = own(c, grad_down, done)
        return (total_of(sums[0], [sums[g] for g in range(1, groups)]), grad_down[None])

    inward, outward = [(1, 2), (2, 1)], [(1, 0), (2, 3)]
    plane = me // PLANE
    middle = (plane == 1) | (plane == 2)

    beside(0)
    one, over = flip(block, PLANE), planes(block, inward)
    xs[0], ys[0], one, over, g_rows, u_rows = sync(xs[0], ys[0], one, over, g_rows, u_rows)

    zs[1] = [one]
    beside(1)
    second, edge_two = planes(one, inward), planes(over, outward)
    act, *factors = activate(xs[0])
    spreads(0, act)
    cut_zero = cut(after(xs[0][0], hot[0]), ys[0][0], piece_a)
    xs[1], ys[1], second, edge_two, hot[0], cut_zero, act, factors = sync(
        xs[1], ys[1], second, edge_two, hot[0], cut_zero, act, factors
    )

    zs[2] = [jnp.where(middle, second, edge_two)]
    beside(2)
    edge_three = planes(second, outward)
    mine = fetch_share()
    spreads(1, zs[2][0])
    cut_one = cut(after(xs[1][0], hot[1]), ys[1][0], piece_a)
    xs[2], ys[2], edge_three, hot[1], cut_one = sync(xs[2], ys[2], edge_three, hot[1], cut_one)

    cut_two = cut(xs[2][0], ys[2][0], piece_a)
    corner(2, cut_two)
    zs[3] = [jnp.where(middle, over, after(edge_three, cut_two))]
    beside(3)
    spreads(2, zs[3][0])
    to_rows(2, hot[2])
    xs[3], ys[3], hot[2], rows[2], prows[2], parts[2], mine = sync(
        xs[3], ys[3], hot[2], rows[2], prows[2], parts[2], mine
    )

    exchange(2)
    corner(3)
    corner(1, cut_one)
    to_back(2, xs[3])
    to_rows(3, state[2][0])
    ds[1], state[2], rows[3], prows[3], parts[3] = sync(ds[1], state[2], rows[3], prows[3], parts[3])

    exchange(3)
    first_hop(2)
    corner(0, cut_zero)
    to_back(3, state[2][0], tok)
    to_rows(1, state[3][0])
    state[2], ds[0], state[3], rows[1], prows[1], parts[1] = sync(
        state[2], ds[0], state[3], rows[1], prows[1], parts[1]
    )

    exchange(1)
    both_hops(2, 3)
    spreads(3, state[2][0])
    to_back(1, hot[3], tok)
    to_rows(0, state[1][0])
    state[2], state[3], state[1], rows[0], prows[0], parts[0], hot[3] = sync(
        state[2], state[3], state[1], rows[0], prows[0], parts[0], hot[3]
    )

    exchange(0)
    both_hops(3, 1)
    sums[2] = flip(plane_sum(2, []), PLANE)
    pact = all_shares(mine)
    to_back(0, state[3][0], tok)
    sums[2], state[3], state[1], state[0], pact = sync(sums[2], state[3], state[1], state[0], pact)

    total = plane_sum(3, [sums[2]])
    sums[3] = flip(total, 3 * PLANE)
    state[1] = after(state[1], total)
    both_hops(1, 0)
    grad_down = own(0, None, state[1][0])
    state[1], state[0], grad_down = sync(state[1], state[0], grad_down)

    sums[1] = flip(plane_sum(1, []), PLANE)
    second_hop(0)
    for c in range(1, calls):
        grad_down = own(c, grad_down, state[0][0])
    state[0], sums[1], sums[3], grad_down = sync(state[0], sums[1], sums[3], grad_down)
    return (plane_sum(0, [sums[1], sums[3]]), grad_down[None])


def solution(mesh):
    in_specs = (
        P("node", "local"),
        P("node", None),
        P("node", None),
        P(),
        P("node", None, None, None, None),
        P("node", "local", None),
        P("node", "local", None),
        P("node", None, "local"),
    )
    out_specs = (P("node", "local"), P("node", None, "local"))
    return jax.shard_map(body, mesh=mesh, in_specs=in_specs, out_specs=out_specs, check_vma=False)
```

```python
import functools

import jax
import jax.numpy as jnp
from jax import lax
from jax.experimental import pallas as pl
from jax.experimental.pallas import tpu as pltpu
from jax.sharding import PartitionSpec as P

F32 = jnp.float32
BF16 = jnp.bfloat16
LANES = 128
MIB = 1 << 20
VMEM_MIB = 64
PLANE = 4
CONTRACT_LAST = (((1,), (1,)), ((), ()))


def params(mib, ndims=0):
    sem = ("arbitrary",) * ndims if ndims else None
    return pltpu.CompilerParams(vmem_limit_bytes=mib * MIB - (MIB >> 4), dimension_semantics=sem)


COST = pl.CostEstimate(flops=1000, bytes_accessed=1000, transcendentals=0)


def dot(a, b):
    return jnp.dot(a, b, preferred_element_type=F32)


def attach_kernel(top, grad_ref, routes_ref, gate_ref, out_ref):
    tok, feats = grad_ref.shape
    out_ref[:, :feats] = grad_ref[...]
    gate = gate_ref[...]
    high = gate.astype(BF16).astype(F32)
    mid = (gate - high).astype(BF16).astype(F32)
    low = gate - high - mid
    names = routes_ref[...].astype(F32)
    pad = jnp.zeros((LANES - 4 * top, tok), F32)
    meta = jnp.concatenate([names, high, mid, low, pad], axis=0)
    out_ref[:, feats:] = jnp.transpose(meta).astype(BF16)


def attach(grad_out, routes, gate_prob):
    tok, feats = grad_out.shape
    routes, gate_prob = routes.T, gate_prob.T
    return pl.pallas_call(
        functools.partial(attach_kernel, routes.shape[0]),
        out_shape=jax.ShapeDtypeStruct((tok, feats + LANES), BF16),
        compiler_params=params(VMEM_MIB),
        cost_estimate=COST,
        name="attach",
    )(grad_out, routes, gate_prob)


def cut_kernel(piece_a, x, y, a_out, b_out, a_ref, b_ref, sem):
    pieces = ((x.at[:, :piece_a], a_ref, a_out), (y.at[:, piece_a:], b_ref, b_out))
    loads = [pltpu.make_async_copy(s, v, sem.at[i]) for i, (s, v, _) in enumerate(pieces)]
    stores = [pltpu.make_async_copy(v, t, sem.at[2 + i]) for i, (_, v, t) in enumerate(pieces)]
    for load in loads:
        load.start()
    for load, store in zip(loads, stores):
        load.wait()
        store.start()
    for store in stores:
        store.wait()


def cut(x, y, piece_a):
    tok, width = x.shape
    anywhere = pl.BlockSpec(memory_space=pl.ANY)
    widths = (piece_a, width - piece_a)
    return pl.pallas_call(
        functools.partial(cut_kernel, piece_a),
        in_specs=[anywhere] * 2,
        out_specs=[anywhere] * 2,
        out_shape=[jax.ShapeDtypeStruct((tok, w), BF16) for w in widths],
        scratch_shapes=[*[pltpu.VMEM((tok, w), BF16) for w in widths], pltpu.SemaphoreType.DMA((4,))],
        compiler_params=params(VMEM_MIB),
        cost_estimate=COST,
        name="cut",
    )(x, y)


def ranks(meta, slot, top, width):
    tok = meta.shape[0]
    lane = lax.broadcasted_iota(jnp.int32, meta.shape, 1)
    hit = jnp.where((lane < top) & (meta == slot.astype(F32)), 1.0, 0.0)
    named = jnp.broadcast_to(jnp.sum(hit, axis=1, keepdims=True), (tok, width))
    row = lax.broadcasted_iota(jnp.int32, (tok, tok), 0)
    col = lax.broadcasted_iota(jnp.int32, (tok, tok), 1)
    earlier = jnp.where(row > col, 1.0, 0.0).astype(BF16)
    return jnp.where(named > 0.5, dot(earlier, named.astype(BF16)), -1.0)


def row_gates(picked, slot, top):
    lane = lax.broadcasted_iota(jnp.int32, picked.shape, 1)
    high = pltpu.roll(picked, LANES - top, 1)
    mid = pltpu.roll(picked, LANES - 2 * top, 1)
    low = pltpu.roll(picked, LANES - 3 * top, 1)
    gate = (high + mid) + low
    chosen = jnp.where((lane < top) & (picked == slot.astype(F32)), gate, 0.0)
    return jnp.sum(chosen, axis=1, keepdims=True)


def selection(meta_refs, slots, top, cap, sel_ref, gate_ref):
    at = 0
    for meta_ref in meta_refs:
        meta = meta_ref[...]
        for slot in slots:
            rank = ranks(meta.astype(F32), slot, top, LANES)
            turned = jnp.transpose(rank)[:cap]
            want = lax.broadcasted_iota(jnp.int32, turned.shape, 0).astype(F32)
            sel = jnp.where(turned == want, 1.0, 0.0).astype(BF16)
            sel_ref[at : at + cap, :] = sel
            gates = row_gates(dot(sel, meta), slot, top)
            gate_ref[at : at + cap, :] = jnp.broadcast_to(gates, (cap, LANES))
            at += cap


def staged(copies, ahead=2):
    for copy in copies[:ahead]:
        copy.start()
    place = iter(range(len(copies)))

    def arrive():
        c = next(place)
        copies[c].wait()
        if c + ahead < len(copies):
            copies[c + ahead].start()

    return arrive


def rows_kernel(sizes, layout, first, many, waits, who_ref, wd, *refs):
    tok, feats, piece_a, chunk, cap, top = sizes
    blocks, refs = refs[: len(layout)], refs[len(layout) + waits :]
    rows_out, prows_out, part_out, *refs = refs
    tok_ref, wd_ref, rows_ref, prows_ref, sel_ref, gate_ref, acc_ref, part_ref, m_sem, b_sem, w_sem, out_sem = refs
    steps = feats // chunk
    place = slice(first * cap, (first + many) * cap)
    metas, weights, writes = [], [], []
    bodies = [[] for _ in range(steps)]
    for (q, lo), block in zip(layout, blocks):
        if lo + block.shape[1] > feats:
            copy = pltpu.make_async_copy(block.at[:, feats - lo :], tok_ref.at[q, :, feats:], m_sem.at[q])
            copy.start()
            metas.append(copy)
    for c in range(steps):
        at = c * chunk
        for (q, lo), block in zip(layout, blocks):
            if lo <= at < min(lo + block.shape[1], feats):
                source = block.at[:, at - lo : at - lo + chunk]
                copy = pltpu.make_async_copy(source, tok_ref.at[q, :, at : at + chunk], b_sem.at[c * many + q])
                copy.start()
                bodies[c].append(copy)
        cols = slice(at, at + chunk)
        weights.append(pltpu.make_async_copy(wd.at[:, cols], wd_ref.at[:, cols], w_sem.at[c]))
    weight_arrives = staged(weights)
    for copy in metas:
        copy.wait()
    selection(
        [tok_ref.at[q, :, feats:] for q in range(many)], (who_ref[0], who_ref[2]), top, cap, sel_ref, gate_ref
    )
    for c in range(steps):
        cols = slice(c * chunk, (c + 1) * chunk)
        for copy in bodies[c]:
            copy.wait()
        for q in range(many):
            at = slice(2 * q * cap, 2 * (q + 1) * cap)
            both = (dot(sel_ref[at, :], tok_ref[q, :, cols]) * gate_ref[at, :1]).astype(BF16)
            rows_ref[q * cap : (q + 1) * cap, cols] = both[:cap]
            prows_ref[q * cap : (q + 1) * cap, cols] = both[cap:]
        for i, (source, target) in enumerate(((rows_ref, rows_out), (prows_ref, prows_out))):
            writes.append(
                pltpu.make_async_copy(source.at[:, cols], target.at[place, cols], out_sem.at[2 * c + i])
            )
            writes[-1].start()
        weight_arrives()
        term = lax.dot_general(
            rows_ref[:, cols], wd_ref[:, cols], CONTRACT_LAST, preferred_element_type=F32
        )
        if c == 0 and steps > 1:
            acc_ref[...] = term
        elif c < steps - 1:
            acc_ref[...] += term
        else:
            part_ref[...] = ((acc_ref[...] + term) if steps > 1 else term).astype(BF16)
    writes.append(pltpu.make_async_copy(part_ref, part_out.at[place, :], out_sem.at[2 * steps]))
    writes[-1].start()
    for copy in writes:
        copy.wait()


def make_rows(who, blocks, first, before, w_down, sizes, name):
    tok, feats, piece_a, chunk, cap, top = sizes
    hidden = w_down.shape[0]
    count = PLANE * cap
    many = len(blocks)
    steps = feats // chunk
    layout, pieces = [], []
    for q, block in enumerate(blocks):
        lo = 0
        for piece in block:
            layout.append((q, lo))
            pieces.append(piece)
            lo += piece.shape[1]
    anywhere = pl.BlockSpec(memory_space=pl.ANY)
    return pl.pallas_call(
        functools.partial(rows_kernel, sizes, layout, first, many, len(before)),
        in_specs=[pl.BlockSpec(memory_space=pltpu.SMEM)] + [anywhere] * (1 + len(pieces) + len(before)),
        out_specs=[anywhere] * 3,
        scratch_shapes=[
            pltpu.VMEM((many, tok, feats + LANES), BF16),
            pltpu.VMEM((hidden, feats), BF16),
            pltpu.VMEM((many * cap, feats), BF16),
            pltpu.VMEM((many * cap, feats), BF16),
            pltpu.VMEM((2 * many * cap, tok), BF16),
            pltpu.VMEM((2 * many * cap, LANES), F32),
            pltpu.VMEM((many * cap, hidden), F32),
            pltpu.VMEM((many * cap, hidden), BF16),
            pltpu.SemaphoreType.DMA((many,)),
            pltpu.SemaphoreType.DMA((many * steps,)),
            pltpu.SemaphoreType.DMA((steps,)),
            pltpu.SemaphoreType.DMA((2 * steps + 1,)),
        ],
        out_shape=[
            jax.ShapeDtypeStruct((count, feats), BF16),
            jax.ShapeDtypeStruct((count, feats), BF16),
            jax.ShapeDtypeStruct((count, hidden), BF16),
        ],
        input_output_aliases={2 + len(pieces) + i: i for i in range(len(before))},
        compiler_params=params(VMEM_MIB),
        cost_estimate=COST,
        name=name,
    )(who, w_down, *pieces, *before)


def act_kernel(cap, many, who_ref, g_ref, u_ref, act_ref, dg_ref, du_ref):
    rows = g_ref.shape[0]
    width = many * cap
    for i in range(rows // width):
        pieces = []
        for q in range(many):
            at = pl.ds(pl.multiple_of((who_ref[0] ^ (i * many + q)) * cap, cap), cap)
            g = g_ref[at, :].astype(F32)
            u = u_ref[at, :].astype(F32)
            sig = jax.nn.sigmoid(g)
            pieces.append(g * sig * u)
            to = slice((i * many + q) * cap, (i * many + q + 1) * cap)
            dg_ref[to, :] = (u * sig * (1.0 + g * (1.0 - sig))).astype(BF16)
            du_ref[to, :] = (g * sig).astype(BF16)
        block = jnp.concatenate(pieces, axis=0) if many > 1 else pieces[0]
        act_ref[:, i * width : (i + 1) * width] = jnp.transpose(block).astype(BF16)


def activations(who, g, u, cap):
    rows, hidden = g.shape
    many = max(1, LANES // cap)
    vmem = pl.BlockSpec(memory_space=pltpu.VMEM)
    return pl.pallas_call(
        functools.partial(act_kernel, cap, many),
        in_specs=[pl.BlockSpec(memory_space=pltpu.SMEM), vmem, vmem],
        out_specs=[vmem] * 3,
        out_shape=[
            jax.ShapeDtypeStruct((hidden, rows), BF16),
            jax.ShapeDtypeStruct((rows, hidden), BF16),
            jax.ShapeDtypeStruct((rows, hidden), BF16),
        ],
        compiler_params=params(VMEM_MIB),
        cost_estimate=COST,
        name="activation",
    )(who, g, u)


def back_kernel(sizes, group, room, mine, other, dg_all, du_all, wg, wu, keep_out, a_out, b_out, *refs):
    tok, feats, piece_a, chunk, cap, top = sizes
    m_ref, o_ref, fg_ref, fu_ref, wg_ref, wu_ref, dg_ref, du_ref, keep_ref, a_ref, b_ref, sem, w_sem, out_sem = refs
    steps = feats // chunk
    count = PLANE * cap
    at = slice(group * count, (group + 1) * count)
    loads, weights, writes = [], [], []
    pairs = ((mine, m_ref), (other, o_ref), (dg_all.at[at, :], fg_ref), (du_all.at[at, :], fu_ref))
    for i, (source, target) in enumerate(pairs):
        loads.append(pltpu.make_async_copy(source, target, sem.at[i]))
        loads[-1].start()
    for c in range(steps):
        rows = slice(c * chunk, (c + 1) * chunk)
        for i, (source, target) in enumerate(((wg, wg_ref), (wu, wu_ref))):
            weights.append(
                pltpu.make_async_copy(source.at[rows, :], target.at[rows, :], w_sem.at[2 * c + i])
            )
    weight_arrives = staged(weights, 4)
    for copy in loads:
        copy.wait()
    for q in range(PLANE):
        rows = slice(q * cap, (q + 1) * cap)
        dhid = m_ref[rows, :].astype(F32) + o_ref[rows, :].astype(F32)
        dg_ref[rows, :] = (dhid * fg_ref[rows, :].astype(F32)).astype(BF16)
        du_ref[rows, :] = (dhid * fu_ref[rows, :].astype(F32)).astype(BF16)
    for c in range(steps):
        cols = slice(c * chunk, (c + 1) * chunk)
        weight_arrives()
        weight_arrives()
        back = lax.dot_general(
            dg_ref[...], wg_ref[cols, :], CONTRACT_LAST, preferred_element_type=F32
        )
        back += lax.dot_general(
            du_ref[...], wu_ref[cols, :], CONTRACT_LAST, preferred_element_type=F32
        )
        back = back.astype(BF16)
        if c * chunk < piece_a:
            keep_ref[:cap, cols] = back[:cap]
            keep_ref[cap:, cols] = back[2 * cap : 3 * cap]
            a_ref[:cap, cols] = back[cap : 2 * cap]
            a_ref[cap:, cols] = back[3 * cap :]
            source, target, to = a_ref, a_out, cols
        else:
            to = slice(c * chunk - piece_a, (c + 1) * chunk - piece_a)
            keep_ref[:, cols] = back[: 2 * cap]
            b_ref[:, to] = back[2 * cap :]
            source, target = b_ref, b_out
        writes.append(
            pltpu.make_async_copy(keep_ref.at[:, cols], keep_out.at[:, cols], out_sem.at[2 * c])
        )
        writes[-1].start()
        writes.append(
            pltpu.make_async_copy(
                source.at[:, to], target.at[: 2 * cap, to], out_sem.at[2 * c + 1]
            )
        )
        writes[-1].start()
    for copy in writes:
        copy.wait()


def make_back(part, other, factors, w_gate, w_up, sizes, group, room, name):
    tok, feats, piece_a, chunk, cap, top = sizes
    hidden = part.shape[1]
    count = PLANE * cap
    steps = feats // chunk
    anywhere = pl.BlockSpec(memory_space=pl.ANY)
    widths = [feats, piece_a, feats - piece_a]
    heights = [2 * cap, 2 * cap + room, 2 * cap + room]
    return pl.pallas_call(
        functools.partial(back_kernel, sizes, group, room),
        in_specs=[anywhere] * 6,
        out_specs=[anywhere] * 3,
        scratch_shapes=[
            pltpu.VMEM((count, hidden), part.dtype),
            pltpu.VMEM((count, hidden), other.dtype),
            pltpu.VMEM((count, hidden), BF16),
            pltpu.VMEM((count, hidden), BF16),
            pltpu.VMEM((feats, hidden), BF16),
            pltpu.VMEM((feats, hidden), BF16),
            pltpu.VMEM((count, hidden), BF16),
            pltpu.VMEM((count, hidden), BF16),
            *[pltpu.VMEM((2 * cap, w), BF16) for w in widths],
            pltpu.SemaphoreType.DMA((4,)),
            pltpu.SemaphoreType.DMA((2 * steps,)),
            pltpu.SemaphoreType.DMA((2 * steps,)),
        ],
        out_shape=[jax.ShapeDtypeStruct((h, w), BF16) for h, w in zip(heights, widths)],
        compiler_params=params(VMEM_MIB),
        cost_estimate=COST,
        name=name,
    )(part, other, *factors, w_gate, w_up)


def spread_kernel(top, cap, who_ref, mz, mx, my, out_ref):
    me = who_ref[0]
    width = max(LANES, 2 * cap)
    tok = mz.shape[0]
    for i, (meta_ref, bit) in enumerate(((mz, 1), (my, 1), (mz, 2), (mx, 2))):
        meta = meta_ref[...].astype(F32)
        mine = ranks(meta, me, top, width)[:, : 2 * cap]
        theirs = ranks(meta, me ^ bit, top, width)[:, : 2 * cap]
        lane = lax.broadcasted_iota(jnp.int32, mine.shape, 1)
        off = jnp.where(lane < cap, mine, theirs + cap) - lane.astype(F32)
        out_ref[i * tok : (i + 1) * tok, :] = jnp.where(off == 0.0, 1.0, 0.0).astype(BF16)


def make_spread(who, z, x, y, sizes, name):
    tok, feats, piece_a, chunk, cap, top = sizes

    def meta(piece):
        place = piece.shape[1] // LANES - 1
        return pl.BlockSpec((tok, LANES), lambda i, who: (0, place))

    return pl.pallas_call(
        functools.partial(spread_kernel, top, cap),
        grid_spec=pltpu.PrefetchScalarGridSpec(
            num_scalar_prefetch=1,
            grid=(1,),
            in_specs=[meta(z), meta(x), meta(y)],
            out_specs=pl.BlockSpec((4 * tok, 2 * cap), lambda i, who: (0, 0)),
        ),
        out_shape=jax.ShapeDtypeStruct((4 * tok, 2 * cap), BF16),
        compiler_params=params(VMEM_MIB, 1),
        cost_estimate=COST,
        name=name,
    )(who, z, x, y)


def join_kernel(sizes, hot, keep, got_a, got_b, *refs):
    tok, feats, piece_a, chunk, cap, top = sizes
    out_ref, a_ref, b_ref = refs[-3:]

    def tokens(i, at, cols, got):
        both = jnp.concatenate([keep[at, cols], got[at, :]], axis=0)
        return dot(hot[i * tok : (i + 1) * tok, :], both).astype(BF16)

    near, far = slice(0, cap), slice(cap, 2 * cap)
    cols_a, cols_b = slice(0, piece_a), slice(piece_a, feats)
    a_ref[...] = tokens(1, far, cols_a, got_a)
    b_ref[...] = tokens(3, far, cols_b, got_b)
    out_ref[:, cols_a] = tokens(0, near, cols_a, got_a)
    out_ref[:, cols_b] = tokens(2, near, cols_b, got_b)


def join(hot, keep, got_a, got_b, into, sizes, name):
    tok, feats, piece_a, chunk, cap, top = sizes
    widths = (feats, piece_a, feats - piece_a)

    def whole(shape, row=0):
        return pl.BlockSpec(shape, lambda i: (row, 0))

    out_specs = [whole((tok, w)) for w in widths]
    out_shape = [jax.ShapeDtypeStruct((tok, w), BF16) for w in widths]
    aliases = {}
    if into:
        for_x, for_y = into
        place = for_x.shape[0] // tok - 1
        out_specs[1:] = [whole((tok, w), place) for w in widths[1:]]
        out_shape[1:] = [jax.ShapeDtypeStruct(a.shape, BF16) for a in (for_y, for_x)]
        aliases = {4: 1, 5: 2}
        into = [for_y, for_x]
    in_specs = [whole(a.shape) for a in (hot, keep)] + [whole((2 * cap, w)) for w in widths[1:]]
    return pl.pallas_call(
        functools.partial(join_kernel, sizes),
        grid=(1,),
        in_specs=in_specs + [pl.BlockSpec(memory_space=pl.ANY)] * len(into),
        out_specs=out_specs,
        out_shape=out_shape,
        input_output_aliases=aliases,
        compiler_params=params(VMEM_MIB, 1),
        cost_estimate=COST,
        name=name,
    )(hot, keep, got_a, got_b, *into)


def add_kernel(pieces, kept, *refs):
    got, others, out_ref = refs[:pieces], refs[pieces:-1], refs[-1]
    lo = 0
    for got_ref in got:
        at = slice(lo, lo + got_ref.shape[1])
        total = kept[:, at].astype(F32) + got_ref[...].astype(F32)
        for other in others:
            total += other[:, at].astype(F32)
        out_ref[:, at] = total.astype(BF16)
        lo = at.stop


def add(kept, got, others, name):
    tok = kept.shape[0]
    some = tok // 2 if tok % 32 == 0 else tok

    def part(a):
        skip = (a.shape[0] - tok) // some
        return pl.BlockSpec((some, a.shape[1]), lambda i: (i + skip, 0))

    args = [kept, *got, *others]
    return pl.pallas_call(
        functools.partial(add_kernel, len(got)),
        grid=(tok // some,),
        in_specs=[part(a) for a in args],
        out_specs=part(kept),
        out_shape=jax.ShapeDtypeStruct(kept.shape, BF16),
        compiler_params=params(VMEM_MIB, 1),
        cost_estimate=COST,
        name=name,
    )(*args)


def total_kernel(*refs):
    *parts, out_ref = refs
    total = parts[0][...].astype(F32)
    for part in parts[1:]:
        total += part[...].astype(F32)
    out_ref[...] = total.astype(BF16)


def total_of(first, others):
    vmem = pl.BlockSpec(memory_space=pltpu.VMEM)
    return pl.pallas_call(
        total_kernel,
        in_specs=[vmem] * (1 + len(others)),
        out_specs=vmem,
        out_shape=jax.ShapeDtypeStruct(first.shape, BF16),
        compiler_params=params(VMEM_MIB),
        cost_estimate=COST,
        name="total",
    )(first, *others)


def own_kernel(groups, flag_ref, act_ref, pact_ref, *refs):
    rows, prows, out_ref = refs[:groups], refs[groups : 2 * groups], refs[-1]
    count = rows[0].shape[0]

    def product(a_ref, b_refs, order):
        total = None
        for g in range(groups):
            at = order(g) * count
            term = dot(a_ref[:, at : at + count], b_refs[g][...])
            total = term if total is None else total + term
        return total.astype(BF16).astype(F32)

    own = product(act_ref, rows, lambda g: g)
    paired = product(pact_ref, prows, lambda g: g ^ (groups // 2))
    out_ref[...] = (own + flag_ref[0] * paired).astype(BF16)


def make_own(flag, act, pact, rows, prows, before, start, count, chunk, feats, name):
    groups = len(rows)
    hidden, width = act.shape
    full = pl.BlockSpec((hidden, width), lambda i, flag: (0, 0))
    part = pl.BlockSpec((rows[0].shape[0], chunk), lambda i, flag: (0, i + start))
    in_specs = [full, full] + [part] * (2 * groups)
    args = [flag, act, pact, *rows, *prows]
    aliases = {}
    if before is not None:
        in_specs.append(pl.BlockSpec(memory_space=pl.ANY))
        aliases = {len(args): 0}
        args.append(before)
    return pl.pallas_call(
        functools.partial(own_kernel, groups),
        grid_spec=pltpu.PrefetchScalarGridSpec(
            num_scalar_prefetch=1,
            grid=(count,),
            in_specs=in_specs,
            out_specs=pl.BlockSpec((hidden, chunk), lambda i, flag: (0, i + start)),
        ),
        out_shape=jax.ShapeDtypeStruct((hidden, feats), BF16),
        input_output_aliases=aliases,
        compiler_params=params(VMEM_MIB, 1),
        cost_estimate=COST,
        name=name,
    )(*args)


def after(value, *first):
    return lax.optimization_barrier((value, first))[0]


def sync(*values):
    return lax.optimization_barrier(values)


def flip(block, bits):
    count = lax.axis_size("node")
    return lax.ppermute(block, "node", [(i, i ^ bits) for i in range(count)])


def planes(block, pairs):
    route = [(PLANE * a + i, PLANE * b + i) for a, b in pairs for i in range(PLANE)]
    return lax.ppermute(block, "node", route)


def body(grad_out, gate_prob, routes, paired, saved_pre, w_gate, w_up, w_down):
    tok, feats = grad_out.shape
    nodes = lax.axis_size("node")
    locals_ = lax.axis_size("local")
    top = routes.shape[1]
    cap = saved_pre.shape[2]
    hidden = saved_pre.shape[4]
    groups = nodes // PLANE
    half = nodes // 2
    piece_a = feats // (2 * LANES) * LANES
    widths = (768, 512, 384, 256, 128)
    chunk = max(c for c in widths if piece_a % c == 0 and (feats - piece_a) % c == 0)
    own_chunk = max(c for c in (512, 384, 256, 128) if feats % c == 0)
    sizes = (tok, feats, piece_a, chunk, cap, top)
    back_chunk = max(c for c in (512, 384, 256, 128) if piece_a % c == 0 and (feats - piece_a) % c == 0)
    back_sizes = (tok, feats, piece_a, back_chunk, cap, top)
    w_down, w_gate, w_up = w_down[0], w_gate[0], w_up[0]
    ring = [(i, (i + 1) % locals_) for i in range(locals_)]

    me = lax.axis_index("node")
    side = lax.axis_index("local")
    who = jnp.stack([me, side, me ^ half]).astype(jnp.int32)
    flag = jnp.sum(jnp.where(jnp.arange(half, dtype=jnp.int32) == me % half, paired, 0)).astype(F32)[None]

    zs, xs, ys, ds, hot, rows, prows, parts, state, sums = ({} for _ in range(10))
    block = attach(grad_out, routes, gate_prob)
    zs[0] = [block]
    saved_rows = saved_pre[0].reshape(nodes * cap, 2, hidden)
    g_rows, u_rows = saved_rows[:, 0, :], saved_rows[:, 1, :]

    def flips(pieces, bits):
        return [flip(piece, bits) for piece in pieces]

    def beside(g):
        xs[g], ys[g] = flips(zs[g], 1), flips(zs[g], 2)

    def corner(g, pieces=None):
        from_x, from_y = pieces or cut(xs[g][0], ys[g][0], piece_a)
        ds[g] = [flip(from_x, 2), flip(from_y, 1)]

    def spreads(g, done):
        hot[g] = make_spread(after(who, done), zs[g][-1], xs[g][-1], ys[g][-1], sizes, f"spread_{g}")

    made = {}

    def near_rows(g, done):
        blocks = [zs[g], xs[g], ys[g]]
        made[g] = make_rows(after(who, done), blocks, 0, (), w_down, sizes, f"near_{g}")

    def to_rows(g, done):
        if g in made:
            call = [ds[g]], PLANE - 1, made[g]
        else:
            call = [zs[g], xs[g], ys[g], ds[g]], 0, ()
        rows[g], prows[g], parts[g] = make_rows(after(who, done), *call, w_down, sizes, f"partial_{g}")

    def exchange(g):
        piece = lax.ppermute(parts[g], "local", ring)
        if locals_ > 2:
            other = piece.astype(F32)
            for _ in range(locals_ - 2):
                piece = lax.ppermute(piece, "local", ring)
                other = other + piece.astype(F32)
            piece = other
        parts[g] = [parts[g], piece]

    def to_back(g, done, room=0):
        mine, other = parts[g]
        state[g] = make_back(
            after(mine, done), other, factors, w_gate, w_up, back_sizes, g, room, f"back_{g}"
        )

    def first_hop(g):
        keep, send_a, send_b = state[g]
        state[g] = [keep, flip(send_a, 1), flip(send_b, 2)]

    def second_hop(g):
        kept, send_a, send_b = join(hot[g], *state[g], [], sizes, f"join_{g}")
        state[g] = [kept, flip(send_a, 2), flip(send_b, 1)]

    def both_hops(g, h):
        keep, for_x, for_y = state[h]
        kept, for_y, for_x = join(hot[g], *state[g], [for_x, for_y], sizes, f"join_{g}")
        got_x, got_y = flip(for_x, 1), flip(for_y, 2)
        state[g] = [kept, got_y, got_x]
        state[h] = [keep, got_x, got_y]

    def plane_sum(g, others):
        kept, *got = state[g]
        return add(kept, got, others, f"sum_{g}")

    share = hidden // locals_

    def fetch_share(part, count):
        some = share // count
        return flip(lax.dynamic_slice_in_dim(act, side * share + part * some, some, 0), half)

    def all_shares(pieces):
        whole = jnp.zeros((hidden, nodes * cap), BF16)
        done = 0
        for piece in pieces:
            some = piece.shape[0]
            for i in range(locals_):
                start = (side - i) % locals_ * share + done
                whole = lax.dynamic_update_slice_in_dim(whole, piece, start, 0)
                if i < locals_ - 1:
                    piece = lax.ppermute(piece, "local", ring)
            done += some
        return whole

    steps = feats // own_chunk
    calls = min(2, steps)

    def own(c, before, done):
        start, stop = steps * c // calls, steps * (c + 1) // calls
        lists = [[r[g] for g in range(groups)] for r in (rows, prows)]
        return make_own(
            after(flag, done), act, pact, *lists, before, start, stop - start, own_chunk, feats, f"own_{c}"
        )

    def activate(done):
        return activations(after(who, done), g_rows, u_rows, cap)

    if groups != 4 or 2 * piece_a != feats or tok != 2 * cap:
        act, *factors = activate(block)
        pact = all_shares([fetch_share(0, 1)])
        done = act
        for g in range(groups):
            if g:
                zs[g] = [flip(after(block, done), PLANE * g)]
            beside(g)
            corner(g)
            spreads(g, done)
            to_rows(g, done)
            exchange(g)
            to_back(g, done)
            first_hop(g)
            second_hop(g)
            sums[g] = done = plane_sum(g, [])
            if g:
                sums[g] = done = flip(sums[g], PLANE * g)
        grad_down = None
        for c in range(calls):
            grad_down = own(c, grad_down, done)
        return (total_of(sums[0], [sums[g] for g in range(1, groups)]), grad_down[None])

    inward, outward = [(1, 2), (2, 1)], [(1, 0), (2, 3)]
    plane = me // PLANE
    middle = (plane == 1) | (plane == 2)

    beside(0)
    one, over = flip(block, PLANE), planes(block, inward)
    xs[0], ys[0], one, over, g_rows, u_rows = sync(xs[0], ys[0], one, over, g_rows, u_rows)

    zs[1] = [one]
    beside(1)
    second, edge_two = planes(one, inward), planes(over, outward)
    act, *factors = activate(xs[0])
    spreads(0, act)
    near_rows(0, hot[0])
    xs[1], ys[1], second, edge_two, hot[0], act, factors, made[0] = sync(
        xs[1], ys[1], second, edge_two, hot[0], act, factors, made[0]
    )

    zs[2] = [jnp.where(middle, second, edge_two)]
    beside(2)
    edge_three = planes(second, outward)
    spreads(1, zs[2][0])
    cut_zero = cut(after(xs[0][0], hot[1]), ys[0][0], piece_a)
    cut_one = cut(after(xs[1][0], cut_zero), ys[1][0], piece_a)
    near_rows(1, cut_one)
    xs[2], ys[2], edge_three, hot[1], cut_zero, cut_one, made[1] = sync(
        xs[2], ys[2], edge_three, hot[1], cut_zero, cut_one, made[1]
    )

    cut_two = cut(xs[2][0], ys[2][0], piece_a)
    corner(2, cut_two)
    zs[3] = [jnp.where(middle, over, after(edge_three, cut_two))]
    beside(3)
    spreads(2, zs[3][0])
    to_rows(2, hot[2])
    exchange(2)
    xs[3], ys[3], hot[2], rows[2], prows[2], parts[2] = sync(
        xs[3], ys[3], hot[2], rows[2], prows[2], parts[2]
    )

    corner(3)
    corner(1, cut_one)
    mine = [fetch_share(0, 2)]
    to_back(2, xs[3])
    to_rows(3, state[2][0])
    ds[1], state[2], rows[3], prows[3], parts[3], mine = sync(
        ds[1], state[2], rows[3], prows[3], parts[3], mine
    )

    exchange(3)
    first_hop(2)
    corner(0, cut_zero)
    mine += [fetch_share(2, 4)]
    to_back(3, state[2][0], tok)
    to_rows(1, state[3][0])
    state[2], ds[0], state[3], rows[1], prows[1], parts[1], mine = sync(
        state[2], ds[0], state[3], rows[1], prows[1], parts[1], mine
    )

    exchange(1)
    both_hops(2, 3)
    mine += [fetch_share(3, 4)]
    spreads(3, state[2][0])
    to_back(1, hot[3], tok)
    to_rows(0, state[1][0])
    state[2], state[3], state[1], rows[0], prows[0], parts[0], hot[3], mine = sync(
        state[2], state[3], state[1], rows[0], prows[0], parts[0], hot[3], mine
    )

    exchange(0)
    both_hops(3, 1)
    sums[2] = flip(plane_sum(2, []), PLANE)
    pact = all_shares(mine)
    to_back(0, state[3][0], tok)
    sums[2], state[3], state[1], state[0], pact = sync(sums[2], state[3], state[1], state[0], pact)

    total = plane_sum(3, [sums[2]])
    sums[3] = flip(total, 3 * PLANE)
    state[1] = after(state[1], total)
    both_hops(1, 0)
    grad_down = own(0, None, state[1][0])
    state[1], state[0], grad_down = sync(state[1], state[0], grad_down)

    sums[1] = flip(plane_sum(1, []), PLANE)
    second_hop(0)
    for c in range(1, calls):
        grad_down = own(c, grad_down, state[0][0])
    state[0], sums[1], sums[3], grad_down = sync(state[0], sums[1], sums[3], grad_down)
    return (plane_sum(0, [sums[1], sums[3]]), grad_down[None])


def solution(mesh):
    in_specs = (
        P("node", "local"),
        P("node", None),
        P("node", None),
        P(),
        P("node", None, None, None, None),
        P("node", "local", None),
        P("node", "local", None),
        P("node", None, "local"),
    )
    out_specs = (P("node", "local"), P("node", None, "local"))
    return jax.shard_map(body, mesh=mesh, in_specs=in_specs, out_specs=out_specs, check_vma=False)
```

```python
import functools

import jax
import jax.numpy as jnp
from jax import lax
from jax.experimental import pallas as pl
from jax.experimental.pallas import tpu as pltpu
from jax.sharding import PartitionSpec as P

F32 = jnp.float32
BF16 = jnp.bfloat16
LANES = 128
MIB = 1 << 20
VMEM_MIB = 64
PLANE = 4
CONTRACT_LAST = (((1,), (1,)), ((), ()))


def params(mib, ndims=0):
    sem = ("arbitrary",) * ndims if ndims else None
    return pltpu.CompilerParams(vmem_limit_bytes=mib * MIB - (MIB >> 4), dimension_semantics=sem)


COST = pl.CostEstimate(flops=1000, bytes_accessed=1000, transcendentals=0)


def dot(a, b):
    return jnp.dot(a, b, preferred_element_type=F32)


def attach_kernel(top, grad_ref, routes_ref, gate_ref, out_ref):
    tok, feats = grad_ref.shape
    out_ref[:, :feats] = grad_ref[...]
    gate = gate_ref[...]
    high = gate.astype(BF16).astype(F32)
    mid = (gate - high).astype(BF16).astype(F32)
    low = gate - high - mid
    names = routes_ref[...].astype(F32)
    pad = jnp.zeros((LANES - 4 * top, tok), F32)
    meta = jnp.concatenate([names, high, mid, low, pad], axis=0)
    out_ref[:, feats:] = jnp.transpose(meta).astype(BF16)


def attach(grad_out, routes, gate_prob):
    tok, feats = grad_out.shape
    routes, gate_prob = routes.T, gate_prob.T
    return pl.pallas_call(
        functools.partial(attach_kernel, routes.shape[0]),
        out_shape=jax.ShapeDtypeStruct((tok, feats + LANES), BF16),
        compiler_params=params(VMEM_MIB),
        cost_estimate=COST,
        name="attach",
    )(grad_out, routes, gate_prob)


def cut_kernel(piece_a, x, y, a_out, b_out, a_ref, b_ref, sem):
    pieces = ((x.at[:, :piece_a], a_ref, a_out), (y.at[:, piece_a:], b_ref, b_out))
    loads = [pltpu.make_async_copy(s, v, sem.at[i]) for i, (s, v, _) in enumerate(pieces)]
    stores = [pltpu.make_async_copy(v, t, sem.at[2 + i]) for i, (_, v, t) in enumerate(pieces)]
    for load in loads:
        load.start()
    for load, store in zip(loads, stores):
        load.wait()
        store.start()
    for store in stores:
        store.wait()


def cut(x, y, piece_a):
    tok, width = x.shape
    anywhere = pl.BlockSpec(memory_space=pl.ANY)
    widths = (piece_a, width - piece_a)
    return pl.pallas_call(
        functools.partial(cut_kernel, piece_a),
        in_specs=[anywhere] * 2,
        out_specs=[anywhere] * 2,
        out_shape=[jax.ShapeDtypeStruct((tok, w), BF16) for w in widths],
        scratch_shapes=[*[pltpu.VMEM((tok, w), BF16) for w in widths], pltpu.SemaphoreType.DMA((4,))],
        compiler_params=params(VMEM_MIB),
        cost_estimate=COST,
        name="cut",
    )(x, y)


def ranks(meta, slot, top, width):
    tok = meta.shape[0]
    lane = lax.broadcasted_iota(jnp.int32, meta.shape, 1)
    hit = jnp.where((lane < top) & (meta == slot.astype(F32)), 1.0, 0.0)
    named = jnp.broadcast_to(jnp.sum(hit, axis=1, keepdims=True), (tok, width))
    row = lax.broadcasted_iota(jnp.int32, (tok, tok), 0)
    col = lax.broadcasted_iota(jnp.int32, (tok, tok), 1)
    earlier = jnp.where(row > col, 1.0, 0.0).astype(BF16)
    return jnp.where(named > 0.5, dot(earlier, named.astype(BF16)), -1.0)


def row_gates(picked, slot, top):
    lane = lax.broadcasted_iota(jnp.int32, picked.shape, 1)
    high = pltpu.roll(picked, LANES - top, 1)
    mid = pltpu.roll(picked, LANES - 2 * top, 1)
    low = pltpu.roll(picked, LANES - 3 * top, 1)
    gate = (high + mid) + low
    chosen = jnp.where((lane < top) & (picked == slot.astype(F32)), gate, 0.0)
    return jnp.sum(chosen, axis=1, keepdims=True)


def selection(meta_refs, slots, top, cap, sel_ref, gate_ref):
    at = 0
    for meta_ref in meta_refs:
        meta = meta_ref[...]
        for slot in slots:
            rank = ranks(meta.astype(F32), slot, top, LANES)
            turned = jnp.transpose(rank)[:cap]
            want = lax.broadcasted_iota(jnp.int32, turned.shape, 0).astype(F32)
            sel = jnp.where(turned == want, 1.0, 0.0).astype(BF16)
            sel_ref[at : at + cap, :] = sel
            gates = row_gates(dot(sel, meta), slot, top)
            gate_ref[at : at + cap, :] = jnp.broadcast_to(gates, (cap, LANES))
            at += cap


def staged(copies, ahead=2):
    for copy in copies[:ahead]:
        copy.start()
    place = iter(range(len(copies)))

    def arrive():
        c = next(place)
        copies[c].wait()
        if c + ahead < len(copies):
            copies[c + ahead].start()

    return arrive


def rows_kernel(sizes, layout, first, many, waits, who_ref, wd, *refs):
    tok, feats, piece_a, chunk, cap, top = sizes
    blocks, refs = refs[: len(layout)], refs[len(layout) + waits :]
    rows_out, prows_out, part_out, *refs = refs
    tok_ref, wd_ref, rows_ref, prows_ref, sel_ref, gate_ref, acc_ref, part_ref, m_sem, b_sem, w_sem, out_sem = refs
    steps = feats // chunk
    place = slice(first * cap, (first + many) * cap)
    metas, weights, writes = [], [], []
    bodies = [[] for _ in range(steps)]
    for (q, lo), block in zip(layout, blocks):
        if lo + block.shape[1] > feats:
            copy = pltpu.make_async_copy(block.at[:, feats - lo :], tok_ref.at[q, :, feats:], m_sem.at[q])
            copy.start()
            metas.append(copy)
    for c in range(steps):
        at = c * chunk
        for (q, lo), block in zip(layout, blocks):
            if lo <= at < min(lo + block.shape[1], feats):
                source = block.at[:, at - lo : at - lo + chunk]
                copy = pltpu.make_async_copy(source, tok_ref.at[q, :, at : at + chunk], b_sem.at[c * many + q])
                copy.start()
                bodies[c].append(copy)
        cols = slice(at, at + chunk)
        weights.append(pltpu.make_async_copy(wd.at[:, cols], wd_ref.at[:, cols], w_sem.at[c]))
    weight_arrives = staged(weights)
    for copy in metas:
        copy.wait()
    selection(
        [tok_ref.at[q, :, feats:] for q in range(many)], (who_ref[0], who_ref[2]), top, cap, sel_ref, gate_ref
    )
    for c in range(steps):
        cols = slice(c * chunk, (c + 1) * chunk)
        for copy in bodies[c]:
            copy.wait()
        for q in range(many):
            at = slice(2 * q * cap, 2 * (q + 1) * cap)
            both = (dot(sel_ref[at, :], tok_ref[q, :, cols]) * gate_ref[at, :1]).astype(BF16)
            rows_ref[q * cap : (q + 1) * cap, cols] = both[:cap]
            prows_ref[q * cap : (q + 1) * cap, cols] = both[cap:]
        for i, (source, target) in enumerate(((rows_ref, rows_out), (prows_ref, prows_out))):
            writes.append(
                pltpu.make_async_copy(source.at[:, cols], target.at[place, cols], out_sem.at[2 * c + i])
            )
            writes[-1].start()
        weight_arrives()
        term = lax.dot_general(
            rows_ref[:, cols], wd_ref[:, cols], CONTRACT_LAST, preferred_element_type=F32
        )
        if c == 0 and steps > 1:
            acc_ref[...] = term
        elif c < steps - 1:
            acc_ref[...] += term
        else:
            part_ref[...] = ((acc_ref[...] + term) if steps > 1 else term).astype(BF16)
    writes.append(pltpu.make_async_copy(part_ref, part_out.at[place, :], out_sem.at[2 * steps]))
    writes[-1].start()
    for copy in writes:
        copy.wait()


def make_rows(who, blocks, first, before, w_down, sizes, name):
    tok, feats, piece_a, chunk, cap, top = sizes
    hidden = w_down.shape[0]
    count = PLANE * cap
    many = len(blocks)
    steps = feats // chunk
    layout, pieces = [], []
    for q, block in enumerate(blocks):
        lo = 0
        for piece in block:
            layout.append((q, lo))
            pieces.append(piece)
            lo += piece.shape[1]
    anywhere = pl.BlockSpec(memory_space=pl.ANY)
    return pl.pallas_call(
        functools.partial(rows_kernel, sizes, layout, first, many, len(before)),
        in_specs=[pl.BlockSpec(memory_space=pltpu.SMEM)] + [anywhere] * (1 + len(pieces) + len(before)),
        out_specs=[anywhere] * 3,
        scratch_shapes=[
            pltpu.VMEM((many, tok, feats + LANES), BF16),
            pltpu.VMEM((hidden, feats), BF16),
            pltpu.VMEM((many * cap, feats), BF16),
            pltpu.VMEM((many * cap, feats), BF16),
            pltpu.VMEM((2 * many * cap, tok), BF16),
            pltpu.VMEM((2 * many * cap, LANES), F32),
            pltpu.VMEM((many * cap, hidden), F32),
            pltpu.VMEM((many * cap, hidden), BF16),
            pltpu.SemaphoreType.DMA((many,)),
            pltpu.SemaphoreType.DMA((many * steps,)),
            pltpu.SemaphoreType.DMA((steps,)),
            pltpu.SemaphoreType.DMA((2 * steps + 1,)),
        ],
        out_shape=[
            jax.ShapeDtypeStruct((count, feats), BF16),
            jax.ShapeDtypeStruct((count, feats), BF16),
            jax.ShapeDtypeStruct((count, hidden), BF16),
        ],
        input_output_aliases={2 + len(pieces) + i: i for i in range(len(before))},
        compiler_params=params(VMEM_MIB),
        cost_estimate=COST,
        name=name,
    )(who, w_down, *pieces, *before)


def act_kernel(cap, many, who_ref, g_ref, u_ref, act_ref, dg_ref, du_ref):
    rows = g_ref.shape[0]
    width = many * cap
    for i in range(rows // width):
        pieces = []
        for q in range(many):
            at = pl.ds(pl.multiple_of((who_ref[0] ^ (i * many + q)) * cap, cap), cap)
            g = g_ref[at, :].astype(F32)
            u = u_ref[at, :].astype(F32)
            sig = jax.nn.sigmoid(g)
            pieces.append(g * sig * u)
            to = slice((i * many + q) * cap, (i * many + q + 1) * cap)
            dg_ref[to, :] = (u * sig * (1.0 + g * (1.0 - sig))).astype(BF16)
            du_ref[to, :] = (g * sig).astype(BF16)
        block = jnp.concatenate(pieces, axis=0) if many > 1 else pieces[0]
        act_ref[:, i * width : (i + 1) * width] = jnp.transpose(block).astype(BF16)


def activations(who, g, u, cap):
    rows, hidden = g.shape
    many = max(1, LANES // cap)
    vmem = pl.BlockSpec(memory_space=pltpu.VMEM)
    return pl.pallas_call(
        functools.partial(act_kernel, cap, many),
        in_specs=[pl.BlockSpec(memory_space=pltpu.SMEM), vmem, vmem],
        out_specs=[vmem] * 3,
        out_shape=[
            jax.ShapeDtypeStruct((hidden, rows), BF16),
            jax.ShapeDtypeStruct((rows, hidden), BF16),
            jax.ShapeDtypeStruct((rows, hidden), BF16),
        ],
        compiler_params=params(VMEM_MIB),
        cost_estimate=COST,
        name="activation",
    )(who, g, u)


def back_kernel(sizes, group, room, mine, other, dg_all, du_all, wg, wu, keep_out, a_out, b_out, *refs):
    tok, feats, piece_a, chunk, cap, top = sizes
    m_ref, o_ref, fg_ref, fu_ref, wg_ref, wu_ref, dg_ref, du_ref, keep_ref, a_ref, b_ref, sem, w_sem, out_sem = refs
    steps = feats // chunk
    count = PLANE * cap
    at = slice(group * count, (group + 1) * count)
    loads, weights, writes = [], [], []
    pairs = ((mine, m_ref), (other, o_ref), (dg_all.at[at, :], fg_ref), (du_all.at[at, :], fu_ref))
    for i, (source, target) in enumerate(pairs):
        loads.append(pltpu.make_async_copy(source, target, sem.at[i]))
        loads[-1].start()
    for c in range(steps):
        rows = slice(c * chunk, (c + 1) * chunk)
        for i, (source, target) in enumerate(((wg, wg_ref), (wu, wu_ref))):
            weights.append(
                pltpu.make_async_copy(source.at[rows, :], target.at[rows, :], w_sem.at[2 * c + i])
            )
    weight_arrives = staged(weights, 4)
    for copy in loads:
        copy.wait()
    for q in range(PLANE):
        rows = slice(q * cap, (q + 1) * cap)
        dhid = m_ref[rows, :].astype(F32) + o_ref[rows, :].astype(F32)
        dg_ref[rows, :] = (dhid * fg_ref[rows, :].astype(F32)).astype(BF16)
        du_ref[rows, :] = (dhid * fu_ref[rows, :].astype(F32)).astype(BF16)
    for c in range(steps):
        cols = slice(c * chunk, (c + 1) * chunk)
        weight_arrives()
        weight_arrives()
        back = lax.dot_general(
            dg_ref[...], wg_ref[cols, :], CONTRACT_LAST, preferred_element_type=F32
        )
        back += lax.dot_general(
            du_ref[...], wu_ref[cols, :], CONTRACT_LAST, preferred_element_type=F32
        )
        back = back.astype(BF16)
        if c * chunk < piece_a:
            keep_ref[:cap, cols] = back[:cap]
            keep_ref[cap:, cols] = back[2 * cap : 3 * cap]
            a_ref[:cap, cols] = back[cap : 2 * cap]
            a_ref[cap:, cols] = back[3 * cap :]
            source, target, to = a_ref, a_out, cols
        else:
            to = slice(c * chunk - piece_a, (c + 1) * chunk - piece_a)
            keep_ref[:, cols] = back[: 2 * cap]
            b_ref[:, to] = back[2 * cap :]
            source, target = b_ref, b_out
        writes.append(
            pltpu.make_async_copy(keep_ref.at[:, cols], keep_out.at[:, cols], out_sem.at[2 * c])
        )
        writes[-1].start()
        writes.append(
            pltpu.make_async_copy(
                source.at[:, to], target.at[: 2 * cap, to], out_sem.at[2 * c + 1]
            )
        )
        writes[-1].start()
    for copy in writes:
        copy.wait()


def make_back(part, other, factors, w_gate, w_up, sizes, group, room, name):
    tok, feats, piece_a, chunk, cap, top = sizes
    hidden = part.shape[1]
    count = PLANE * cap
    steps = feats // chunk
    anywhere = pl.BlockSpec(memory_space=pl.ANY)
    widths = [feats, piece_a, feats - piece_a]
    heights = [2 * cap, 2 * cap + room, 2 * cap + room]
    return pl.pallas_call(
        functools.partial(back_kernel, sizes, group, room),
        in_specs=[anywhere] * 6,
        out_specs=[anywhere] * 3,
        scratch_shapes=[
            pltpu.VMEM((count, hidden), part.dtype),
            pltpu.VMEM((count, hidden), other.dtype),
            pltpu.VMEM((count, hidden), BF16),
            pltpu.VMEM((count, hidden), BF16),
            pltpu.VMEM((feats, hidden), BF16),
            pltpu.VMEM((feats, hidden), BF16),
            pltpu.VMEM((count, hidden), BF16),
            pltpu.VMEM((count, hidden), BF16),
            *[pltpu.VMEM((2 * cap, w), BF16) for w in widths],
            pltpu.SemaphoreType.DMA((4,)),
            pltpu.SemaphoreType.DMA((2 * steps,)),
            pltpu.SemaphoreType.DMA((2 * steps,)),
        ],
        out_shape=[jax.ShapeDtypeStruct((h, w), BF16) for h, w in zip(heights, widths)],
        compiler_params=params(VMEM_MIB),
        cost_estimate=COST,
        name=name,
    )(part, other, *factors, w_gate, w_up)


def spread_kernel(top, cap, who_ref, mz, mx, my, out_ref):
    me = who_ref[0]
    width = max(LANES, 2 * cap)
    tok = mz.shape[0]
    for i, (meta_ref, bit) in enumerate(((mz, 1), (my, 1), (mz, 2), (mx, 2))):
        meta = meta_ref[...].astype(F32)
        mine = ranks(meta, me, top, width)[:, : 2 * cap]
        theirs = ranks(meta, me ^ bit, top, width)[:, : 2 * cap]
        lane = lax.broadcasted_iota(jnp.int32, mine.shape, 1)
        off = jnp.where(lane < cap, mine, theirs + cap) - lane.astype(F32)
        out_ref[i * tok : (i + 1) * tok, :] = jnp.where(off == 0.0, 1.0, 0.0).astype(BF16)


def make_spread(who, z, x, y, sizes, name):
    tok, feats, piece_a, chunk, cap, top = sizes

    def meta(piece):
        place = piece.shape[1] // LANES - 1
        return pl.BlockSpec((tok, LANES), lambda i, who: (0, place))

    return pl.pallas_call(
        functools.partial(spread_kernel, top, cap),
        grid_spec=pltpu.PrefetchScalarGridSpec(
            num_scalar_prefetch=1,
            grid=(1,),
            in_specs=[meta(z), meta(x), meta(y)],
            out_specs=pl.BlockSpec((4 * tok, 2 * cap), lambda i, who: (0, 0)),
        ),
        out_shape=jax.ShapeDtypeStruct((4 * tok, 2 * cap), BF16),
        compiler_params=params(VMEM_MIB, 1),
        cost_estimate=COST,
        name=name,
    )(who, z, x, y)


def join_kernel(sizes, waits, hot, keep, got_a, got_b, *refs):
    tok, feats, piece_a, chunk, cap, top = sizes
    refs = refs[waits:]
    summed = len(refs) > 3
    if summed:
        *parts, out_ref, a_ref, b_ref, total_ref = refs
    else:
        out_ref, a_ref, b_ref = refs

    def tokens(i, at, cols, got):
        both = jnp.concatenate([keep[at, cols], got[at, :]], axis=0)
        return dot(hot[i * tok : (i + 1) * tok, :], both).astype(BF16)

    near, far = slice(0, cap), slice(cap, 2 * cap)
    cols_a, cols_b = slice(0, piece_a), slice(piece_a, feats)
    a_ref[...] = tokens(1, far, cols_a, got_a)
    b_ref[...] = tokens(3, far, cols_b, got_b)
    out_ref[:, cols_a] = tokens(0, near, cols_a, got_a)
    out_ref[:, cols_b] = tokens(2, near, cols_b, got_b)
    if summed:
        add_kernel(2, *parts, total_ref)


def join(hot, keep, got_a, got_b, into, sizes, name, addends=None):
    tok, feats, piece_a, chunk, cap, top = sizes
    widths = (feats, piece_a, feats - piece_a)

    def whole(shape, row=0):
        return pl.BlockSpec(shape, lambda i: (row, 0))

    out_specs = [whole((tok, w)) for w in widths]
    out_shape = [jax.ShapeDtypeStruct((tok, w), BF16) for w in widths]
    aliases = {}
    if into:
        for_x, for_y = into
        place = for_x.shape[0] // tok - 1
        out_specs[1:] = [whole((tok, w), place) for w in widths[1:]]
        out_shape[1:] = [jax.ShapeDtypeStruct(a.shape, BF16) for a in (for_y, for_x)]
        aliases = {4: 1, 5: 2}
        into = [for_y, for_x]
    in_specs = [whole(a.shape) for a in (hot, keep)] + [whole((2 * cap, w)) for w in widths[1:]]
    in_specs += [pl.BlockSpec(memory_space=pl.ANY)] * len(into)
    args = [hot, keep, got_a, got_b, *into]
    if addends:
        kept, got, others = addends
        for a in (kept, *got, *others):
            in_specs.append(whole((tok, a.shape[1]), a.shape[0] // tok - 1))
            args.append(a)
        out_specs.append(whole((tok, feats)))
        out_shape.append(jax.ShapeDtypeStruct((tok, feats), BF16))
    return pl.pallas_call(
        functools.partial(join_kernel, sizes, len(into)),
        grid=(1,),
        in_specs=in_specs,
        out_specs=out_specs,
        out_shape=out_shape,
        input_output_aliases=aliases,
        compiler_params=params(VMEM_MIB, 1),
        cost_estimate=COST,
        name=name,
    )(*args)


def add_kernel(pieces, kept, *refs):
    got, others, out_ref = refs[:pieces], refs[pieces:-1], refs[-1]
    lo = 0
    for got_ref in got:
        at = slice(lo, lo + got_ref.shape[1])
        total = kept[:, at].astype(F32) + got_ref[...].astype(F32)
        for other in others:
            total += other[:, at].astype(F32)
        out_ref[:, at] = total.astype(BF16)
        lo = at.stop


def add(kept, got, others, name):
    tok = kept.shape[0]
    some = tok // 2 if tok % 32 == 0 else tok

    def part(a):
        skip = (a.shape[0] - tok) // some
        return pl.BlockSpec((some, a.shape[1]), lambda i: (i + skip, 0))

    args = [kept, *got, *others]
    return pl.pallas_call(
        functools.partial(add_kernel, len(got)),
        grid=(tok // some,),
        in_specs=[part(a) for a in args],
        out_specs=part(kept),
        out_shape=jax.ShapeDtypeStruct(kept.shape, BF16),
        compiler_params=params(VMEM_MIB, 1),
        cost_estimate=COST,
        name=name,
    )(*args)


def total_kernel(*refs):
    *parts, out_ref = refs
    total = parts[0][...].astype(F32)
    for part in parts[1:]:
        total += part[...].astype(F32)
    out_ref[...] = total.astype(BF16)


def total_of(first, others):
    vmem = pl.BlockSpec(memory_space=pltpu.VMEM)
    return pl.pallas_call(
        total_kernel,
        in_specs=[vmem] * (1 + len(others)),
        out_specs=vmem,
        out_shape=jax.ShapeDtypeStruct(first.shape, BF16),
        compiler_params=params(VMEM_MIB),
        cost_estimate=COST,
        name="total",
    )(first, *others)


def own_kernel(groups, spots, locals_, flag_ref, who_ref, act_ref, *refs):
    pieces, refs = refs[: len(spots)], refs[len(spots) :]
    rows, prows, (out_ref, pact_ref, sem) = refs[:groups], refs[groups : 2 * groups], refs[-3:]
    count = rows[0].shape[0]
    share = act_ref.shape[0] // locals_

    def loads():
        for n, ((turn, first), piece) in enumerate(zip(spots, pieces)):
            owner = lax.rem(who_ref[1] - turn + locals_, locals_)
            start = pl.multiple_of(owner * share + first, 16)
            yield pltpu.make_async_copy(piece, pact_ref.at[pl.ds(start, piece.shape[0]), :], sem.at[n])

    @pl.when(pl.program_id(0) == 0)
    def _():
        for copy in loads():
            copy.start()

    def product(a_ref, b_refs, order):
        total = None
        for g in range(groups):
            at = order(g) * count
            term = dot(a_ref[:, at : at + count], b_refs[g][...])
            total = term if total is None else total + term
        return total.astype(BF16).astype(F32)

    own = product(act_ref, rows, lambda g: g)

    @pl.when(pl.program_id(0) == 0)
    def _():
        for copy in loads():
            copy.wait()

    paired = product(pact_ref, prows, lambda g: g ^ (groups // 2))
    out_ref[...] = (own + flag_ref[0] * paired).astype(BF16)


def make_own(flag, who, act, pact, rows, prows, before, start, count, chunk, feats, locals_, name):
    groups = len(rows)
    hidden, width = act.shape
    spots = [spot for spot, _ in pact]
    part = pl.BlockSpec((rows[0].shape[0], chunk), lambda i, flag, who: (0, i + start))
    anywhere = pl.BlockSpec(memory_space=pl.ANY)
    in_specs = [pl.BlockSpec((hidden, width), lambda i, flag, who: (0, 0))]
    in_specs += [anywhere] * len(pact) + [part] * (2 * groups)
    args = [flag, who, act, *[piece for _, piece in pact], *rows, *prows]
    aliases = {}
    if before is not None:
        in_specs.append(anywhere)
        aliases = {len(args): 0}
        args.append(before)
    return pl.pallas_call(
        functools.partial(own_kernel, groups, spots, locals_),
        grid_spec=pltpu.PrefetchScalarGridSpec(
            num_scalar_prefetch=2,
            grid=(count,),
            in_specs=in_specs,
            out_specs=pl.BlockSpec((hidden, chunk), lambda i, flag, who: (0, i + start)),
            scratch_shapes=[pltpu.VMEM((hidden, width), BF16), pltpu.SemaphoreType.DMA((len(pact),))],
        ),
        out_shape=jax.ShapeDtypeStruct((hidden, feats), BF16),
        input_output_aliases=aliases,
        compiler_params=params(VMEM_MIB, 1),
        cost_estimate=COST,
        name=name,
    )(*args)


def after(value, *first):
    return lax.optimization_barrier((value, first))[0]


def sync(*values):
    return lax.optimization_barrier(values)


def flip(block, bits):
    count = lax.axis_size("node")
    return lax.ppermute(block, "node", [(i, i ^ bits) for i in range(count)])


def planes(block, pairs):
    route = [(PLANE * a + i, PLANE * b + i) for a, b in pairs for i in range(PLANE)]
    return lax.ppermute(block, "node", route)


def body(grad_out, gate_prob, routes, paired, saved_pre, w_gate, w_up, w_down):
    tok, feats = grad_out.shape
    nodes = lax.axis_size("node")
    locals_ = lax.axis_size("local")
    top = routes.shape[1]
    cap = saved_pre.shape[2]
    hidden = saved_pre.shape[4]
    groups = nodes // PLANE
    half = nodes // 2
    piece_a = feats // (2 * LANES) * LANES
    widths = (768, 512, 384, 256, 128)
    chunk = max(c for c in widths if piece_a % c == 0 and (feats - piece_a) % c == 0)
    own_chunk = max(c for c in (512, 384, 256, 128) if feats % c == 0)
    sizes = (tok, feats, piece_a, chunk, cap, top)
    back_chunk = max(c for c in (512, 384, 256, 128) if piece_a % c == 0 and (feats - piece_a) % c == 0)
    back_sizes = (tok, feats, piece_a, back_chunk, cap, top)
    w_down, w_gate, w_up = w_down[0], w_gate[0], w_up[0]
    ring = [(i, (i + 1) % locals_) for i in range(locals_)]

    me = lax.axis_index("node")
    side = lax.axis_index("local")
    who = jnp.stack([me, side, me ^ half]).astype(jnp.int32)
    flag = jnp.sum(jnp.where(jnp.arange(half, dtype=jnp.int32) == me % half, paired, 0)).astype(F32)[None]

    zs, xs, ys, ds, hot, rows, prows, parts, state, sums = ({} for _ in range(10))
    block = attach(grad_out, routes, gate_prob)
    zs[0] = [block]
    saved_rows = saved_pre[0].reshape(nodes * cap, 2, hidden)
    g_rows, u_rows = saved_rows[:, 0, :], saved_rows[:, 1, :]

    def flips(pieces, bits):
        return [flip(piece, bits) for piece in pieces]

    def beside(g):
        xs[g], ys[g] = flips(zs[g], 1), flips(zs[g], 2)

    def corner(g, pieces=None):
        from_x, from_y = pieces or cut(xs[g][0], ys[g][0], piece_a)
        ds[g] = [flip(from_x, 2), flip(from_y, 1)]

    def spreads(g, done):
        hot[g] = make_spread(after(who, done), zs[g][-1], xs[g][-1], ys[g][-1], sizes, f"spread_{g}")

    made = {}

    def near_rows(g, done):
        blocks = [zs[g], xs[g], ys[g]]
        made[g] = make_rows(after(who, done), blocks, 0, (), w_down, sizes, f"near_{g}")

    def to_rows(g, done):
        if g in made:
            call = [ds[g]], PLANE - 1, made[g]
        else:
            call = [zs[g], xs[g], ys[g], ds[g]], 0, ()
        rows[g], prows[g], parts[g] = make_rows(after(who, done), *call, w_down, sizes, f"partial_{g}")

    def exchange(g):
        piece = lax.ppermute(parts[g], "local", ring)
        if locals_ > 2:
            other = piece.astype(F32)
            for _ in range(locals_ - 2):
                piece = lax.ppermute(piece, "local", ring)
                other = other + piece.astype(F32)
            piece = other
        parts[g] = [parts[g], piece]

    def to_back(g, done, room=0):
        mine, other = parts[g]
        state[g] = make_back(
            after(mine, done), other, factors, w_gate, w_up, back_sizes, g, room, f"back_{g}"
        )

    def first_hop(g):
        keep, send_a, send_b = state[g]
        state[g] = [keep, flip(send_a, 1), flip(send_b, 2)]

    def second_hop(g, addends=None):
        kept, send_a, send_b, *total = join(hot[g], *state[g], [], sizes, f"join_{g}", addends)
        state[g] = [kept, flip(send_a, 2), flip(send_b, 1)]
        return total

    def both_hops(g, h, addends=None):
        keep, for_x, for_y = state[h]
        kept, for_y, for_x, *total = join(hot[g], *state[g], [for_x, for_y], sizes, f"join_{g}", addends)
        got_x, got_y = flip(for_x, 1), flip(for_y, 2)
        state[g] = [kept, got_y, got_x]
        state[h] = [keep, got_x, got_y]
        return total

    def addends(g, others):
        kept, *got = state[g]
        return kept, got, others

    def plane_sum(g, others):
        kept, *got = state[g]
        return add(kept, got, others, f"sum_{g}")

    share = hidden // locals_

    def cut_share(part, count):
        some = share // count
        return lax.dynamic_slice_in_dim(act, side * share + part * some, some, 0)

    def all_shares(pieces):
        found, first = [], 0
        for piece in pieces:
            for turn in range(locals_):
                found.append(((turn, first), piece))
                if turn < locals_ - 1:
                    piece = lax.ppermute(piece, "local", ring)
            first += piece.shape[0]
        return found

    steps = feats // own_chunk
    calls = min(2, steps)

    def own(c, before, done):
        start, stop = steps * c // calls, steps * (c + 1) // calls
        lists = [[r[g] for g in range(groups)] for r in (rows, prows)]
        return make_own(
            after(flag, done), who, act, pact, *lists, before, start, stop - start, own_chunk, feats, locals_, f"own_{c}"
        )

    def activate(done):
        return activations(after(who, done), g_rows, u_rows, cap)

    if groups != 4 or 2 * piece_a != feats or tok != 2 * cap:
        act, *factors = activate(block)
        pact = all_shares([flip(cut_share(0, 1), half)])
        done = act
        for g in range(groups):
            if g:
                zs[g] = [flip(after(block, done), PLANE * g)]
            beside(g)
            corner(g)
            spreads(g, done)
            to_rows(g, done)
            exchange(g)
            to_back(g, done)
            first_hop(g)
            second_hop(g)
            sums[g] = done = plane_sum(g, [])
            if g:
                sums[g] = done = flip(sums[g], PLANE * g)
        grad_down = None
        for c in range(calls):
            grad_down = own(c, grad_down, done)
        return (total_of(sums[0], [sums[g] for g in range(1, groups)]), grad_down[None])

    inward, outward = [(1, 2), (2, 1)], [(1, 0), (2, 3)]
    plane = me // PLANE
    middle = (plane == 1) | (plane == 2)

    beside(0)
    one, over = flip(block, PLANE), planes(block, inward)
    xs[0], ys[0], one, over, g_rows, u_rows = sync(xs[0], ys[0], one, over, g_rows, u_rows)

    zs[1] = [one]
    second, edge_two = planes(one, inward), planes(over, outward)
    beside(1)
    act, *factors = activate(xs[0])
    spreads(0, act)
    near_rows(0, hot[0])
    second, edge_two, xs[1], ys[1], hot[0], act, factors, made[0], flag = sync(
        second, edge_two, xs[1], ys[1], hot[0], act, factors, made[0], flag
    )

    edge_three = planes(second, outward)
    zs[2] = [jnp.where(middle, second, edge_two)]
    beside(2)
    spreads(1, zs[2][0])
    cut_zero = cut(after(xs[0][0], hot[1]), ys[0][0], piece_a)
    cut_one = cut(after(xs[1][0], cut_zero), ys[1][0], piece_a)
    near_rows(1, cut_one)
    shares = [cut_share(0, 2), cut_share(2, 4), cut_share(3, 4)]
    edge_three, xs[2], ys[2], hot[1], cut_zero, cut_one, made[1], shares = sync(
        edge_three, xs[2], ys[2], hot[1], cut_zero, cut_one, made[1], shares
    )

    cut_two = cut(xs[2][0], ys[2][0], piece_a)
    corner(2, cut_two)
    zs[3] = [jnp.where(middle, over, after(edge_three, cut_two))]
    beside(3)
    spreads(2, zs[3][0])
    to_rows(2, hot[2])
    exchange(2)
    xs[3], ys[3], hot[2], rows[2], prows[2], parts[2] = sync(
        xs[3], ys[3], hot[2], rows[2], prows[2], parts[2]
    )

    corner(3)
    corner(1, cut_one)
    mine = [flip(shares[0], half)]
    to_back(2, xs[3])
    to_rows(3, state[2][0])
    ds[1], state[2], rows[3], prows[3], parts[3], mine = sync(
        ds[1], state[2], rows[3], prows[3], parts[3], mine
    )

    exchange(3)
    first_hop(2)
    corner(0, cut_zero)
    mine += [flip(shares[1], half)]
    to_back(3, state[2][0], tok)
    to_rows(1, state[3][0])
    state[2], ds[0], state[3], rows[1], prows[1], parts[1], mine = sync(
        state[2], ds[0], state[3], rows[1], prows[1], parts[1], mine
    )

    exchange(1)
    both_hops(2, 3)
    mine += [flip(shares[2], half)]
    spreads(3, state[2][0])
    to_back(1, hot[3], tok)
    to_rows(0, state[1][0])
    state[2], state[3], state[1], rows[0], prows[0], parts[0], hot[3], mine = sync(
        state[2], state[3], state[1], rows[0], prows[0], parts[0], hot[3], mine
    )

    exchange(0)
    (total,) = both_hops(3, 1, addends(2, []))
    sums[2] = flip(total, PLANE)
    pact = all_shares(mine)
    to_back(0, state[3][0], tok)
    spots, pieces = [spot for spot, _ in pact], [piece for _, piece in pact]
    sums[2], state[3], state[1], state[0], pieces = sync(sums[2], state[3], state[1], state[0], pieces)
    pact = list(zip(spots, pieces))

    (total,) = both_hops(1, 0, addends(3, [sums[2]]))
    sums[3] = flip(total, 3 * PLANE)
    grad_down = own(0, None, state[1][0])
    state[1], state[0], grad_down = sync(state[1], state[0], grad_down)

    (total,) = second_hop(0, addends(1, []))
    sums[1] = flip(total, PLANE)
    for c in range(1, calls):
        grad_down = own(c, grad_down, state[0][0])
    state[0], sums[1], sums[3], grad_down = sync(state[0], sums[1], sums[3], grad_down)
    return (plane_sum(0, [sums[1], sums[3]]), grad_down[None])


def solution(mesh):
    in_specs = (
        P("node", "local"),
        P("node", None),
        P("node", None),
        P(),
        P("node", None, None, None, None),
        P("node", "local", None),
        P("node", "local", None),
        P("node", None, "local"),
    )
    out_specs = (P("node", "local"), P("node", None, "local"))
    return jax.shard_map(body, mesh=mesh, in_specs=in_specs, out_specs=out_specs, check_vma=False)
```

```python
import functools

import jax
import jax.numpy as jnp
from jax import lax
from jax.experimental import pallas as pl
from jax.experimental.pallas import tpu as pltpu
from jax.sharding import PartitionSpec as P

F32 = jnp.float32
BF16 = jnp.bfloat16
LANES = 128
MIB = 1 << 20
VMEM_MIB = 64
PLANE = 4
CONTRACT_LAST = (((1,), (1,)), ((), ()))


def params(mib, ndims=0):
    sem = ("arbitrary",) * ndims if ndims else None
    return pltpu.CompilerParams(vmem_limit_bytes=mib * MIB - (MIB >> 4), dimension_semantics=sem)


COST = pl.CostEstimate(flops=1000, bytes_accessed=1000, transcendentals=0)


def dot(a, b):
    return jnp.dot(a, b, preferred_element_type=F32)


def attach_kernel(top, grad_ref, routes_ref, gate_ref, out_ref):
    tok, feats = grad_ref.shape
    out_ref[:, :feats] = grad_ref[...]
    gate = gate_ref[...]
    high = gate.astype(BF16).astype(F32)
    mid = (gate - high).astype(BF16).astype(F32)
    low = gate - high - mid
    names = routes_ref[...].astype(F32)
    pad = jnp.zeros((LANES - 4 * top, tok), F32)
    meta = jnp.concatenate([names, high, mid, low, pad], axis=0)
    out_ref[:, feats:] = jnp.transpose(meta).astype(BF16)


def attach(grad_out, routes, gate_prob):
    tok, feats = grad_out.shape
    routes, gate_prob = routes.T, gate_prob.T
    return pl.pallas_call(
        functools.partial(attach_kernel, routes.shape[0]),
        out_shape=jax.ShapeDtypeStruct((tok, feats + LANES), BF16),
        compiler_params=params(VMEM_MIB),
        cost_estimate=COST,
        name="attach",
    )(grad_out, routes, gate_prob)


def cut_kernel(piece_a, x, y, a_out, b_out, a_ref, b_ref, sem):
    pieces = ((x.at[:, :piece_a], a_ref, a_out), (y.at[:, piece_a:], b_ref, b_out))
    loads = [pltpu.make_async_copy(s, v, sem.at[i]) for i, (s, v, _) in enumerate(pieces)]
    stores = [pltpu.make_async_copy(v, t, sem.at[2 + i]) for i, (_, v, t) in enumerate(pieces)]
    for load in loads:
        load.start()
    for load, store in zip(loads, stores):
        load.wait()
        store.start()
    for store in stores:
        store.wait()


def cut(x, y, piece_a):
    tok, width = x.shape
    anywhere = pl.BlockSpec(memory_space=pl.ANY)
    widths = (piece_a, width - piece_a)
    return pl.pallas_call(
        functools.partial(cut_kernel, piece_a),
        in_specs=[anywhere] * 2,
        out_specs=[anywhere] * 2,
        out_shape=[jax.ShapeDtypeStruct((tok, w), BF16) for w in widths],
        scratch_shapes=[*[pltpu.VMEM((tok, w), BF16) for w in widths], pltpu.SemaphoreType.DMA((4,))],
        compiler_params=params(VMEM_MIB),
        cost_estimate=COST,
        name="cut",
    )(x, y)


def ranks(meta, slot, top, width):
    tok = meta.shape[0]
    lane = lax.broadcasted_iota(jnp.int32, meta.shape, 1)
    hit = jnp.where((lane < top) & (meta == slot.astype(F32)), 1.0, 0.0)
    named = jnp.broadcast_to(jnp.sum(hit, axis=1, keepdims=True), (tok, width))
    row = lax.broadcasted_iota(jnp.int32, (tok, tok), 0)
    col = lax.broadcasted_iota(jnp.int32, (tok, tok), 1)
    earlier = jnp.where(row > col, 1.0, 0.0).astype(BF16)
    return jnp.where(named > 0.5, dot(earlier, named.astype(BF16)), -1.0)


def row_gates(picked, slot, top):
    lane = lax.broadcasted_iota(jnp.int32, picked.shape, 1)
    high = pltpu.roll(picked, LANES - top, 1)
    mid = pltpu.roll(picked, LANES - 2 * top, 1)
    low = pltpu.roll(picked, LANES - 3 * top, 1)
    gate = (high + mid) + low
    chosen = jnp.where((lane < top) & (picked == slot.astype(F32)), gate, 0.0)
    return jnp.sum(chosen, axis=1, keepdims=True)


def selection(meta_refs, slots, top, cap, sel_ref, gate_ref):
    at = 0
    for meta_ref in meta_refs:
        meta = meta_ref[...]
        for slot in slots:
            rank = ranks(meta.astype(F32), slot, top, LANES)
            turned = jnp.transpose(rank)[:cap]
            want = lax.broadcasted_iota(jnp.int32, turned.shape, 0).astype(F32)
            sel = jnp.where(turned == want, 1.0, 0.0).astype(BF16)
            sel_ref[at : at + cap, :] = sel
            gates = row_gates(dot(sel, meta), slot, top)
            gate_ref[at : at + cap, :] = jnp.broadcast_to(gates, (cap, LANES))
            at += cap


def staged(copies, ahead=2):
    for copy in copies[:ahead]:
        copy.start()
    place = iter(range(len(copies)))

    def arrive():
        c = next(place)
        copies[c].wait()
        if c + ahead < len(copies):
            copies[c + ahead].start()

    return arrive


def rows_kernel(sizes, layout, first, many, waits, who_ref, wd, *refs):
    tok, feats, piece_a, chunk, cap, top = sizes
    blocks, refs = refs[: len(layout)], refs[len(layout) + waits :]
    rows_out, prows_out, part_out, *refs = refs
    tok_ref, wd_ref, rows_ref, prows_ref, sel_ref, gate_ref, acc_ref, part_ref, m_sem, b_sem, w_sem, out_sem = refs
    steps = feats // chunk
    place = slice(first * cap, (first + many) * cap)
    metas, weights, writes = [], [], []
    bodies = [[] for _ in range(steps)]
    for (q, lo), block in zip(layout, blocks):
        if lo + block.shape[1] > feats:
            copy = pltpu.make_async_copy(block.at[:, feats - lo :], tok_ref.at[q, :, feats:], m_sem.at[q])
            copy.start()
            metas.append(copy)
    for c in range(steps):
        at = c * chunk
        for (q, lo), block in zip(layout, blocks):
            if lo <= at < min(lo + block.shape[1], feats):
                source = block.at[:, at - lo : at - lo + chunk]
                copy = pltpu.make_async_copy(source, tok_ref.at[q, :, at : at + chunk], b_sem.at[c * many + q])
                copy.start()
                bodies[c].append(copy)
        cols = slice(at, at + chunk)
        weights.append(pltpu.make_async_copy(wd.at[:, cols], wd_ref.at[:, cols], w_sem.at[c]))
    weight_arrives = staged(weights)
    for copy in metas:
        copy.wait()
    selection(
        [tok_ref.at[q, :, feats:] for q in range(many)], (who_ref[0], who_ref[2]), top, cap, sel_ref, gate_ref
    )
    for c in range(steps):
        cols = slice(c * chunk, (c + 1) * chunk)
        for copy in bodies[c]:
            copy.wait()
        for q in range(many):
            at = slice(2 * q * cap, 2 * (q + 1) * cap)
            both = (dot(sel_ref[at, :], tok_ref[q, :, cols]) * gate_ref[at, :1]).astype(BF16)
            rows_ref[q * cap : (q + 1) * cap, cols] = both[:cap]
            prows_ref[q * cap : (q + 1) * cap, cols] = both[cap:]
        for i, (source, target) in enumerate(((rows_ref, rows_out), (prows_ref, prows_out))):
            writes.append(
                pltpu.make_async_copy(source.at[:, cols], target.at[place, cols], out_sem.at[2 * c + i])
            )
            writes[-1].start()
        weight_arrives()
        term = lax.dot_general(
            rows_ref[:, cols], wd_ref[:, cols], CONTRACT_LAST, preferred_element_type=F32
        )
        if c == 0 and steps > 1:
            acc_ref[...] = term
        elif c < steps - 1:
            acc_ref[...] += term
        else:
            part_ref[...] = ((acc_ref[...] + term) if steps > 1 else term).astype(BF16)
    writes.append(pltpu.make_async_copy(part_ref, part_out.at[place, :], out_sem.at[2 * steps]))
    writes[-1].start()
    for copy in writes:
        copy.wait()


def make_rows(who, blocks, first, before, w_down, sizes, name):
    tok, feats, piece_a, chunk, cap, top = sizes
    hidden = w_down.shape[0]
    count = PLANE * cap
    many = len(blocks)
    steps = feats // chunk
    layout, pieces = [], []
    for q, block in enumerate(blocks):
        lo = 0
        for piece in block:
            layout.append((q, lo))
            pieces.append(piece)
            lo += piece.shape[1]
    anywhere = pl.BlockSpec(memory_space=pl.ANY)
    return pl.pallas_call(
        functools.partial(rows_kernel, sizes, layout, first, many, len(before)),
        in_specs=[pl.BlockSpec(memory_space=pltpu.SMEM)] + [anywhere] * (1 + len(pieces) + len(before)),
        out_specs=[anywhere] * 3,
        scratch_shapes=[
            pltpu.VMEM((many, tok, feats + LANES), BF16),
            pltpu.VMEM((hidden, feats), BF16),
            pltpu.VMEM((many * cap, feats), BF16),
            pltpu.VMEM((many * cap, feats), BF16),
            pltpu.VMEM((2 * many * cap, tok), BF16),
            pltpu.VMEM((2 * many * cap, LANES), F32),
            pltpu.VMEM((many * cap, hidden), F32),
            pltpu.VMEM((many * cap, hidden), BF16),
            pltpu.SemaphoreType.DMA((many,)),
            pltpu.SemaphoreType.DMA((many * steps,)),
            pltpu.SemaphoreType.DMA((steps,)),
            pltpu.SemaphoreType.DMA((2 * steps + 1,)),
        ],
        out_shape=[
            jax.ShapeDtypeStruct((count, feats), BF16),
            jax.ShapeDtypeStruct((count, feats), BF16),
            jax.ShapeDtypeStruct((count, hidden), BF16),
        ],
        input_output_aliases={2 + len(pieces) + i: i for i in range(len(before))},
        compiler_params=params(VMEM_MIB),
        cost_estimate=COST,
        name=name,
    )(who, w_down, *pieces, *before)


def act_kernel(cap, many, who_ref, g_ref, u_ref, act_ref, dg_ref, du_ref):
    rows = g_ref.shape[0]
    width = many * cap
    for i in range(rows // width):
        pieces = []
        for q in range(many):
            at = pl.ds(pl.multiple_of((who_ref[0] ^ (i * many + q)) * cap, cap), cap)
            g = g_ref[at, :].astype(F32)
            u = u_ref[at, :].astype(F32)
            sig = jax.nn.sigmoid(g)
            pieces.append(g * sig * u)
            to = slice((i * many + q) * cap, (i * many + q + 1) * cap)
            dg_ref[to, :] = (u * sig * (1.0 + g * (1.0 - sig))).astype(BF16)
            du_ref[to, :] = (g * sig).astype(BF16)
        block = jnp.concatenate(pieces, axis=0) if many > 1 else pieces[0]
        act_ref[:, i * width : (i + 1) * width] = jnp.transpose(block).astype(BF16)


def activations(who, g, u, cap):
    rows, hidden = g.shape
    many = max(1, LANES // cap)
    vmem = pl.BlockSpec(memory_space=pltpu.VMEM)
    return pl.pallas_call(
        functools.partial(act_kernel, cap, many),
        in_specs=[pl.BlockSpec(memory_space=pltpu.SMEM), vmem, vmem],
        out_specs=[vmem] * 3,
        out_shape=[
            jax.ShapeDtypeStruct((hidden, rows), BF16),
            jax.ShapeDtypeStruct((rows, hidden), BF16),
            jax.ShapeDtypeStruct((rows, hidden), BF16),
        ],
        compiler_params=params(VMEM_MIB),
        cost_estimate=COST,
        name="activation",
    )(who, g, u)


def back_kernel(sizes, group, room, mine, other, dg_all, du_all, wg, wu, keep_out, a_out, b_out, *refs):
    tok, feats, piece_a, chunk, cap, top = sizes
    m_ref, o_ref, fg_ref, fu_ref, wg_ref, wu_ref, dg_ref, du_ref, keep_ref, a_ref, b_ref, sem, w_sem, out_sem = refs
    steps = feats // chunk
    count = PLANE * cap
    at = slice(group * count, (group + 1) * count)
    loads, weights, writes = [], [], []
    pairs = ((mine, m_ref), (other, o_ref), (dg_all.at[at, :], fg_ref), (du_all.at[at, :], fu_ref))
    for i, (source, target) in enumerate(pairs):
        loads.append(pltpu.make_async_copy(source, target, sem.at[i]))
        loads[-1].start()
    for c in range(steps):
        rows = slice(c * chunk, (c + 1) * chunk)
        for i, (source, target) in enumerate(((wg, wg_ref), (wu, wu_ref))):
            weights.append(
                pltpu.make_async_copy(source.at[rows, :], target.at[rows, :], w_sem.at[2 * c + i])
            )
    weight_arrives = staged(weights, 4)
    for copy in loads:
        copy.wait()
    for q in range(PLANE):
        rows = slice(q * cap, (q + 1) * cap)
        dhid = m_ref[rows, :].astype(F32) + o_ref[rows, :].astype(F32)
        dg_ref[rows, :] = (dhid * fg_ref[rows, :].astype(F32)).astype(BF16)
        du_ref[rows, :] = (dhid * fu_ref[rows, :].astype(F32)).astype(BF16)
    for c in range(steps):
        cols = slice(c * chunk, (c + 1) * chunk)
        weight_arrives()
        weight_arrives()
        back = lax.dot_general(
            dg_ref[...], wg_ref[cols, :], CONTRACT_LAST, preferred_element_type=F32
        )
        back += lax.dot_general(
            du_ref[...], wu_ref[cols, :], CONTRACT_LAST, preferred_element_type=F32
        )
        back = back.astype(BF16)
        if c * chunk < piece_a:
            keep_ref[:cap, cols] = back[:cap]
            keep_ref[cap:, cols] = back[2 * cap : 3 * cap]
            a_ref[:cap, cols] = back[cap : 2 * cap]
            a_ref[cap:, cols] = back[3 * cap :]
            source, target, to = a_ref, a_out, cols
        else:
            to = slice(c * chunk - piece_a, (c + 1) * chunk - piece_a)
            keep_ref[:, cols] = back[: 2 * cap]
            b_ref[:, to] = back[2 * cap :]
            source, target = b_ref, b_out
        writes.append(
            pltpu.make_async_copy(keep_ref.at[:, cols], keep_out.at[:, cols], out_sem.at[2 * c])
        )
        writes[-1].start()
        writes.append(
            pltpu.make_async_copy(
                source.at[:, to], target.at[: 2 * cap, to], out_sem.at[2 * c + 1]
            )
        )
        writes[-1].start()
    for copy in writes:
        copy.wait()


def make_back(part, other, factors, w_gate, w_up, sizes, group, room, name):
    tok, feats, piece_a, chunk, cap, top = sizes
    hidden = part.shape[1]
    count = PLANE * cap
    steps = feats // chunk
    anywhere = pl.BlockSpec(memory_space=pl.ANY)
    widths = [feats, piece_a, feats - piece_a]
    heights = [2 * cap, 2 * cap + room, 2 * cap + room]
    return pl.pallas_call(
        functools.partial(back_kernel, sizes, group, room),
        in_specs=[anywhere] * 6,
        out_specs=[anywhere] * 3,
        scratch_shapes=[
            pltpu.VMEM((count, hidden), part.dtype),
            pltpu.VMEM((count, hidden), other.dtype),
            pltpu.VMEM((count, hidden), BF16),
            pltpu.VMEM((count, hidden), BF16),
            pltpu.VMEM((feats, hidden), BF16),
            pltpu.VMEM((feats, hidden), BF16),
            pltpu.VMEM((count, hidden), BF16),
            pltpu.VMEM((count, hidden), BF16),
            *[pltpu.VMEM((2 * cap, w), BF16) for w in widths],
            pltpu.SemaphoreType.DMA((4,)),
            pltpu.SemaphoreType.DMA((2 * steps,)),
            pltpu.SemaphoreType.DMA((2 * steps,)),
        ],
        out_shape=[jax.ShapeDtypeStruct((h, w), BF16) for h, w in zip(heights, widths)],
        compiler_params=params(VMEM_MIB),
        cost_estimate=COST,
        name=name,
    )(part, other, *factors, w_gate, w_up)


def spread_kernel(top, cap, who_ref, mz, mx, my, out_ref):
    me = who_ref[0]
    width = max(LANES, 2 * cap)
    tok = mz.shape[0]
    for i, (meta_ref, bit) in enumerate(((mz, 1), (my, 1), (mz, 2), (mx, 2))):
        meta = meta_ref[...].astype(F32)
        mine = ranks(meta, me, top, width)[:, : 2 * cap]
        theirs = ranks(meta, me ^ bit, top, width)[:, : 2 * cap]
        lane = lax.broadcasted_iota(jnp.int32, mine.shape, 1)
        off = jnp.where(lane < cap, mine, theirs + cap) - lane.astype(F32)
        out_ref[i * tok : (i + 1) * tok, :] = jnp.where(off == 0.0, 1.0, 0.0).astype(BF16)


def make_spread(who, z, x, y, sizes, name):
    tok, feats, piece_a, chunk, cap, top = sizes

    def meta(piece):
        place = piece.shape[1] // LANES - 1
        return pl.BlockSpec((tok, LANES), lambda i, who: (0, place))

    return pl.pallas_call(
        functools.partial(spread_kernel, top, cap),
        grid_spec=pltpu.PrefetchScalarGridSpec(
            num_scalar_prefetch=1,
            grid=(1,),
            in_specs=[meta(z), meta(x), meta(y)],
            out_specs=pl.BlockSpec((4 * tok, 2 * cap), lambda i, who: (0, 0)),
        ),
        out_shape=jax.ShapeDtypeStruct((4 * tok, 2 * cap), BF16),
        compiler_params=params(VMEM_MIB, 1),
        cost_estimate=COST,
        name=name,
    )(who, z, x, y)


def join_kernel(sizes, waits, hot, keep, got_a, got_b, *refs):
    tok, feats, piece_a, chunk, cap, top = sizes
    refs = refs[waits:]
    summed = len(refs) > 3
    if summed:
        *parts, out_ref, a_ref, b_ref, total_ref = refs
    else:
        out_ref, a_ref, b_ref = refs

    def tokens(i, at, cols, got):
        both = jnp.concatenate([keep[at, cols], got[at, :]], axis=0)
        return dot(hot[i * tok : (i + 1) * tok, :], both).astype(BF16)

    near, far = slice(0, cap), slice(cap, 2 * cap)
    cols_a, cols_b = slice(0, piece_a), slice(piece_a, feats)
    a_ref[...] = tokens(1, far, cols_a, got_a)
    b_ref[...] = tokens(3, far, cols_b, got_b)
    out_ref[:, cols_a] = tokens(0, near, cols_a, got_a)
    out_ref[:, cols_b] = tokens(2, near, cols_b, got_b)
    if summed:
        add_kernel(2, *parts, total_ref)


def join(hot, keep, got_a, got_b, into, sizes, name, addends=None):
    tok, feats, piece_a, chunk, cap, top = sizes
    widths = (feats, piece_a, feats - piece_a)

    def whole(shape, row=0):
        return pl.BlockSpec(shape, lambda i: (row, 0))

    out_specs = [whole((tok, w)) for w in widths]
    out_shape = [jax.ShapeDtypeStruct((tok, w), BF16) for w in widths]
    aliases = {}
    if into:
        for_x, for_y = into
        place = for_x.shape[0] // tok - 1
        out_specs[1:] = [whole((tok, w), place) for w in widths[1:]]
        out_shape[1:] = [jax.ShapeDtypeStruct(a.shape, BF16) for a in (for_y, for_x)]
        aliases = {4: 1, 5: 2}
        into = [for_y, for_x]
    in_specs = [whole(a.shape) for a in (hot, keep)] + [whole((2 * cap, w)) for w in widths[1:]]
    in_specs += [pl.BlockSpec(memory_space=pl.ANY)] * len(into)
    args = [hot, keep, got_a, got_b, *into]
    if addends:
        kept, got, others = addends
        for a in (kept, *got, *others):
            in_specs.append(whole((tok, a.shape[1]), a.shape[0] // tok - 1))
            args.append(a)
        out_specs.append(whole((tok, feats)))
        out_shape.append(jax.ShapeDtypeStruct((tok, feats), BF16))
    return pl.pallas_call(
        functools.partial(join_kernel, sizes, len(into)),
        grid=(1,),
        in_specs=in_specs,
        out_specs=out_specs,
        out_shape=out_shape,
        input_output_aliases=aliases,
        compiler_params=params(VMEM_MIB, 1),
        cost_estimate=COST,
        name=name,
    )(*args)


def add_kernel(pieces, kept, *refs):
    got, others, out_ref = refs[:pieces], refs[pieces:-1], refs[-1]
    lo = 0
    for got_ref in got:
        at = slice(lo, lo + got_ref.shape[1])
        total = kept[:, at].astype(F32) + got_ref[...].astype(F32)
        for other in others:
            total += other[:, at].astype(F32)
        out_ref[:, at] = total.astype(BF16)
        lo = at.stop


def add(kept, got, others, name):
    tok = kept.shape[0]
    some = tok // 2 if tok % 32 == 0 else tok

    def part(a):
        skip = (a.shape[0] - tok) // some
        return pl.BlockSpec((some, a.shape[1]), lambda i: (i + skip, 0))

    args = [kept, *got, *others]
    return pl.pallas_call(
        functools.partial(add_kernel, len(got)),
        grid=(tok // some,),
        in_specs=[part(a) for a in args],
        out_specs=part(kept),
        out_shape=jax.ShapeDtypeStruct(kept.shape, BF16),
        compiler_params=params(VMEM_MIB, 1),
        cost_estimate=COST,
        name=name,
    )(*args)


def total_kernel(*refs):
    *parts, out_ref = refs
    total = parts[0][...].astype(F32)
    for part in parts[1:]:
        total += part[...].astype(F32)
    out_ref[...] = total.astype(BF16)


def total_of(first, others):
    vmem = pl.BlockSpec(memory_space=pltpu.VMEM)
    return pl.pallas_call(
        total_kernel,
        in_specs=[vmem] * (1 + len(others)),
        out_specs=vmem,
        out_shape=jax.ShapeDtypeStruct(first.shape, BF16),
        compiler_params=params(VMEM_MIB),
        cost_estimate=COST,
        name="total",
    )(first, *others)


def own_kernel(groups, spots, locals_, flag_ref, who_ref, act_ref, *refs):
    pieces, refs = refs[: len(spots)], refs[len(spots) :]
    rows, prows, (out_ref, pact_ref, sem) = refs[:groups], refs[groups : 2 * groups], refs[-3:]
    count = rows[0].shape[0]
    share = act_ref.shape[0] // locals_

    def loads():
        for n, ((turn, first), piece) in enumerate(zip(spots, pieces)):
            owner = lax.rem(who_ref[1] - turn + locals_, locals_)
            start = pl.multiple_of(owner * share + first, 16)
            yield pltpu.make_async_copy(piece, pact_ref.at[pl.ds(start, piece.shape[0]), :], sem.at[n])

    @pl.when(pl.program_id(0) == 0)
    def _():
        for copy in loads():
            copy.start()

    def product(a_ref, b_refs, order):
        total = None
        for g in range(groups):
            at = order(g) * count
            term = dot(a_ref[:, at : at + count], b_refs[g][...])
            total = term if total is None else total + term
        return total.astype(BF16).astype(F32)

    own = product(act_ref, rows, lambda g: g)

    @pl.when(pl.program_id(0) == 0)
    def _():
        for copy in loads():
            copy.wait()

    paired = product(pact_ref, prows, lambda g: g ^ (groups // 2))
    out_ref[...] = (own + flag_ref[0] * paired).astype(BF16)


def make_own(flag, who, act, pact, rows, prows, before, start, count, chunk, feats, locals_, name):
    groups = len(rows)
    hidden, width = act.shape
    spots = [spot for spot, _ in pact]
    part = pl.BlockSpec((rows[0].shape[0], chunk), lambda i, flag, who: (0, i + start))
    anywhere = pl.BlockSpec(memory_space=pl.ANY)
    in_specs = [pl.BlockSpec((hidden, width), lambda i, flag, who: (0, 0))]
    in_specs += [anywhere] * len(pact) + [part] * (2 * groups)
    args = [flag, who, act, *[piece for _, piece in pact], *rows, *prows]
    aliases = {}
    if before is not None:
        in_specs.append(anywhere)
        aliases = {len(args): 0}
        args.append(before)
    return pl.pallas_call(
        functools.partial(own_kernel, groups, spots, locals_),
        grid_spec=pltpu.PrefetchScalarGridSpec(
            num_scalar_prefetch=2,
            grid=(count,),
            in_specs=in_specs,
            out_specs=pl.BlockSpec((hidden, chunk), lambda i, flag, who: (0, i + start)),
            scratch_shapes=[pltpu.VMEM((hidden, width), BF16), pltpu.SemaphoreType.DMA((len(pact),))],
        ),
        out_shape=jax.ShapeDtypeStruct((hidden, feats), BF16),
        input_output_aliases=aliases,
        compiler_params=params(VMEM_MIB, 1),
        cost_estimate=COST,
        name=name,
    )(*args)


def after(value, *first):
    return lax.optimization_barrier((value, first))[0]


def sync(*values):
    return lax.optimization_barrier(values)


def flip(block, bits):
    count = lax.axis_size("node")
    return lax.ppermute(block, "node", [(i, i ^ bits) for i in range(count)])


def planes(block, pairs):
    route = [(PLANE * a + i, PLANE * b + i) for a, b in pairs for i in range(PLANE)]
    return lax.ppermute(block, "node", route)


def body(grad_out, gate_prob, routes, paired, saved_pre, w_gate, w_up, w_down):
    tok, feats = grad_out.shape
    nodes = lax.axis_size("node")
    locals_ = lax.axis_size("local")
    top = routes.shape[1]
    cap = saved_pre.shape[2]
    hidden = saved_pre.shape[4]
    groups = nodes // PLANE
    half = nodes // 2
    piece_a = feats // (2 * LANES) * LANES
    widths = (1536, 768, 512, 384, 256, 128)
    chunk = max(c for c in widths if piece_a % c == 0 and (feats - piece_a) % c == 0)
    own_chunk = max(c for c in (512, 384, 256, 128) if feats % c == 0)
    sizes = (tok, feats, piece_a, chunk, cap, top)
    back_chunk = max(c for c in (512, 384, 256, 128) if piece_a % c == 0 and (feats - piece_a) % c == 0)
    back_sizes = (tok, feats, piece_a, back_chunk, cap, top)
    w_down, w_gate, w_up = w_down[0], w_gate[0], w_up[0]
    ring = [(i, (i + 1) % locals_) for i in range(locals_)]

    me = lax.axis_index("node")
    side = lax.axis_index("local")
    who = jnp.stack([me, side, me ^ half]).astype(jnp.int32)
    flag = jnp.sum(jnp.where(jnp.arange(half, dtype=jnp.int32) == me % half, paired, 0)).astype(F32)[None]

    zs, xs, ys, ds, hot, rows, prows, parts, state, sums = ({} for _ in range(10))
    block = attach(grad_out, routes, gate_prob)
    zs[0] = [block]
    saved_rows = saved_pre[0].reshape(nodes * cap, 2, hidden)
    g_rows, u_rows = saved_rows[:, 0, :], saved_rows[:, 1, :]

    def flips(pieces, bits):
        return [flip(piece, bits) for piece in pieces]

    def beside(g):
        xs[g], ys[g] = flips(zs[g], 1), flips(zs[g], 2)

    def corner(g, pieces=None):
        from_x, from_y = pieces or cut(xs[g][0], ys[g][0], piece_a)
        ds[g] = [flip(from_x, 2), flip(from_y, 1)]

    def spreads(g, done):
        hot[g] = make_spread(after(who, done), zs[g][-1], xs[g][-1], ys[g][-1], sizes, f"spread_{g}")

    made = {}

    def near_rows(g, done):
        blocks = [zs[g], xs[g], ys[g]]
        made[g] = make_rows(after(who, done), blocks, 0, (), w_down, sizes, f"near_{g}")

    def to_rows(g, done):
        if g in made:
            call = [ds[g]], PLANE - 1, made[g]
        else:
            call = [zs[g], xs[g], ys[g], ds[g]], 0, ()
        rows[g], prows[g], parts[g] = make_rows(after(who, done), *call, w_down, sizes, f"partial_{g}")

    def exchange(g):
        piece = lax.ppermute(parts[g], "local", ring)
        if locals_ > 2:
            other = piece.astype(F32)
            for _ in range(locals_ - 2):
                piece = lax.ppermute(piece, "local", ring)
                other = other + piece.astype(F32)
            piece = other
        parts[g] = [parts[g], piece]

    def to_back(g, done, room=0):
        mine, other = parts[g]
        state[g] = make_back(
            after(mine, done), other, factors, w_gate, w_up, back_sizes, g, room, f"back_{g}"
        )

    def first_hop(g):
        keep, send_a, send_b = state[g]
        state[g] = [keep, flip(send_a, 1), flip(send_b, 2)]

    def second_hop(g, addends=None):
        kept, send_a, send_b, *total = join(hot[g], *state[g], [], sizes, f"join_{g}", addends)
        state[g] = [kept, flip(send_a, 2), flip(send_b, 1)]
        return total

    def both_hops(g, h, addends=None):
        keep, for_x, for_y = state[h]
        kept, for_y, for_x, *total = join(hot[g], *state[g], [for_x, for_y], sizes, f"join_{g}", addends)
        got_x, got_y = flip(for_x, 1), flip(for_y, 2)
        state[g] = [kept, got_y, got_x]
        state[h] = [keep, got_x, got_y]
        return total

    def addends(g, others):
        kept, *got = state[g]
        return kept, got, others

    def plane_sum(g, others):
        kept, *got = state[g]
        return add(kept, got, others, f"sum_{g}")

    share = hidden // locals_

    def cut_share(part, count):
        some = share // count
        return lax.dynamic_slice_in_dim(act, side * share + part * some, some, 0)

    def all_shares(pieces):
        found, first = [], 0
        for piece in pieces:
            for turn in range(locals_):
                found.append(((turn, first), piece))
                if turn < locals_ - 1:
                    piece = lax.ppermute(piece, "local", ring)
            first += piece.shape[0]
        return found

    steps = feats // own_chunk
    calls = min(2, steps)

    def own(c, before, done):
        start, stop = steps * c // calls, steps * (c + 1) // calls
        lists = [[r[g] for g in range(groups)] for r in (rows, prows)]
        return make_own(
            after(flag, done), who, act, pact, *lists, before, start, stop - start, own_chunk, feats, locals_, f"own_{c}"
        )

    def activate(done):
        return activations(after(who, done), g_rows, u_rows, cap)

    if groups != 4 or 2 * piece_a != feats or tok != 2 * cap:
        act, *factors = activate(block)
        pact = all_shares([flip(cut_share(0, 1), half)])
        done = act
        for g in range(groups):
            if g:
                zs[g] = [flip(after(block, done), PLANE * g)]
            beside(g)
            corner(g)
            spreads(g, done)
            to_rows(g, done)
            exchange(g)
            to_back(g, done)
            first_hop(g)
            second_hop(g)
            sums[g] = done = plane_sum(g, [])
            if g:
                sums[g] = done = flip(sums[g], PLANE * g)
        grad_down = None
        for c in range(calls):
            grad_down = own(c, grad_down, done)
        return (total_of(sums[0], [sums[g] for g in range(1, groups)]), grad_down[None])

    inward, outward = [(1, 2), (2, 1)], [(1, 0), (2, 3)]
    plane = me // PLANE
    middle = (plane == 1) | (plane == 2)

    beside(0)
    one, over = flip(block, PLANE), planes(block, inward)
    xs[0], ys[0], one, over, g_rows, u_rows = sync(xs[0], ys[0], one, over, g_rows, u_rows)

    zs[1] = [one]
    second, edge_two = planes(one, inward), planes(over, outward)
    beside(1)
    act, *factors = activate(xs[0])
    spreads(0, act)
    near_rows(0, hot[0])
    second, edge_two, xs[1], ys[1], hot[0], act, factors, made[0], flag = sync(
        second, edge_two, xs[1], ys[1], hot[0], act, factors, made[0], flag
    )

    edge_three = planes(second, outward)
    zs[2] = [jnp.where(middle, second, edge_two)]
    beside(2)
    spreads(1, zs[2][0])
    cut_zero = cut(after(xs[0][0], hot[1]), ys[0][0], piece_a)
    cut_one = cut(after(xs[1][0], cut_zero), ys[1][0], piece_a)
    near_rows(1, cut_one)
    shares = [cut_share(0, 2), cut_share(2, 4), cut_share(3, 4)]
    edge_three, xs[2], ys[2], hot[1], cut_zero, cut_one, made[1], shares = sync(
        edge_three, xs[2], ys[2], hot[1], cut_zero, cut_one, made[1], shares
    )

    cut_two = cut(xs[2][0], ys[2][0], piece_a)
    corner(2, cut_two)
    zs[3] = [jnp.where(middle, over, after(edge_three, cut_two))]
    beside(3)
    spreads(2, zs[3][0])
    to_rows(2, hot[2])
    exchange(2)
    xs[3], ys[3], hot[2], rows[2], prows[2], parts[2] = sync(
        xs[3], ys[3], hot[2], rows[2], prows[2], parts[2]
    )

    corner(3)
    corner(1, cut_one)
    mine = [flip(shares[0], half)]
    to_back(2, xs[3])
    to_rows(3, state[2][0])
    ds[1], state[2], rows[3], prows[3], parts[3], mine = sync(
        ds[1], state[2], rows[3], prows[3], parts[3], mine
    )

    exchange(3)
    first_hop(2)
    corner(0, cut_zero)
    mine += [flip(shares[1], half)]
    to_back(3, state[2][0], tok)
    to_rows(1, state[3][0])
    state[2], ds[0], state[3], rows[1], prows[1], parts[1], mine = sync(
        state[2], ds[0], state[3], rows[1], prows[1], parts[1], mine
    )

    exchange(1)
    both_hops(2, 3)
    mine += [flip(shares[2], half)]
    spreads(3, state[2][0])
    to_back(1, hot[3], tok)
    to_rows(0, state[1][0])
    state[2], state[3], state[1], rows[0], prows[0], parts[0], hot[3], mine = sync(
        state[2], state[3], state[1], rows[0], prows[0], parts[0], hot[3], mine
    )

    exchange(0)
    (total,) = both_hops(3, 1, addends(2, []))
    sums[2] = flip(total, PLANE)
    pact = all_shares(mine)
    to_back(0, state[3][0], tok)
    spots, pieces = [spot for spot, _ in pact], [piece for _, piece in pact]
    sums[2], state[3], state[1], state[0], pieces = sync(sums[2], state[3], state[1], state[0], pieces)
    pact = list(zip(spots, pieces))

    (total,) = both_hops(1, 0, addends(3, [sums[2]]))
    sums[3] = flip(total, 3 * PLANE)
    grad_down = own(0, None, state[1][0])
    state[1], state[0], grad_down = sync(state[1], state[0], grad_down)

    (total,) = second_hop(0, addends(1, []))
    sums[1] = flip(total, PLANE)
    for c in range(1, calls):
        grad_down = own(c, grad_down, state[0][0])
    state[0], sums[1], sums[3], grad_down = sync(state[0], sums[1], sums[3], grad_down)
    return (plane_sum(0, [sums[1], sums[3]]), grad_down[None])


def solution(mesh):
    in_specs = (
        P("node", "local"),
        P("node", None),
        P("node", None),
        P(),
        P("node", None, None, None, None),
        P("node", "local", None),
        P("node", "local", None),
        P("node", None, "local"),
    )
    out_specs = (P("node", "local"), P("node", None, "local"))
    return jax.shard_map(body, mesh=mesh, in_specs=in_specs, out_specs=out_specs, check_vma=False)
```

```python
import functools

import jax
import jax.numpy as jnp
from jax import lax
from jax.experimental import pallas as pl
from jax.experimental.pallas import tpu as pltpu
from jax.sharding import PartitionSpec as P

F32 = jnp.float32
BF16 = jnp.bfloat16
LANES = 128
MIB = 1 << 20
VMEM_MIB = 64
PLANE = 4
CONTRACT_LAST = (((1,), (1,)), ((), ()))


def params(mib, ndims=0):
    sem = ("arbitrary",) * ndims if ndims else None
    return pltpu.CompilerParams(vmem_limit_bytes=mib * MIB - (MIB >> 4), dimension_semantics=sem)


COST = pl.CostEstimate(flops=1000, bytes_accessed=1000, transcendentals=0)


def dot(a, b):
    return jnp.dot(a, b, preferred_element_type=F32)


def attach_kernel(top, grad_ref, routes_ref, gate_ref, out_ref):
    tok, feats = grad_ref.shape
    out_ref[:, :feats] = grad_ref[...]
    gate = gate_ref[...]
    high = gate.astype(BF16).astype(F32)
    mid = (gate - high).astype(BF16).astype(F32)
    low = gate - high - mid
    names = routes_ref[...].astype(F32)
    pad = jnp.zeros((LANES - 4 * top, tok), F32)
    meta = jnp.concatenate([names, high, mid, low, pad], axis=0)
    out_ref[:, feats:] = jnp.transpose(meta).astype(BF16)


def attach(grad_out, routes, gate_prob):
    tok, feats = grad_out.shape
    routes, gate_prob = routes.T, gate_prob.T
    return pl.pallas_call(
        functools.partial(attach_kernel, routes.shape[0]),
        out_shape=jax.ShapeDtypeStruct((tok, feats + LANES), BF16),
        compiler_params=params(VMEM_MIB),
        cost_estimate=COST,
        name="attach",
    )(grad_out, routes, gate_prob)


def cut_kernel(piece_a, x, y, a_out, b_out, a_ref, b_ref, sem):
    pieces = ((x.at[:, :piece_a], a_ref, a_out), (y.at[:, piece_a:], b_ref, b_out))
    loads = [pltpu.make_async_copy(s, v, sem.at[i]) for i, (s, v, _) in enumerate(pieces)]
    stores = [pltpu.make_async_copy(v, t, sem.at[2 + i]) for i, (_, v, t) in enumerate(pieces)]
    for load in loads:
        load.start()
    for load, store in zip(loads, stores):
        load.wait()
        store.start()
    for store in stores:
        store.wait()


def cut(x, y, piece_a):
    tok, width = x.shape
    anywhere = pl.BlockSpec(memory_space=pl.ANY)
    widths = (piece_a, width - piece_a)
    return pl.pallas_call(
        functools.partial(cut_kernel, piece_a),
        in_specs=[anywhere] * 2,
        out_specs=[anywhere] * 2,
        out_shape=[jax.ShapeDtypeStruct((tok, w), BF16) for w in widths],
        scratch_shapes=[*[pltpu.VMEM((tok, w), BF16) for w in widths], pltpu.SemaphoreType.DMA((4,))],
        compiler_params=params(VMEM_MIB),
        cost_estimate=COST,
        name="cut",
    )(x, y)


def ranks(meta, slot, top, width):
    tok = meta.shape[0]
    lane = lax.broadcasted_iota(jnp.int32, meta.shape, 1)
    hit = jnp.where((lane < top) & (meta == slot.astype(F32)), 1.0, 0.0)
    named = jnp.broadcast_to(jnp.sum(hit, axis=1, keepdims=True), (tok, width))
    row = lax.broadcasted_iota(jnp.int32, (tok, tok), 0)
    col = lax.broadcasted_iota(jnp.int32, (tok, tok), 1)
    earlier = jnp.where(row > col, 1.0, 0.0).astype(BF16)
    return jnp.where(named > 0.5, dot(earlier, named.astype(BF16)), -1.0)


def row_gates(picked, slot, top):
    lane = lax.broadcasted_iota(jnp.int32, picked.shape, 1)
    high = pltpu.roll(picked, LANES - top, 1)
    mid = pltpu.roll(picked, LANES - 2 * top, 1)
    low = pltpu.roll(picked, LANES - 3 * top, 1)
    gate = (high + mid) + low
    chosen = jnp.where((lane < top) & (picked == slot.astype(F32)), gate, 0.0)
    return jnp.sum(chosen, axis=1, keepdims=True)


def selection(meta_refs, slots, top, cap, sel_ref, gate_ref):
    at = 0
    for meta_ref in meta_refs:
        meta = meta_ref[...]
        for slot in slots:
            rank = ranks(meta.astype(F32), slot, top, LANES)
            turned = jnp.transpose(rank)[:cap]
            want = lax.broadcasted_iota(jnp.int32, turned.shape, 0).astype(F32)
            sel = jnp.where(turned == want, 1.0, 0.0).astype(BF16)
            sel_ref[at : at + cap, :] = sel
            gates = row_gates(dot(sel, meta), slot, top)
            gate_ref[at : at + cap, :] = jnp.broadcast_to(gates, (cap, LANES))
            at += cap


def staged(copies, ahead=2):
    for copy in copies[:ahead]:
        copy.start()
    place = iter(range(len(copies)))

    def arrive():
        c = next(place)
        copies[c].wait()
        if c + ahead < len(copies):
            copies[c + ahead].start()

    return arrive


def rows_kernel(sizes, layout, first, many, waits, who_ref, wd, *refs):
    tok, feats, piece_a, chunk, cap, top = sizes
    blocks, refs = refs[: len(layout)], refs[len(layout) + waits :]
    rows_out, prows_out, part_out, *refs = refs
    tok_ref, wd_ref, rows_ref, prows_ref, sel_ref, gate_ref, acc_ref, part_ref, m_sem, b_sem, w_sem, out_sem = refs
    steps = feats // chunk
    place = slice(first * cap, (first + many) * cap)
    metas, weights, writes = [], [], []
    bodies = [[] for _ in range(steps)]
    for (q, lo), block in zip(layout, blocks):
        if lo + block.shape[1] > feats:
            copy = pltpu.make_async_copy(block.at[:, feats - lo :], tok_ref.at[q, :, feats:], m_sem.at[q])
            copy.start()
            metas.append(copy)
    for c in range(steps):
        at = c * chunk
        for (q, lo), block in zip(layout, blocks):
            if lo <= at < min(lo + block.shape[1], feats):
                source = block.at[:, at - lo : at - lo + chunk]
                copy = pltpu.make_async_copy(source, tok_ref.at[q, :, at : at + chunk], b_sem.at[c * many + q])
                copy.start()
                bodies[c].append(copy)
        cols = slice(at, at + chunk)
        weights.append(pltpu.make_async_copy(wd.at[:, cols], wd_ref.at[:, cols], w_sem.at[c]))
    weight_arrives = staged(weights)
    for copy in metas:
        copy.wait()
    selection(
        [tok_ref.at[q, :, feats:] for q in range(many)], (who_ref[0], who_ref[2]), top, cap, sel_ref, gate_ref
    )
    for c in range(steps):
        cols = slice(c * chunk, (c + 1) * chunk)
        for copy in bodies[c]:
            copy.wait()
        for q in range(many):
            at = slice(2 * q * cap, 2 * (q + 1) * cap)
            both = (dot(sel_ref[at, :], tok_ref[q, :, cols]) * gate_ref[at, :1]).astype(BF16)
            rows_ref[q * cap : (q + 1) * cap, cols] = both[:cap]
            prows_ref[q * cap : (q + 1) * cap, cols] = both[cap:]
        for i, (source, target) in enumerate(((rows_ref, rows_out), (prows_ref, prows_out))):
            writes.append(
                pltpu.make_async_copy(source.at[:, cols], target.at[place, cols], out_sem.at[2 * c + i])
            )
            writes[-1].start()
        weight_arrives()
        term = lax.dot_general(
            rows_ref[:, cols], wd_ref[:, cols], CONTRACT_LAST, preferred_element_type=F32
        )
        if c == 0 and steps > 1:
            acc_ref[...] = term
        elif c < steps - 1:
            acc_ref[...] += term
        else:
            part_ref[...] = ((acc_ref[...] + term) if steps > 1 else term).astype(BF16)
    writes.append(pltpu.make_async_copy(part_ref, part_out.at[place, :], out_sem.at[2 * steps]))
    writes[-1].start()
    for copy in writes:
        copy.wait()


def make_rows(who, blocks, first, before, w_down, sizes, name):
    tok, feats, piece_a, chunk, cap, top = sizes
    hidden = w_down.shape[0]
    count = PLANE * cap
    many = len(blocks)
    steps = feats // chunk
    layout, pieces = [], []
    for q, block in enumerate(blocks):
        lo = 0
        for piece in block:
            layout.append((q, lo))
            pieces.append(piece)
            lo += piece.shape[1]
    anywhere = pl.BlockSpec(memory_space=pl.ANY)
    return pl.pallas_call(
        functools.partial(rows_kernel, sizes, layout, first, many, len(before)),
        in_specs=[pl.BlockSpec(memory_space=pltpu.SMEM)] + [anywhere] * (1 + len(pieces) + len(before)),
        out_specs=[anywhere] * 3,
        scratch_shapes=[
            pltpu.VMEM((many, tok, feats + LANES), BF16),
            pltpu.VMEM((hidden, feats), BF16),
            pltpu.VMEM((many * cap, feats), BF16),
            pltpu.VMEM((many * cap, feats), BF16),
            pltpu.VMEM((2 * many * cap, tok), BF16),
            pltpu.VMEM((2 * many * cap, LANES), F32),
            pltpu.VMEM((many * cap, hidden), F32),
            pltpu.VMEM((many * cap, hidden), BF16),
            pltpu.SemaphoreType.DMA((many,)),
            pltpu.SemaphoreType.DMA((many * steps,)),
            pltpu.SemaphoreType.DMA((steps,)),
            pltpu.SemaphoreType.DMA((2 * steps + 1,)),
        ],
        out_shape=[
            jax.ShapeDtypeStruct((count, feats), BF16),
            jax.ShapeDtypeStruct((count, feats), BF16),
            jax.ShapeDtypeStruct((count, hidden), BF16),
        ],
        input_output_aliases={2 + len(pieces) + i: i for i in range(len(before))},
        compiler_params=params(VMEM_MIB),
        cost_estimate=COST,
        name=name,
    )(who, w_down, *pieces, *before)


def act_kernel(cap, many, who_ref, g_ref, u_ref, act_ref, dg_ref, du_ref):
    rows = g_ref.shape[0]
    width = many * cap
    for i in range(rows // width):
        pieces = []
        for q in range(many):
            at = pl.ds(pl.multiple_of((who_ref[0] ^ (i * many + q)) * cap, cap), cap)
            g = g_ref[at, :].astype(F32)
            u = u_ref[at, :].astype(F32)
            sig = jax.nn.sigmoid(g)
            pieces.append(g * sig * u)
            to = slice((i * many + q) * cap, (i * many + q + 1) * cap)
            dg_ref[to, :] = (u * sig * (1.0 + g * (1.0 - sig))).astype(BF16)
            du_ref[to, :] = (g * sig).astype(BF16)
        block = jnp.concatenate(pieces, axis=0) if many > 1 else pieces[0]
        act_ref[:, i * width : (i + 1) * width] = jnp.transpose(block).astype(BF16)


def activations(who, g, u, cap):
    rows, hidden = g.shape
    many = max(1, LANES // cap)
    vmem = pl.BlockSpec(memory_space=pltpu.VMEM)
    return pl.pallas_call(
        functools.partial(act_kernel, cap, many),
        in_specs=[pl.BlockSpec(memory_space=pltpu.SMEM), vmem, vmem],
        out_specs=[vmem] * 3,
        out_shape=[
            jax.ShapeDtypeStruct((hidden, rows), BF16),
            jax.ShapeDtypeStruct((rows, hidden), BF16),
            jax.ShapeDtypeStruct((rows, hidden), BF16),
        ],
        compiler_params=params(VMEM_MIB),
        cost_estimate=COST,
        name="activation",
    )(who, g, u)


def back_kernel(sizes, group, room, mine, other, dg_all, du_all, wg, wu, keep_out, a_out, b_out, *refs):
    tok, feats, piece_a, chunk, cap, top = sizes
    m_ref, o_ref, fg_ref, fu_ref, wg_ref, wu_ref, dg_ref, du_ref, keep_ref, a_ref, b_ref, sem, w_sem, out_sem = refs
    steps = feats // chunk
    count = PLANE * cap
    at = slice(group * count, (group + 1) * count)
    loads, weights, writes = [], [], []
    pairs = ((mine, m_ref), (other, o_ref), (dg_all.at[at, :], fg_ref), (du_all.at[at, :], fu_ref))
    for i, (source, target) in enumerate(pairs):
        loads.append(pltpu.make_async_copy(source, target, sem.at[i]))
        loads[-1].start()
    for c in range(steps):
        rows = slice(c * chunk, (c + 1) * chunk)
        for i, (source, target) in enumerate(((wg, wg_ref), (wu, wu_ref))):
            weights.append(
                pltpu.make_async_copy(source.at[rows, :], target.at[rows, :], w_sem.at[2 * c + i])
            )
    weight_arrives = staged(weights, 4)
    for copy in loads:
        copy.wait()
    for q in range(PLANE):
        rows = slice(q * cap, (q + 1) * cap)
        dhid = m_ref[rows, :].astype(F32) + o_ref[rows, :].astype(F32)
        dg_ref[rows, :] = (dhid * fg_ref[rows, :].astype(F32)).astype(BF16)
        du_ref[rows, :] = (dhid * fu_ref[rows, :].astype(F32)).astype(BF16)
    for c in range(steps):
        cols = slice(c * chunk, (c + 1) * chunk)
        weight_arrives()
        weight_arrives()
        back = lax.dot_general(
            dg_ref[...], wg_ref[cols, :], CONTRACT_LAST, preferred_element_type=F32
        )
        back += lax.dot_general(
            du_ref[...], wu_ref[cols, :], CONTRACT_LAST, preferred_element_type=F32
        )
        back = back.astype(BF16)
        if c * chunk < piece_a:
            keep_ref[:cap, cols] = back[:cap]
            keep_ref[cap:, cols] = back[2 * cap : 3 * cap]
            a_ref[:cap, cols] = back[cap : 2 * cap]
            a_ref[cap:, cols] = back[3 * cap :]
            source, target, to = a_ref, a_out, cols
        else:
            to = slice(c * chunk - piece_a, (c + 1) * chunk - piece_a)
            keep_ref[:, cols] = back[: 2 * cap]
            b_ref[:, to] = back[2 * cap :]
            source, target = b_ref, b_out
        writes.append(
            pltpu.make_async_copy(keep_ref.at[:, cols], keep_out.at[:, cols], out_sem.at[2 * c])
        )
        writes[-1].start()
        writes.append(
            pltpu.make_async_copy(
                source.at[:, to], target.at[: 2 * cap, to], out_sem.at[2 * c + 1]
            )
        )
        writes[-1].start()
    for copy in writes:
        copy.wait()


def make_back(part, other, factors, w_gate, w_up, sizes, group, room, name):
    tok, feats, piece_a, chunk, cap, top = sizes
    hidden = part.shape[1]
    count = PLANE * cap
    steps = feats // chunk
    anywhere = pl.BlockSpec(memory_space=pl.ANY)
    widths = [feats, piece_a, feats - piece_a]
    heights = [2 * cap, 2 * cap + room, 2 * cap + room]
    return pl.pallas_call(
        functools.partial(back_kernel, sizes, group, room),
        in_specs=[anywhere] * 6,
        out_specs=[anywhere] * 3,
        scratch_shapes=[
            pltpu.VMEM((count, hidden), part.dtype),
            pltpu.VMEM((count, hidden), other.dtype),
            pltpu.VMEM((count, hidden), BF16),
            pltpu.VMEM((count, hidden), BF16),
            pltpu.VMEM((feats, hidden), BF16),
            pltpu.VMEM((feats, hidden), BF16),
            pltpu.VMEM((count, hidden), BF16),
            pltpu.VMEM((count, hidden), BF16),
            *[pltpu.VMEM((2 * cap, w), BF16) for w in widths],
            pltpu.SemaphoreType.DMA((4,)),
            pltpu.SemaphoreType.DMA((2 * steps,)),
            pltpu.SemaphoreType.DMA((2 * steps,)),
        ],
        out_shape=[jax.ShapeDtypeStruct((h, w), BF16) for h, w in zip(heights, widths)],
        compiler_params=params(VMEM_MIB),
        cost_estimate=COST,
        name=name,
    )(part, other, *factors, w_gate, w_up)


def spread_kernel(top, cap, who_ref, mz, mx, my, out_ref):
    me = who_ref[0]
    width = max(LANES, 2 * cap)
    tok = mz.shape[0]
    for i, (meta_ref, bit) in enumerate(((mz, 1), (my, 1), (mz, 2), (mx, 2))):
        meta = meta_ref[...].astype(F32)
        mine = ranks(meta, me, top, width)[:, : 2 * cap]
        theirs = ranks(meta, me ^ bit, top, width)[:, : 2 * cap]
        lane = lax.broadcasted_iota(jnp.int32, mine.shape, 1)
        off = jnp.where(lane < cap, mine, theirs + cap) - lane.astype(F32)
        out_ref[i * tok : (i + 1) * tok, :] = jnp.where(off == 0.0, 1.0, 0.0).astype(BF16)


def make_spread(who, z, x, y, sizes, name):
    tok, feats, piece_a, chunk, cap, top = sizes

    def meta(piece):
        place = piece.shape[1] // LANES - 1
        return pl.BlockSpec((tok, LANES), lambda i, who: (0, place))

    return pl.pallas_call(
        functools.partial(spread_kernel, top, cap),
        grid_spec=pltpu.PrefetchScalarGridSpec(
            num_scalar_prefetch=1,
            grid=(1,),
            in_specs=[meta(z), meta(x), meta(y)],
            out_specs=pl.BlockSpec((4 * tok, 2 * cap), lambda i, who: (0, 0)),
        ),
        out_shape=jax.ShapeDtypeStruct((4 * tok, 2 * cap), BF16),
        compiler_params=params(VMEM_MIB, 1),
        cost_estimate=COST,
        name=name,
    )(who, z, x, y)


def join_kernel(sizes, waits, hot, keep, got_a, got_b, *refs):
    tok, feats, piece_a, chunk, cap, top = sizes
    refs = refs[waits:]
    summed = len(refs) > 3
    if summed:
        *parts, out_ref, a_ref, b_ref, total_ref = refs
    else:
        out_ref, a_ref, b_ref = refs

    def tokens(i, at, cols, got):
        both = jnp.concatenate([keep[at, cols], got[at, :]], axis=0)
        return dot(hot[i * tok : (i + 1) * tok, :], both).astype(BF16)

    near, far = slice(0, cap), slice(cap, 2 * cap)
    cols_a, cols_b = slice(0, piece_a), slice(piece_a, feats)
    a_ref[...] = tokens(1, far, cols_a, got_a)
    b_ref[...] = tokens(3, far, cols_b, got_b)
    out_ref[:, cols_a] = tokens(0, near, cols_a, got_a)
    out_ref[:, cols_b] = tokens(2, near, cols_b, got_b)
    if summed:
        add_kernel(2, *parts, total_ref)


def join(hot, keep, got_a, got_b, into, sizes, name, addends=None):
    tok, feats, piece_a, chunk, cap, top = sizes
    widths = (feats, piece_a, feats - piece_a)

    def whole(shape, row=0):
        return pl.BlockSpec(shape, lambda i: (row, 0))

    out_specs = [whole((tok, w)) for w in widths]
    out_shape = [jax.ShapeDtypeStruct((tok, w), BF16) for w in widths]
    aliases = {}
    if into:
        for_x, for_y = into
        place = for_x.shape[0] // tok - 1
        out_specs[1:] = [whole((tok, w), place) for w in widths[1:]]
        out_shape[1:] = [jax.ShapeDtypeStruct(a.shape, BF16) for a in (for_y, for_x)]
        aliases = {4: 1, 5: 2}
        into = [for_y, for_x]
    in_specs = [whole(a.shape) for a in (hot, keep)] + [whole((2 * cap, w)) for w in widths[1:]]
    in_specs += [pl.BlockSpec(memory_space=pl.ANY)] * len(into)
    args = [hot, keep, got_a, got_b, *into]
    if addends:
        kept, got, others = addends
        for a in (kept, *got, *others):
            in_specs.append(whole((tok, a.shape[1]), a.shape[0] // tok - 1))
            args.append(a)
        out_specs.append(whole((tok, feats)))
        out_shape.append(jax.ShapeDtypeStruct((tok, feats), BF16))
    return pl.pallas_call(
        functools.partial(join_kernel, sizes, len(into)),
        grid=(1,),
        in_specs=in_specs,
        out_specs=out_specs,
        out_shape=out_shape,
        input_output_aliases=aliases,
        compiler_params=params(VMEM_MIB, 1),
        cost_estimate=COST,
        name=name,
    )(*args)


def add_kernel(pieces, kept, *refs):
    got, others, out_ref = refs[:pieces], refs[pieces:-1], refs[-1]
    lo = 0
    for got_ref in got:
        at = slice(lo, lo + got_ref.shape[1])
        total = kept[:, at].astype(F32) + got_ref[...].astype(F32)
        for other in others:
            total += other[:, at].astype(F32)
        out_ref[:, at] = total.astype(BF16)
        lo = at.stop


def add(kept, got, others, name):
    tok = kept.shape[0]
    some = tok // 2 if tok % 32 == 0 else tok

    def part(a):
        skip = (a.shape[0] - tok) // some
        return pl.BlockSpec((some, a.shape[1]), lambda i: (i + skip, 0))

    args = [kept, *got, *others]
    return pl.pallas_call(
        functools.partial(add_kernel, len(got)),
        grid=(tok // some,),
        in_specs=[part(a) for a in args],
        out_specs=part(kept),
        out_shape=jax.ShapeDtypeStruct(kept.shape, BF16),
        compiler_params=params(VMEM_MIB, 1),
        cost_estimate=COST,
        name=name,
    )(*args)


def total_kernel(*refs):
    *parts, out_ref = refs
    total = parts[0][...].astype(F32)
    for part in parts[1:]:
        total += part[...].astype(F32)
    out_ref[...] = total.astype(BF16)


def total_of(first, others):
    vmem = pl.BlockSpec(memory_space=pltpu.VMEM)
    return pl.pallas_call(
        total_kernel,
        in_specs=[vmem] * (1 + len(others)),
        out_specs=vmem,
        out_shape=jax.ShapeDtypeStruct(first.shape, BF16),
        compiler_params=params(VMEM_MIB),
        cost_estimate=COST,
        name="total",
    )(first, *others)


def own_kernel(groups, spots, locals_, flag_ref, who_ref, act_ref, *refs):
    pieces, refs = refs[: len(spots)], refs[len(spots) :]
    rows, prows, (out_ref, pact_ref, sem) = refs[:groups], refs[groups : 2 * groups], refs[-3:]
    count = rows[0].shape[0]
    share = act_ref.shape[0] // locals_

    def loads():
        for n, ((turn, first), piece) in enumerate(zip(spots, pieces)):
            owner = lax.rem(who_ref[1] - turn + locals_, locals_)
            start = pl.multiple_of(owner * share + first, 16)
            yield pltpu.make_async_copy(piece, pact_ref.at[pl.ds(start, piece.shape[0]), :], sem.at[n])

    @pl.when(pl.program_id(0) == 0)
    def _():
        for copy in loads():
            copy.start()

    def product(a_ref, b_refs, order):
        total = None
        for g in range(groups):
            at = order(g) * count
            term = dot(a_ref[:, at : at + count], b_refs[g][...])
            total = term if total is None else total + term
        return total.astype(BF16).astype(F32)

    own = product(act_ref, rows, lambda g: g)

    @pl.when(pl.program_id(0) == 0)
    def _():
        for copy in loads():
            copy.wait()

    paired = product(pact_ref, prows, lambda g: g ^ (groups // 2))
    out_ref[...] = (own + flag_ref[0] * paired).astype(BF16)


def make_own(flag, who, act, pact, rows, prows, before, start, count, chunk, feats, locals_, name):
    groups = len(rows)
    hidden, width = act.shape
    spots = [spot for spot, _ in pact]
    part = pl.BlockSpec((rows[0].shape[0], chunk), lambda i, flag, who: (0, i + start))
    anywhere = pl.BlockSpec(memory_space=pl.ANY)
    in_specs = [pl.BlockSpec((hidden, width), lambda i, flag, who: (0, 0))]
    in_specs += [anywhere] * len(pact) + [part] * (2 * groups)
    args = [flag, who, act, *[piece for _, piece in pact], *rows, *prows]
    aliases = {}
    if before is not None:
        in_specs.append(anywhere)
        aliases = {len(args): 0}
        args.append(before)
    return pl.pallas_call(
        functools.partial(own_kernel, groups, spots, locals_),
        grid_spec=pltpu.PrefetchScalarGridSpec(
            num_scalar_prefetch=2,
            grid=(count,),
            in_specs=in_specs,
            out_specs=pl.BlockSpec((hidden, chunk), lambda i, flag, who: (0, i + start)),
            scratch_shapes=[pltpu.VMEM((hidden, width), BF16), pltpu.SemaphoreType.DMA((len(pact),))],
        ),
        out_shape=jax.ShapeDtypeStruct((hidden, feats), BF16),
        input_output_aliases=aliases,
        compiler_params=params(VMEM_MIB, 1),
        cost_estimate=COST,
        name=name,
    )(*args)


def after(value, *first):
    return lax.optimization_barrier((value, first))[0]


def sync(*values):
    return lax.optimization_barrier(values)


def flip(block, bits):
    count = lax.axis_size("node")
    return lax.ppermute(block, "node", [(i, i ^ bits) for i in range(count)])


def planes(block, pairs):
    route = [(PLANE * a + i, PLANE * b + i) for a, b in pairs for i in range(PLANE)]
    return lax.ppermute(block, "node", route)


def body(grad_out, gate_prob, routes, paired, saved_pre, w_gate, w_up, w_down):
    tok, feats = grad_out.shape
    nodes = lax.axis_size("node")
    locals_ = lax.axis_size("local")
    top = routes.shape[1]
    cap = saved_pre.shape[2]
    hidden = saved_pre.shape[4]
    groups = nodes // PLANE
    half = nodes // 2
    piece_a = feats // (2 * LANES) * LANES
    widths = (1536, 768, 512, 384, 256, 128)
    chunk = max(c for c in widths if piece_a % c == 0 and (feats - piece_a) % c == 0)
    own_chunk = max(c for c in (768, 512, 384, 256, 128) if feats % c == 0)
    sizes = (tok, feats, piece_a, chunk, cap, top)
    back_chunk = max(c for c in (512, 384, 256, 128) if piece_a % c == 0 and (feats - piece_a) % c == 0)
    back_sizes = (tok, feats, piece_a, back_chunk, cap, top)
    w_down, w_gate, w_up = w_down[0], w_gate[0], w_up[0]
    ring = [(i, (i + 1) % locals_) for i in range(locals_)]

    me = lax.axis_index("node")
    side = lax.axis_index("local")
    who = jnp.stack([me, side, me ^ half]).astype(jnp.int32)
    flag = jnp.sum(jnp.where(jnp.arange(half, dtype=jnp.int32) == me % half, paired, 0)).astype(F32)[None]

    zs, xs, ys, ds, hot, rows, prows, parts, state, sums = ({} for _ in range(10))
    block = attach(grad_out, routes, gate_prob)
    zs[0] = [block]
    saved_rows = saved_pre[0].reshape(nodes * cap, 2, hidden)
    g_rows, u_rows = saved_rows[:, 0, :], saved_rows[:, 1, :]

    def flips(pieces, bits):
        return [flip(piece, bits) for piece in pieces]

    def beside(g):
        xs[g], ys[g] = flips(zs[g], 1), flips(zs[g], 2)

    def corner(g, pieces=None):
        from_x, from_y = pieces or cut(xs[g][0], ys[g][0], piece_a)
        ds[g] = [flip(from_x, 2), flip(from_y, 1)]

    def spreads(g, done):
        hot[g] = make_spread(after(who, done), zs[g][-1], xs[g][-1], ys[g][-1], sizes, f"spread_{g}")

    made = {}

    def near_rows(g, done):
        blocks = [zs[g], xs[g], ys[g]]
        made[g] = make_rows(after(who, done), blocks, 0, (), w_down, sizes, f"near_{g}")

    def to_rows(g, done):
        if g in made:
            call = [ds[g]], PLANE - 1, made[g]
        else:
            call = [zs[g], xs[g], ys[g], ds[g]], 0, ()
        rows[g], prows[g], parts[g] = make_rows(after(who, done), *call, w_down, sizes, f"partial_{g}")

    def exchange(g):
        piece = lax.ppermute(parts[g], "local", ring)
        if locals_ > 2:
            other = piece.astype(F32)
            for _ in range(locals_ - 2):
                piece = lax.ppermute(piece, "local", ring)
                other = other + piece.astype(F32)
            piece = other
        parts[g] = [parts[g], piece]

    def to_back(g, done, room=0):
        mine, other = parts[g]
        state[g] = make_back(
            after(mine, done), other, factors, w_gate, w_up, back_sizes, g, room, f"back_{g}"
        )

    def first_hop(g):
        keep, send_a, send_b = state[g]
        state[g] = [keep, flip(send_a, 1), flip(send_b, 2)]

    def second_hop(g, addends=None):
        kept, send_a, send_b, *total = join(hot[g], *state[g], [], sizes, f"join_{g}", addends)
        state[g] = [kept, flip(send_a, 2), flip(send_b, 1)]
        return total

    def both_hops(g, h, addends=None):
        keep, for_x, for_y = state[h]
        kept, for_y, for_x, *total = join(hot[g], *state[g], [for_x, for_y], sizes, f"join_{g}", addends)
        got_x, got_y = flip(for_x, 1), flip(for_y, 2)
        state[g] = [kept, got_y, got_x]
        state[h] = [keep, got_x, got_y]
        return total

    def addends(g, others):
        kept, *got = state[g]
        return kept, got, others

    def plane_sum(g, others):
        kept, *got = state[g]
        return add(kept, got, others, f"sum_{g}")

    share = hidden // locals_

    def cut_share(part, count):
        some = share // count
        return lax.dynamic_slice_in_dim(act, side * share + part * some, some, 0)

    def all_shares(pieces):
        found, first = [], 0
        for piece in pieces:
            for turn in range(locals_):
                found.append(((turn, first), piece))
                if turn < locals_ - 1:
                    piece = lax.ppermute(piece, "local", ring)
            first += piece.shape[0]
        return found

    steps = feats // own_chunk
    calls = min(2, steps)

    def own(c, before, done):
        start, stop = steps * c // calls, steps * (c + 1) // calls
        lists = [[r[g] for g in range(groups)] for r in (rows, prows)]
        return make_own(
            after(flag, done), who, act, pact, *lists, before, start, stop - start, own_chunk, feats, locals_, f"own_{c}"
        )

    def activate(done):
        return activations(after(who, done), g_rows, u_rows, cap)

    if groups != 4 or 2 * piece_a != feats or tok != 2 * cap:
        act, *factors = activate(block)
        pact = all_shares([flip(cut_share(0, 1), half)])
        done = act
        for g in range(groups):
            if g:
                zs[g] = [flip(after(block, done), PLANE * g)]
            beside(g)
            corner(g)
            spreads(g, done)
            to_rows(g, done)
            exchange(g)
            to_back(g, done)
            first_hop(g)
            second_hop(g)
            sums[g] = done = plane_sum(g, [])
            if g:
                sums[g] = done = flip(sums[g], PLANE * g)
        grad_down = None
        for c in range(calls):
            grad_down = own(c, grad_down, done)
        return (total_of(sums[0], [sums[g] for g in range(1, groups)]), grad_down[None])

    inward, outward = [(1, 2), (2, 1)], [(1, 0), (2, 3)]
    plane = me // PLANE
    middle = (plane == 1) | (plane == 2)

    beside(0)
    one, over = flip(block, PLANE), planes(block, inward)
    xs[0], ys[0], one, over, g_rows, u_rows = sync(xs[0], ys[0], one, over, g_rows, u_rows)

    zs[1] = [one]
    second, edge_two = planes(one, inward), planes(over, outward)
    beside(1)
    act, *factors = activate(xs[0])
    spreads(0, act)
    near_rows(0, hot[0])
    second, edge_two, xs[1], ys[1], hot[0], act, factors, made[0], flag = sync(
        second, edge_two, xs[1], ys[1], hot[0], act, factors, made[0], flag
    )

    edge_three = planes(second, outward)
    zs[2] = [jnp.where(middle, second, edge_two)]
    beside(2)
    spreads(1, zs[2][0])
    cut_zero = cut(after(xs[0][0], hot[1]), ys[0][0], piece_a)
    cut_one = cut(after(xs[1][0], cut_zero), ys[1][0], piece_a)
    near_rows(1, cut_one)
    shares = [cut_share(0, 2), cut_share(2, 4), cut_share(3, 4)]
    edge_three, xs[2], ys[2], hot[1], cut_zero, cut_one, made[1], shares = sync(
        edge_three, xs[2], ys[2], hot[1], cut_zero, cut_one, made[1], shares
    )

    cut_two = cut(xs[2][0], ys[2][0], piece_a)
    corner(2, cut_two)
    zs[3] = [jnp.where(middle, over, after(edge_three, cut_two))]
    beside(3)
    spreads(2, zs[3][0])
    to_rows(2, hot[2])
    exchange(2)
    xs[3], ys[3], hot[2], rows[2], prows[2], parts[2] = sync(
        xs[3], ys[3], hot[2], rows[2], prows[2], parts[2]
    )

    corner(3)
    corner(1, cut_one)
    mine = [flip(shares[0], half)]
    to_back(2, xs[3])
    to_rows(3, state[2][0])
    ds[1], state[2], rows[3], prows[3], parts[3], mine = sync(
        ds[1], state[2], rows[3], prows[3], parts[3], mine
    )

    exchange(3)
    first_hop(2)
    corner(0, cut_zero)
    mine += [flip(shares[1], half)]
    to_back(3, state[2][0], tok)
    to_rows(1, state[3][0])
    state[2], ds[0], state[3], rows[1], prows[1], parts[1], mine = sync(
        state[2], ds[0], state[3], rows[1], prows[1], parts[1], mine
    )

    exchange(1)
    both_hops(2, 3)
    mine += [flip(shares[2], half)]
    spreads(3, state[2][0])
    to_back(1, hot[3], tok)
    to_rows(0, state[1][0])
    state[2], state[3], state[1], rows[0], prows[0], parts[0], hot[3], mine = sync(
        state[2], state[3], state[1], rows[0], prows[0], parts[0], hot[3], mine
    )

    exchange(0)
    (total,) = both_hops(3, 1, addends(2, []))
    sums[2] = flip(total, PLANE)
    pact = all_shares(mine)
    to_back(0, state[3][0], tok)
    spots, pieces = [spot for spot, _ in pact], [piece for _, piece in pact]
    sums[2], state[3], state[1], state[0], pieces = sync(sums[2], state[3], state[1], state[0], pieces)
    pact = list(zip(spots, pieces))

    (total,) = both_hops(1, 0, addends(3, [sums[2]]))
    sums[3] = flip(total, 3 * PLANE)
    grad_down = own(0, None, state[1][0])
    state[1], state[0], grad_down = sync(state[1], state[0], grad_down)

    (total,) = second_hop(0, addends(1, []))
    sums[1] = flip(total, PLANE)
    for c in range(1, calls):
        grad_down = own(c, grad_down, state[0][0])
    state[0], sums[1], sums[3], grad_down = sync(state[0], sums[1], sums[3], grad_down)
    return (plane_sum(0, [sums[1], sums[3]]), grad_down[None])


def solution(mesh):
    in_specs = (
        P("node", "local"),
        P("node", None),
        P("node", None),
        P(),
        P("node", None, None, None, None),
        P("node", "local", None),
        P("node", "local", None),
        P("node", None, "local"),
    )
    out_specs = (P("node", "local"), P("node", None, "local"))
    return jax.shard_map(body, mesh=mesh, in_specs=in_specs, out_specs=out_specs, check_vma=False)
```
